32 devices in a mesh: ctx: 4 (over y, core), exp: 8 (over z, x).
Axes of the slice: x: 2, y: 2, z: 4, core: 2. Of those that a mesh axis runs over, the one named last changes fastest.
Arguments:
- residual_in: bfloat16 [2048, 3584], P(('ctx', 'exp')), may hold values from -1.5 to 1.5
- norm_gain: float32 [3584], replicated, may hold values from 0.25 to 1.75
- q_nope: bfloat16 [2048, 16, 512], P('ctx', 'exp'), may hold values from -64 to 64
- q_rope: bfloat16 [2048, 1024], P('ctx', 'exp'), may hold values from -6 to 6
- latent: bfloat16 [2048, 512], P('ctx'), may hold values from -6 to 6
- k_rope: bfloat16 [2048, 64], P('ctx'), may hold values from -6 to 6
- doc_ids: int32 [2048], P('ctx'), may hold values from 0 to 3, never falling along the last dimension, each value on 1 to 1024 neighbouring positions
- uv_weight: bfloat16 [16, 512, 128], P('exp'), may hold values from -0.25 to 0.25
- out_weight: bfloat16 [2048, 3584], P('exp'), may hold values from -0.125 to 0.125
- expert_ids: int32 [2048, 8], P(('ctx', 'exp')), may hold values from 0 to 7, all different within a row; in each aligned block of 64 rows (0 to 63, 64 to 127, ...) at most 64 rows name the same one
- gate_levels: int32 [2048, 8], P(('ctx', 'exp')), may hold values from 1 to 255
- bin_ids: int32 [2048, 8], P(('ctx', 'exp')), may hold values from 0 to 2047
- gate_weight: bfloat16 [8, 3584, 1024], P('exp', None, 'ctx'), may hold values from -0.09375 to 0.09375
- up_weight: bfloat16 [8, 3584, 1024], P('exp', None, 'ctx'), may hold values from -0.09375 to 0.09375
- down_weight: bfloat16 [8, 1024, 3584], P('exp', 'ctx'), may hold values from -0.1875 to 0.1875
Outputs:
- layer_out: bfloat16 [2048, 3584], P(('ctx', 'exp'))
- histogram: float32 [8, 2048], P('exp', 'ctx')
The draws below stay inside these ranges and needn't reach their ends.
Inputs may be any that keep to these rules, and one draw needn't show every extreme that they name: `expert_ids`: each row names 8 different experts; within the rows of one device (aligned blocks of 64 rows) no expert is named more than 64 times, a bound that some block reaches. `doc_ids`: document numbers never fall along the sequence; each document has 1 to 1024 tokens, one exactly 1024.
All inputs are finite; a program needn't handle non-finite values.
Results may differ from the reference program's by a relative error of at most 0.03.
Values may be sent and summed in bfloat16 or wider, within the bound.
No kernel may reach another device: no remote copies, remote signals or barrier semaphores. Data moves between devices by JAX's collectives and lax.ppermute only.
A program may use at most 128 MiB of HBM per device.

```python
import math
import jax
import jax.numpy as jnp
import numpy as np
from jax import lax

D = 3584
LAT = 512
ROPE = 64
VDIM = 128
HID = 1024
TOPK = 8
NBINS = 2048
BLOCK = 512
SEQ = 2048
HEADS = 16
EXPERTS = 8
TOK = 64
CAP = 64
N_CTX = 4
N_EXP = 8


def shared_latent(key):
    return jax.random.normal(jax.random.fold_in(key, 11), (SEQ, LAT), jnp.float32)


def draw_latent(key, part):
    base = shared_latent(key)
    return jnp.clip(base, -6.0, 6.0).astype(jnp.bfloat16)


def draw_q_nope(key, part):
    values = jax.random.normal(jax.random.fold_in(key, 23), (SEQ, HEADS, LAT), jnp.float32)
    return jnp.clip(values, -64.0, 64.0).astype(jnp.bfloat16)


def set_ends(array, own_key, low, top_value):
    dims = array.shape
    place = [jax.random.randint(jax.random.fold_in(own_key, axis), (), 0, dims[axis]) for axis in range(len(dims))]
    array = array.at[tuple(place)].set(low)
    longest = dims.index(max(dims))
    place[longest] = (place[longest] + 1) % dims[longest]
    return array.at[tuple(place)].set(top_value)


def shard_levels(rng, dims, split, least, top_value):
    loudness = 1.0
    for axis_at, blocks in split:
        heights = jax.random.uniform(jax.random.fold_in(jax.random.fold_in(rng, 6), axis_at), (blocks,), jnp.float32, least / len(split), top_value / len(split))
        loudness = loudness * jnp.repeat(jnp.exp(heights), dims[axis_at] // blocks).reshape((-1,) + (1,) * (len(dims) - 1 - axis_at))
    return loudness


def profile(amount, total, bound, slope):
    weights = [(1 << 20) // math.isqrt(standing ** slope) + 1 for standing in range(2, amount + 1)]
    surplus, given = total - bound - (amount - 1), [1] * (amount - 1)
    while surplus > 0:
        movable = [i for i in range(amount - 1) if given[i] < bound]
        pool, remaining = sum([weights[i] for i in movable]), surplus
        for i in movable:
            extra = min(bound - given[i], max(1, remaining * weights[i] // pool), surplus)
            given[i] = given[i] + extra
            surplus = surplus - extra
    return np.array([bound] + given)


def uneven_parts(own_key, count, total, most, slope):
    if count == 2:
        one = jax.random.randint(own_key, (), max(1, total - most), min(most, total - 1) + 1)
        return jnp.stack([one, total - one])
    lengths = jnp.asarray(profile(count, total, most, slope), jnp.int32)
    twos = (count - 1) // 2
    giver, taker = lengths[1:1 + 2 * twos:2], lengths[2:2 + 2 * twos:2]
    room = jnp.minimum(giver - 1, most - taker)
    moved = jax.random.randint(jax.random.fold_in(own_key, 1), (twos,), 0, 1 << 20) % (room + 1)
    lengths = lengths.at[1:1 + 2 * twos:2].set(giver - moved).at[2:2 + 2 * twos:2].set(taker + moved)
    return lengths[jax.random.permutation(jax.random.fold_in(own_key, 2), count)]


def routed_block(own_key, own, number, rows, amount, top, bound, skew):
    order = jax.random.permutation(own_key, amount)
    crowded, usual = shares(amount, rows * top, bound, skew, True), shares(amount, rows * top, bound, skew, False)
    places = jnp.arange(amount)

    def named(tallies, offset_by):
        used = int((tallies > 0).sum())
        fixed = max(1, used // 4)
        moved = fixed + (places - fixed + offset_by * (used - fixed)) % max(1, amount - fixed)
        return jnp.zeros((amount,), jnp.int32).at[order[jnp.where(places < fixed, places, moved)]].set(jnp.asarray(tallies, jnp.int32))

    tallies = jnp.where(number % 4 == 0, named(crowded, number // 4), named(usual, number - number // 4 - 1))
    mixed = jax.random.permutation(jax.random.fold_in(own, 3), amount)
    donor, sink = mixed[0:amount // 2 * 2:2], mixed[1:amount // 2 * 2:2]
    room = jnp.minimum(tallies[donor] - 1, bound - tallies[sink]) // 2
    room = jnp.where((donor == order[0]) | (sink == order[0]) | (tallies[sink] == 0), 0, jnp.maximum(room, 0))
    moved = jax.random.randint(jax.random.fold_in(own, 4), (amount // 2,), 0, 1 << 20) % (room + 1)
    tallies = tallies.at[donor].add(-moved).at[sink].add(moved)
    labels = jnp.searchsorted(jnp.cumsum(tallies), jnp.arange(rows * top), side="right").astype(jnp.int32)
    listing = labels.reshape(top, rows).T
    listing = listing[jax.random.permutation(jax.random.fold_in(own, 1), rows)]
    offset_by = jax.random.randint(jax.random.fold_in(own, 2), (rows, 1), 0, top)
    return jnp.take_along_axis(listing, (jnp.arange(top)[None, :] + offset_by) % top, axis=1)


def shares(number_of, total, reach, slope, full):
    weights = [(1 << 20) // math.isqrt(grade ** slope) + 1 for grade in range(1, number_of + 1)]
    largest = reach if full else min(reach, max(-(-total // number_of), total * weights[0] // sum(weights)))
    least = 1 if total - largest >= number_of - 1 else 0
    given, rest = [largest] + [least] * (number_of - 1), total - largest - least * (number_of - 1)
    while rest > 0:
        candidates = [i for i in range(1, number_of) if given[i] < largest] or [i for i in range(1, number_of) if given[i] < reach]
        mass, budget = sum([weights[i] for i in candidates]), rest
        for i in candidates:
            addition = min(reach - given[i], max(1, budget * weights[i] // mass), rest)
            given[i] = given[i] + addition
            rest = rest - addition
    return np.array(given)


def bell_draw(rng, extent, spread, reach, split=(), held_as=jnp.bfloat16):
    loudness = shard_levels(rng, extent, split, -0.22, 0.18) if split else 1.0
    values = jax.random.normal(rng, extent, jnp.float32) * spread * loudness
    return jnp.minimum(jnp.maximum(values, -reach), reach).astype(held_as)


def setup_inputs(seed: int = 0) -> dict:
    key_of = jax.random.split(jax.random.key(seed), 16)
    residual_in = bell_draw(key_of[0], (SEQ, D), 0.25, 1.5, ((0, 32),))
    norm_gain = jnp.clip(1.0 + 0.15 * jax.random.normal(key_of[1], (D,), jnp.float32), 0.25, 1.75)
    q_nope = draw_q_nope(jax.random.fold_in(key_of[15], 71), 0)
    q_rope = bell_draw(key_of[3], (SEQ, HEADS * ROPE), 1.0, 6.0, ((0, 4), (1, 8)))
    latent = draw_latent(jax.random.fold_in(key_of[15], 71), 0)
    k_rope = bell_draw(key_of[5], (SEQ, ROPE), 1.0, 6.0, ((0, 4),))
    doc_ids = jnp.searchsorted(jnp.cumsum(uneven_parts(key_of[6], N_CTX, SEQ, 2 * BLOCK, 0)), jnp.arange(SEQ), side="right").astype(jnp.int32)
    uv_weight = bell_draw(key_of[7], (HEADS, LAT, VDIM), LAT ** -0.5, 0.25, ((0, 8),))
    out_weight = bell_draw(key_of[8], (HEADS * VDIM, D), (HEADS * VDIM) ** -0.5, 0.125, ((0, 8),))
    expert_ids_keys = jax.random.split(jax.random.fold_in(key_of[9], 1), SEQ // TOK)
    expert_ids_turns = jax.random.permutation(jax.random.fold_in(key_of[9], 3), SEQ // TOK)
    expert_ids = jax.vmap(lambda own, number: routed_block(jax.random.fold_in(key_of[9], 2), own, number, TOK, EXPERTS, TOPK, CAP, 2))(expert_ids_keys, expert_ids_turns).reshape((SEQ, TOPK))
    gate_levels = set_ends(jax.random.randint(key_of[10], (SEQ, TOPK), 1, 256), jax.random.fold_in(key_of[10], 1), 1, 255).astype(jnp.int32)
    bin_ids = set_ends(jax.random.randint(key_of[11], (SEQ, TOPK), 0, NBINS), jax.random.fold_in(key_of[11], 1), 0, NBINS - 1).astype(jnp.int32)
    gate_weight = bell_draw(key_of[12], (EXPERTS, D, HID), D ** -0.5, 0.09375, ((0, 8), (2, 4)))
    up_weight = bell_draw(key_of[13], (EXPERTS, D, HID), D ** -0.5, 0.09375, ((0, 8), (2, 4)))
    down_weight = bell_draw(key_of[14], (EXPERTS, HID, D), HID ** -0.5, 0.1875, ((0, 8), (1, 4)))
    return dict(residual_in=residual_in, norm_gain=norm_gain, q_nope=q_nope, q_rope=q_rope, latent=latent, k_rope=k_rope, doc_ids=doc_ids, uv_weight=uv_weight, out_weight=out_weight, expert_ids=expert_ids, gate_levels=gate_levels, bin_ids=bin_ids, gate_weight=gate_weight, up_weight=up_weight, down_weight=down_weight)


softmax_scale = 192.0 ** (-0.5)
norm_eps = 1e-06

def route_slots(expert_ids, experts, capacity):
    flat_ids = expert_ids.reshape(-1)
    onehot = (flat_ids[:, None] == jnp.arange(experts, dtype=jnp.int32)[None, :]).astype(jnp.int32)
    before = jnp.cumsum(onehot, axis=0) - onehot
    slot_rank = lax.optimization_barrier(jnp.sum(before * onehot, axis=1))
    return (flat_ids * capacity + slot_rank).reshape(expert_ids.shape)

def reference(residual_in, norm_gain, q_nope, q_rope, latent, k_rope, doc_ids, uv_weight, out_weight, expert_ids, gate_levels, bin_ids, gate_weight, up_weight, down_weight):
    positions = jnp.arange(SEQ, dtype=jnp.int32)
    allowed = (positions[None, :] <= positions[:, None]) & (doc_ids[None, :] == doc_ids[:, None])
    query_rope = q_rope.reshape(SEQ, HEADS, ROPE)

    def attend_head(head_index):
        head_nope = q_nope[:, head_index, :]
        head_rope = query_rope[:, head_index, :]
        scores = jnp.dot(head_nope, latent.T, preferred_element_type=jnp.float32)
        scores = (scores + jnp.dot(head_rope, k_rope.T, preferred_element_type=jnp.float32)) * softmax_scale
        scores = jnp.where(allowed, scores, -jnp.inf)
        row_max = lax.optimization_barrier(jnp.max(scores, axis=1, keepdims=True))
        exp_terms = jnp.where(allowed, jnp.exp(scores - row_max), 0.0)
        weights = (exp_terms / lax.optimization_barrier(jnp.sum(exp_terms, axis=1, keepdims=True))).astype(jnp.bfloat16)
        context = jnp.dot(weights, latent, preferred_element_type=jnp.float32).astype(jnp.bfloat16)
        return jnp.dot(context, uv_weight[head_index], preferred_element_type=jnp.float32).astype(jnp.bfloat16)
    values = lax.map(attend_head, jnp.arange(HEADS, dtype=jnp.int32))
    values = values.transpose(1, 0, 2).reshape(SEQ, HEADS * VDIM)
    attended = jnp.dot(values, out_weight, preferred_element_type=jnp.float32)
    stream_state = residual_in.astype(jnp.float32) + attended
    normed = (stream_state * lax.rsqrt(lax.optimization_barrier(jnp.mean(stream_state * stream_state, axis=1, keepdims=True)) + norm_eps) * norm_gain).astype(jnp.bfloat16)
    device_count = N_CTX * N_EXP
    slot_total = EXPERTS * CAP
    slot_index = jnp.arange(slot_total, dtype=jnp.int32)
    block_ids = expert_ids.reshape(device_count, TOK, TOPK)
    destination = jax.vmap(lambda ids_block: route_slots(ids_block, EXPERTS, CAP))(block_ids)

    def pack_slots(dest_block, row_block, bin_block):
        slot_match = dest_block[:, :, None] == slot_index[None, None, :]
        selector = lax.optimization_barrier(jnp.sum(slot_match.astype(jnp.int32), axis=1)).astype(jnp.bfloat16)
        outgoing = jnp.einsum('ts,td->sd', selector, row_block, preferred_element_type=jnp.float32).astype(jnp.bfloat16)
        slot_bins = lax.optimization_barrier(jnp.sum(jnp.where(slot_match, bin_block[:, :, None], 0), axis=(0, 1))).astype(jnp.int32)
        return (outgoing, slot_bins)
    sends, send_bins = jax.vmap(pack_slots)(destination, normed.reshape(device_count, TOK, D), bin_ids.reshape(device_count, TOK, TOPK))
    sends = sends.reshape(device_count, EXPERTS, CAP, D)
    send_bins = send_bins.reshape(device_count, EXPERTS, CAP)

    def run_expert(expert_index):
        row_data = sends[:, expert_index].reshape(device_count * CAP, D)
        slot_bins = send_bins[:, expert_index].reshape(device_count * CAP)
        gate_part = jnp.dot(row_data, gate_weight[expert_index], preferred_element_type=jnp.float32)
        up_part = jnp.dot(row_data, up_weight[expert_index], preferred_element_type=jnp.float32)
        activation = jax.nn.silu(gate_part) * up_part
        hidden = activation.astype(jnp.bfloat16)
        energy = lax.optimization_barrier(jnp.sum(activation * activation, axis=1)) / HID
        onehot = (slot_bins[:, None] == jnp.arange(NBINS, dtype=jnp.int32)[None, :]).astype(jnp.float32)
        bin_sums = jnp.dot(energy[None, :], onehot, precision=lax.Precision.HIGHEST)[0]
        expert_rows = jnp.dot(hidden, down_weight[expert_index], preferred_element_type=jnp.float32).astype(jnp.bfloat16)
        return (expert_rows.reshape(device_count, CAP, D), bin_sums)
    expert_out, histogram = lax.map(run_expert, jnp.arange(EXPERTS, dtype=jnp.int32))
    levels = gate_levels.astype(jnp.float32)
    route_weights = levels / lax.optimization_barrier(jnp.sum(levels, axis=1, keepdims=True))

    def combine_rows(dest_block, weight_block, returned):
        slot_match = dest_block[:, :, None] == slot_index[None, None, :]
        combiner = lax.optimization_barrier(jnp.sum(jnp.where(slot_match, weight_block[:, :, None], 0.0), axis=1))
        return jnp.dot(combiner, returned.reshape(slot_total, D).astype(jnp.float32), precision=lax.Precision.HIGHEST)
    mixture = jax.vmap(combine_rows)(destination, route_weights.reshape(device_count, TOK, TOPK), expert_out.transpose(1, 0, 2, 3))
    layer_out = (stream_state + mixture.reshape(SEQ, D)).astype(jnp.bfloat16)
    return (layer_out, histogram)
```

```python
import jax
import jax.numpy as jnp
from jax import lax
from jax.experimental import pallas as pl
from jax.experimental.pallas import tpu as pltpu
from jax.sharding import PartitionSpec as P

HID = 1024
NBINS = 2048


softmax_scale = 192.0 ** (-0.5)
norm_eps = 1e-06
masked_score = -1e30


def route_slots(expert_ids, experts, capacity):
    flat_ids = expert_ids.reshape(-1)
    onehot = (flat_ids[:, None] == jnp.arange(experts, dtype=jnp.int32)[None, :]).astype(jnp.int32)
    before = jnp.cumsum(onehot, axis=0) - onehot
    slot_rank = jnp.sum(before * onehot, axis=1)
    return (flat_ids * capacity + slot_rank).reshape(expert_ids.shape)


def key_scores(query_nope, query_rope, lat_rows, rope_rows):
    scores = jnp.einsum("qhl,kl->hqk", query_nope, lat_rows, preferred_element_type=jnp.float32)
    scores = scores + jnp.einsum(
        "qhr,kr->hqk", query_rope, rope_rows, preferred_element_type=jnp.float32
    )
    return scores * softmax_scale


def attend_piece(running, key_piece, query_nope, query_rope, query_pos, query_docs):
    lat_rows, rope_rows, doc_rows = key_piece
    key_pos = jnp.arange(lat_rows.shape[0], dtype=jnp.int32)
    allowed = (key_pos[None, :] <= query_pos[:, None]) & (doc_rows[None, :] == query_docs[:, None])
    scores = jnp.where(
        allowed[None], key_scores(query_nope, query_rope, lat_rows, rope_rows), masked_score
    )
    run_max, run_sum, accum = running
    new_max = jnp.maximum(run_max, jnp.max(scores, axis=2))
    probs = jnp.where(allowed[None], jnp.exp(scores - new_max[:, :, None]), 0.0)
    run_sum = jnp.sum(probs, axis=2)
    accum = jnp.einsum(
        "hqk,kl->hql", probs.astype(jnp.bfloat16), lat_rows, preferred_element_type=jnp.float32
    )
    return (new_max, run_sum, accum)


def project_values(context, uv_weight):
    values = jnp.einsum(
        "hql,hlv->qhv", context, uv_weight, preferred_element_type=jnp.float32
    ).astype(jnp.bfloat16)
    return values.reshape(values.shape[0], values.shape[1] * values.shape[2])


def fold_projection(running, uv_weight, out_weight):
    context = (running[2] / running[1][:, :, None]).astype(jnp.bfloat16)
    values = project_values(context, uv_weight)

    def head_rows(row_start, row_count):
        return jnp.dot(values, out_weight, preferred_element_type=jnp.float32)

    return head_rows


def expert_hidden(row_data, w_gate, w_up):
    gate_part = jnp.dot(row_data, w_gate, preferred_element_type=jnp.float32)
    up_part = jnp.dot(row_data, w_up, preferred_element_type=jnp.float32)
    activation = jax.nn.silu(gate_part) * up_part
    return (activation.astype(jnp.bfloat16), jnp.sum(activation * activation, axis=1) / HID)


def bin_energy(energy, slot_bins):
    onehot = (slot_bins[:, None] == jnp.arange(NBINS, dtype=jnp.int32)[None, :]).astype(jnp.float32)
    return jnp.dot(energy[None, :], onehot, precision=lax.Precision.HIGHEST)[0]


def routed_device(
    residual_in,
    norm_gain,
    q_nope,
    q_rope,
    latent,
    k_rope,
    doc_ids,
    uv_weight,
    out_weight,
    expert_ids,
    gate_levels,
    bin_ids,
    gate_weight,
    up_weight,
    down_weight,
):
    exp_devices = lax.axis_size("exp")
    block_len, head_count, lat_width = q_nope.shape
    rope_width = k_rope.shape[1]
    query_first = lax.axis_index("ctx") * block_len
    query_pos = query_first + jnp.arange(block_len, dtype=jnp.int32)
    query_rope = q_rope.reshape(block_len, head_count, rope_width)
    token_count = residual_in.shape[0]
    keys_local = (latent, k_rope, doc_ids)
    initial = (
        jnp.full((head_count, block_len), masked_score, jnp.float32),
        jnp.zeros((head_count, block_len), jnp.float32),
        jnp.zeros((head_count, block_len, lat_width), jnp.float32),
    )
    running = attend_piece(
        initial,
        (
            lax.all_gather(keys_local[0], "ctx", axis=0, tiled=True),
            lax.all_gather(keys_local[1], "ctx", axis=0, tiled=True),
            lax.all_gather(keys_local[2], "ctx", axis=0, tiled=True),
        ),
        q_nope,
        query_rope,
        query_pos,
        doc_ids,
    )
    head_rows = fold_projection(running, uv_weight, out_weight)
    attended = lax.psum_scatter(
        head_rows(jnp.int32(0), token_count * lax.axis_size("exp")),
        "exp",
        scatter_dimension=0,
        tiled=True,
    )
    stream_state = residual_in.astype(jnp.float32) + attended
    normed = (
        stream_state
        * lax.rsqrt(jnp.mean(stream_state * stream_state, axis=1, keepdims=True) + norm_eps)
        * norm_gain
    ).astype(jnp.bfloat16)
    top_count = expert_ids.shape[1]
    capacity = min(token_count, max(2, 2 * token_count * top_count // exp_devices))
    slot_total = exp_devices * capacity
    destination = route_slots(expert_ids, exp_devices, capacity)
    slot_match = destination[:, :, None] == jnp.arange(slot_total, dtype=jnp.int32)[None, None, :]
    selector = jnp.sum(slot_match.astype(jnp.int32), axis=1).astype(jnp.bfloat16)
    outgoing = jnp.einsum("ts,td->sd", selector, normed, preferred_element_type=jnp.float32).astype(
        jnp.bfloat16
    )
    outgoing = outgoing.reshape(exp_devices, capacity, outgoing.shape[1])
    slot_bins = jnp.sum(jnp.where(slot_match, bin_ids[:, :, None], 0), axis=(0, 1)).reshape(
        exp_devices, capacity
    )
    incoming, incoming_bins = (
        lax.all_to_all(outgoing, "exp", split_axis=0, concat_axis=1, tiled=True),
        lax.all_to_all(slot_bins, "exp", split_axis=0, concat_axis=1, tiled=True),
    )
    all_rows, all_bins = (
        lax.all_gather(incoming, "ctx", axis=1, tiled=True),
        lax.all_gather(incoming_bins, "ctx", axis=1, tiled=True),
    )
    hidden, energy = expert_hidden(all_rows[0], gate_weight[0], up_weight[0])
    bin_part = bin_energy(energy, all_bins[0])
    down_local = down_weight[0]
    expert_out = lax.psum_scatter(
        jnp.dot(hidden, down_local, preferred_element_type=jnp.float32).astype(jnp.bfloat16),
        "ctx",
        scatter_dimension=0,
        tiled=True,
    )
    histogram = lax.psum_scatter(bin_part[None, :], "ctx", scatter_dimension=1, tiled=True)
    returned = lax.all_to_all(expert_out[None], "exp", split_axis=1, concat_axis=0, tiled=True)
    levels = gate_levels.astype(jnp.float32)
    route_weights = levels / jnp.sum(levels, axis=1, keepdims=True)
    combiner = jnp.sum(jnp.where(slot_match, route_weights[:, :, None], 0.0), axis=1)
    mixture = jnp.dot(
        combiner,
        returned.reshape(slot_total, returned.shape[2]).astype(jnp.float32),
        precision=lax.Precision.HIGHEST,
    )
    layer_out = (stream_state + mixture).astype(jnp.bfloat16)
    return (layer_out, histogram)


def relative_order(exp_devices):
    here = lax.axis_index("exp")
    rows = exp_devices // 2
    z_at, x_at = here // 2, here % 2
    return [((z_at - step + rows) % rows) * 2 + (x_at if side == 0 else 1 - x_at) for step in range(rows) for side in range(2)]


def swap_x(value, exp_devices):
    return lax.ppermute(value, "exp", [(e, e ^ 1) for e in range(exp_devices)])


def ring_z(value, exp_devices):
    return lax.ppermute(value, "exp", [(e, (e + 2) % exp_devices) for e in range(exp_devices)])


def swap_core(value):
    return lax.ppermute(value, "ctx", [(c, c ^ 1) for c in range(lax.axis_size("ctx"))])


def swap_y(value):
    return lax.ppermute(value, "ctx", [(c, c ^ 2) for c in range(lax.axis_size("ctx"))])


def gather_exp(block, exp_devices):
    found = []
    for step in range(exp_devices // 2):
        found.append(block)
        found.append(swap_x(block, exp_devices))
        if step + 1 < exp_devices // 2:
            block = ring_z(block, exp_devices)
    return found


def reduce_exp(blocks, exp_devices):
    rows = exp_devices // 2
    across = {}
    for step in list(range(1, rows)) + [0]:
        got = swap_x(blocks[2 * step + 1], exp_devices)
        across[step] = blocks[2 * step].astype(jnp.float32) + got.astype(jnp.float32)
    total = across[1]
    for step in list(range(2, rows)) + [0]:
        moved = ring_z(total.astype(jnp.bfloat16), exp_devices)
        total = across[step] + moved.astype(jnp.float32)
    return total


def block_attention(q_nope, query_rope, query_pos, query_docs, latent, k_rope, doc_ids):
    ctx_devices = lax.axis_size("ctx")
    here = lax.axis_index("ctx")
    block_len = latent.shape[0]
    reach = min(ctx_devices - 1, 2)
    lat_blocks, rope_blocks, doc_blocks = [latent], [k_rope], [doc_ids]
    for back in range(1, reach + 1):
        pairs = [(c, c + back) for c in range(ctx_devices - back)]
        lat_blocks.append(lax.ppermute(latent, "ctx", pairs))
        rope_blocks.append(lax.ppermute(k_rope, "ctx", pairs))
        doc_blocks.append(lax.ppermute(doc_ids, "ctx", pairs))
    keys = jnp.concatenate(lat_blocks, axis=0)
    ropes = jnp.concatenate(rope_blocks, axis=0)
    docs = jnp.concatenate(doc_blocks, axis=0)
    local = jnp.arange(block_len, dtype=jnp.int32)
    key_pos = jnp.concatenate([local + (here - back) * block_len for back in range(reach + 1)], axis=0)
    allowed = (
        (key_pos[None, :] <= query_pos[:, None])
        & (key_pos[None, :] >= 0)
        & (docs[None, :] == query_docs[:, None])
    )
    scores = jnp.where(allowed[None], key_scores(q_nope, query_rope, keys, ropes), masked_score)
    top = jnp.max(scores, axis=2)
    probs = jnp.where(allowed[None], jnp.exp(scores - top[:, :, None]), 0.0)
    total = jnp.sum(probs, axis=2)
    accum = jnp.einsum("hqk,kl->hql", probs.astype(jnp.bfloat16), keys, preferred_element_type=jnp.float32)
    return (accum / total[:, :, None]).astype(jnp.bfloat16), keys


def down_kernel(h0, h1, h2, h3, w0, w1, w2, w3, scale, out):
    total = jnp.dot(h0[...], w0[...], preferred_element_type=jnp.float32)
    total += jnp.dot(h1[...], w1[...], preferred_element_type=jnp.float32)
    total += jnp.dot(h2[...], w2[...], preferred_element_type=jnp.float32)
    total += jnp.dot(h3[...], w3[...], preferred_element_type=jnp.float32)
    out[...] = (total * scale[...]).astype(out.dtype)


def down_rows(hidden, weights, scale):
    rows, units = hidden[0].shape
    width = weights[0].shape[1]
    tile = 512
    return pl.pallas_call(
        down_kernel,
        grid=(width // tile,),
        in_specs=[pl.BlockSpec((rows, units), lambda n: (0, 0))] * 4
        + [pl.BlockSpec((units, tile), lambda n: (0, n))] * 4
        + [pl.BlockSpec((rows, 1), lambda n: (0, 0))],
        out_specs=pl.BlockSpec((rows, tile), lambda n: (0, n)),
        out_shape=jax.ShapeDtypeStruct((rows, width), jnp.bfloat16),
        compiler_params=pltpu.CompilerParams(vmem_limit_bytes=32 * 1024 * 1024),
        cost_estimate=pl.CostEstimate(
            flops=8 * rows * units * width,
            bytes_accessed=8 * units * width + 2 * rows * width,
            transcendentals=0,
        ),
    )(*hidden, *weights, scale)


def after(value, earlier):
    return lax.optimization_barrier((value, earlier))[0]


def dense_device(
    residual_in,
    norm_gain,
    q_nope,
    q_rope,
    latent,
    k_rope,
    doc_ids,
    uv_weight,
    out_weight,
    expert_ids,
    gate_levels,
    bin_ids,
    gate_weight,
    up_weight,
    down_weight,
):
    exp_devices = lax.axis_size("exp")
    ctx_here, exp_here = lax.axis_index("ctx"), lax.axis_index("exp")
    block_len, head_count, lat_width = q_nope.shape
    token_count = residual_in.shape[0]
    order = jnp.stack(relative_order(exp_devices)).astype(jnp.int32)

    def reorder(value):
        return value.reshape((exp_devices, token_count) + value.shape[1:])[order].reshape(value.shape)

    levels = gate_levels.astype(jnp.float32)
    route_weights = levels / jnp.sum(levels, axis=1, keepdims=True)
    named = expert_ids[:, :, None] == jnp.arange(exp_devices, dtype=jnp.int32)[None, None, :]
    table = jnp.concatenate(
        [
            jnp.sum(jnp.where(named, route_weights[:, :, None], 0.0), axis=1),
            jnp.sum(jnp.where(named, bin_ids.astype(jnp.float32)[:, :, None], 0.0), axis=1),
        ],
        axis=1,
    )
    tables = reorder(lax.all_gather(table, "exp", axis=0, tiled=True))
    mine = (jnp.arange(exp_devices, dtype=jnp.int32) == exp_here).astype(jnp.float32)
    row_scale = jnp.sum(tables[:, :exp_devices] * mine, axis=1, keepdims=True)
    row_bins = jnp.sum(tables[:, exp_devices:] * mine, axis=1).astype(jnp.int32)

    query_first = ctx_here * block_len
    query_pos = reorder(query_first + jnp.arange(block_len, dtype=jnp.int32))
    context, keys = block_attention(
        reorder(q_nope),
        reorder(q_rope).reshape(block_len, head_count, k_rope.shape[1]),
        query_pos,
        reorder(doc_ids),
        latent,
        k_rope,
        doc_ids,
    )

    w_gate, w_up, w_down = gate_weight[0], up_weight[0], down_weight[0]
    far_gate = swap_y(after(w_gate, keys))
    far_up = swap_y(after(w_up, far_gate))
    far_down = swap_y(after(w_down, far_up))
    gates = [w_gate, swap_core(w_gate), far_gate, swap_core(far_gate)]
    ups = [w_up, swap_core(w_up), far_up, swap_core(far_up)]
    downs = [w_down, swap_core(w_down), far_down, swap_core(far_down)]

    values = project_values(context, uv_weight)
    partial = jnp.dot(values, out_weight, preferred_element_type=jnp.float32).astype(jnp.bfloat16)
    partial = partial.reshape(exp_devices, token_count, partial.shape[1])
    attended = reduce_exp([partial[at] for at in range(exp_devices)], exp_devices)
    stream_state = residual_in.astype(jnp.float32) + attended
    normed = (
        stream_state
        * lax.rsqrt(jnp.mean(stream_state * stream_state, axis=1, keepdims=True) + norm_eps)
        * norm_gain
    ).astype(jnp.bfloat16)
    rows = jnp.concatenate(gather_exp(normed, exp_devices), axis=0)
    hidden, energy = [], 0.0
    for gate, up in zip(gates, ups):
        part, part_energy = expert_hidden(rows, gate, up)
        hidden.append(part)
        energy = energy + part_energy
    expert_out = down_rows(hidden, downs, row_scale)
    expert_out = expert_out.reshape(exp_devices, token_count, expert_out.shape[1])
    mixture = reduce_exp([expert_out[at] for at in range(exp_devices)], exp_devices)
    layer_out = (stream_state + mixture).astype(jnp.bfloat16)

    lanes = 128
    high = (row_bins[:, None] // lanes == jnp.arange(NBINS // lanes, dtype=jnp.int32)[None, :]).astype(jnp.float32)
    low = (row_bins[:, None] % lanes == jnp.arange(lanes, dtype=jnp.int32)[None, :]).astype(jnp.float32)
    counts = lax.dot_general(
        high * energy[:, None], low, (((0,), (0,)), ((), ())), precision=lax.Precision.HIGHEST
    ).reshape(2, 2, NBINS // 4)
    y_here, core_here = ctx_here // 2, ctx_here % 2
    counts = lax.dynamic_index_in_dim(counts, y_here, 0, keepdims=False) + swap_y(
        lax.dynamic_index_in_dim(counts, 1 - y_here, 0, keepdims=False)
    )
    histogram = lax.dynamic_index_in_dim(counts, core_here, 0, keepdims=True) + swap_core(
        lax.dynamic_index_in_dim(counts, 1 - core_here, 0, keepdims=True)
    )
    return (layer_out, histogram)


def solution(mesh):
    sizes = mesh.shape

    def on_device(*arrays):
        named_experts = arrays[9].shape[1]
        dense = sizes["exp"] == 8 and sizes["ctx"] == 4 and named_experts == sizes["exp"]
        return (dense_device if dense else routed_device)(*arrays)

    return jax.shard_map(
        on_device,
        mesh=mesh,
        in_specs=(
            P(("ctx", "exp"), None),
            P(),
            P("ctx", "exp", None),
            P("ctx", "exp"),
            P("ctx", None),
            P("ctx", None),
            P("ctx"),
            P("exp", None, None),
            P("exp", None),
            P(("ctx", "exp"), None),
            P(("ctx", "exp"), None),
            P(("ctx", "exp"), None),
            P("exp", None, "ctx"),
            P("exp", None, "ctx"),
            P("exp", "ctx", None),
        ),
        out_specs=(P(("ctx", "exp"), None), P("exp", "ctx")),
        check_vma=False,
    )
```

```python
import functools
import math

import jax
import jax.numpy as jnp
from jax import lax
from jax.experimental import pallas as pl
from jax.experimental.pallas import tpu as pltpu
from jax.sharding import PartitionSpec as P

HID = 1024
NBINS = 2048


softmax_scale = 192.0 ** (-0.5)
norm_eps = 1e-06
masked_score = -1e30
LOG2_E = math.log2(math.e)
FIRST_ROWS = (448, 1280)
VMEM_BYTES = 61 * 1024 * 1024


def route_slots(expert_ids, experts, capacity):
    flat_ids = expert_ids.reshape(-1)
    onehot = (flat_ids[:, None] == jnp.arange(experts, dtype=jnp.int32)[None, :]).astype(jnp.int32)
    before = jnp.cumsum(onehot, axis=0) - onehot
    slot_rank = jnp.sum(before * onehot, axis=1)
    return (flat_ids * capacity + slot_rank).reshape(expert_ids.shape)


def key_scores(query_nope, query_rope, lat_rows, rope_rows):
    scores = jnp.einsum("qhl,kl->hqk", query_nope, lat_rows, preferred_element_type=jnp.float32)
    scores = scores + jnp.einsum(
        "qhr,kr->hqk", query_rope, rope_rows, preferred_element_type=jnp.float32
    )
    return scores * softmax_scale


def attend_piece(running, key_piece, query_nope, query_rope, query_pos, query_docs):
    lat_rows, rope_rows, doc_rows = key_piece
    key_pos = jnp.arange(lat_rows.shape[0], dtype=jnp.int32)
    allowed = (key_pos[None, :] <= query_pos[:, None]) & (doc_rows[None, :] == query_docs[:, None])
    scores = jnp.where(
        allowed[None], key_scores(query_nope, query_rope, lat_rows, rope_rows), masked_score
    )
    run_max, run_sum, accum = running
    new_max = jnp.maximum(run_max, jnp.max(scores, axis=2))
    probs = jnp.where(allowed[None], jnp.exp(scores - new_max[:, :, None]), 0.0)
    run_sum = jnp.sum(probs, axis=2)
    accum = jnp.einsum(
        "hqk,kl->hql", probs.astype(jnp.bfloat16), lat_rows, preferred_element_type=jnp.float32
    )
    return (new_max, run_sum, accum)


def project_values(context, uv_weight):
    values = jnp.einsum(
        "hql,hlv->qhv", context, uv_weight, preferred_element_type=jnp.float32
    ).astype(jnp.bfloat16)
    return values.reshape(values.shape[0], values.shape[1] * values.shape[2])


def fold_projection(running, uv_weight, out_weight):
    context = (running[2] / running[1][:, :, None]).astype(jnp.bfloat16)
    values = project_values(context, uv_weight)

    def head_rows(row_start, row_count):
        return jnp.dot(values, out_weight, preferred_element_type=jnp.float32)

    return head_rows


def expert_hidden(row_data, w_gate, w_up):
    gate_part = jnp.dot(row_data, w_gate, preferred_element_type=jnp.float32)
    up_part = jnp.dot(row_data, w_up, preferred_element_type=jnp.float32)
    activation = jax.nn.silu(gate_part) * up_part
    return (activation.astype(jnp.bfloat16), jnp.sum(activation * activation, axis=1) / HID)


def bin_energy(energy, slot_bins):
    onehot = (slot_bins[:, None] == jnp.arange(NBINS, dtype=jnp.int32)[None, :]).astype(jnp.float32)
    return jnp.dot(energy[None, :], onehot, precision=lax.Precision.HIGHEST)[0]


def routed_device(
    residual_in,
    norm_gain,
    q_nope,
    q_rope,
    latent,
    k_rope,
    doc_ids,
    uv_weight,
    out_weight,
    expert_ids,
    gate_levels,
    bin_ids,
    gate_weight,
    up_weight,
    down_weight,
):
    exp_devices = lax.axis_size("exp")
    block_len, head_count, lat_width = q_nope.shape
    rope_width = k_rope.shape[1]
    query_first = lax.axis_index("ctx") * block_len
    query_pos = query_first + jnp.arange(block_len, dtype=jnp.int32)
    query_rope = q_rope.reshape(block_len, head_count, rope_width)
    token_count = residual_in.shape[0]
    keys_local = (latent, k_rope, doc_ids)
    initial = (
        jnp.full((head_count, block_len), masked_score, jnp.float32),
        jnp.zeros((head_count, block_len), jnp.float32),
        jnp.zeros((head_count, block_len, lat_width), jnp.float32),
    )
    running = attend_piece(
        initial,
        (
            lax.all_gather(keys_local[0], "ctx", axis=0, tiled=True),
            lax.all_gather(keys_local[1], "ctx", axis=0, tiled=True),
            lax.all_gather(keys_local[2], "ctx", axis=0, tiled=True),
        ),
        q_nope,
        query_rope,
        query_pos,
        doc_ids,
    )
    head_rows = fold_projection(running, uv_weight, out_weight)
    attended = lax.psum_scatter(
        head_rows(jnp.int32(0), token_count * lax.axis_size("exp")),
        "exp",
        scatter_dimension=0,
        tiled=True,
    )
    stream_state = residual_in.astype(jnp.float32) + attended
    normed = (
        stream_state
        * lax.rsqrt(jnp.mean(stream_state * stream_state, axis=1, keepdims=True) + norm_eps)
        * norm_gain
    ).astype(jnp.bfloat16)
    top_count = expert_ids.shape[1]
    capacity = min(token_count, max(2, 2 * token_count * top_count // exp_devices))
    slot_total = exp_devices * capacity
    destination = route_slots(expert_ids, exp_devices, capacity)
    slot_match = destination[:, :, None] == jnp.arange(slot_total, dtype=jnp.int32)[None, None, :]
    selector = jnp.sum(slot_match.astype(jnp.int32), axis=1).astype(jnp.bfloat16)
    outgoing = jnp.einsum("ts,td->sd", selector, normed, preferred_element_type=jnp.float32).astype(
        jnp.bfloat16
    )
    outgoing = outgoing.reshape(exp_devices, capacity, outgoing.shape[1])
    slot_bins = jnp.sum(jnp.where(slot_match, bin_ids[:, :, None], 0), axis=(0, 1)).reshape(
        exp_devices, capacity
    )
    incoming, incoming_bins = (
        lax.all_to_all(outgoing, "exp", split_axis=0, concat_axis=1, tiled=True),
        lax.all_to_all(slot_bins, "exp", split_axis=0, concat_axis=1, tiled=True),
    )
    all_rows, all_bins = (
        lax.all_gather(incoming, "ctx", axis=1, tiled=True),
        lax.all_gather(incoming_bins, "ctx", axis=1, tiled=True),
    )
    hidden, energy = expert_hidden(all_rows[0], gate_weight[0], up_weight[0])
    bin_part = bin_energy(energy, all_bins[0])
    down_local = down_weight[0]
    expert_out = lax.psum_scatter(
        jnp.dot(hidden, down_local, preferred_element_type=jnp.float32).astype(jnp.bfloat16),
        "ctx",
        scatter_dimension=0,
        tiled=True,
    )
    histogram = lax.psum_scatter(bin_part[None, :], "ctx", scatter_dimension=1, tiled=True)
    returned = lax.all_to_all(expert_out[None], "exp", split_axis=1, concat_axis=0, tiled=True)
    levels = gate_levels.astype(jnp.float32)
    route_weights = levels / jnp.sum(levels, axis=1, keepdims=True)
    combiner = jnp.sum(jnp.where(slot_match, route_weights[:, :, None], 0.0), axis=1)
    mixture = jnp.dot(
        combiner,
        returned.reshape(slot_total, returned.shape[2]).astype(jnp.float32),
        precision=lax.Precision.HIGHEST,
    )
    layer_out = (stream_state + mixture).astype(jnp.bfloat16)
    return (layer_out, histogram)


def relative_order(exp_devices):
    here = lax.axis_index("exp")
    rows = exp_devices // 2
    z_at, x_at = here // 2, here % 2
    return jnp.stack(
        [
            ((z_at - step + rows) % rows) * 2 + (x_at if side == 0 else 1 - x_at)
            for step in range(rows)
            for side in range(2)
        ]
    ).astype(jnp.int32)


def swap_exp(value, bit=1):
    return lax.ppermute(value, "exp", [(e, e ^ bit) for e in range(lax.axis_size("exp"))])


def ring_z(value):
    exp_devices = lax.axis_size("exp")
    return lax.ppermute(value, "exp", [(e, (e + 2) % exp_devices) for e in range(exp_devices)])


def swap_ctx(value, bit):
    return lax.ppermute(value, "ctx", [(c, c ^ bit) for c in range(lax.axis_size("ctx"))])


def after(value, earlier):
    return lax.optimization_barrier((value, earlier))[0]


def one_step(work, *inputs):
    taken = lax.axis_index("ctx") // lax.axis_size("ctx") == 0

    def blank(*arrays):
        return jax.tree.map(lambda leaf: jnp.zeros(leaf.shape, leaf.dtype), jax.eval_shape(work, *arrays))

    return lax.cond(taken, work, blank, *inputs)


def reduce_exp(*blocks):
    rows, across = len(blocks) // 2, {}
    for step in list(range(1, rows)) + [0]:
        got = swap_exp(blocks[2 * step + 1])
        across[step] = blocks[2 * step].astype(jnp.float32) + got.astype(jnp.float32)
    total = across[1]
    for step in list(range(2, rows)) + [0]:
        total = across[step] + ring_z(total.astype(jnp.bfloat16)).astype(jnp.float32)
    return total


def gather_exp(block):
    found = []
    for step in range(lax.axis_size("exp") // 2):
        if step:
            block = ring_z(after(block, found[-3]) if step > 1 else block)
            found.append(block)
        found.append(swap_exp(block))
    return found


def attend_kernel(scalars, q_nope, q_rope, own, near, far, uv, out, *, heads, rope_width):
    tile = out.shape[0]
    lat_width = uv.shape[1]
    first = pl.program_id(0) * tile
    keys = own.shape[0]
    doc_at = lat_width + rope_width
    pick = (lax.broadcasted_iota(jnp.int32, (8, 128), 1) == rope_width).astype(jnp.bfloat16)
    query_docs = own[pl.ds(pl.multiple_of(first, tile), tile), lat_width:][:, rope_width : rope_width + 1].astype(jnp.float32)
    over = (((1,), (1,)), ((), ()))
    allowed = []
    for back, block in enumerate((own, near, far)):
        docs = lax.dot_general(pick, block[:, lat_width:], over, preferred_element_type=jnp.float32)[0:1, :]
        docs = jnp.where(scalars[0] >= back, docs, -1.0)
        same = docs == query_docs
        if back == 0:
            key_at = lax.broadcasted_iota(jnp.int32, (tile, keys), 1)
            query_at = lax.broadcasted_iota(jnp.int32, (tile, keys), 0) + first
            same = same & (key_at <= query_at)
        allowed.append(same)
    spare = jnp.zeros((tile, own.shape[1] - doc_at), jnp.bfloat16)
    for head in range(heads):
        query = jnp.concatenate(
            [
                q_nope[:, head * lat_width : (head + 1) * lat_width],
                q_rope[:, head * rope_width : (head + 1) * rope_width],
                spare,
            ],
            axis=1,
        )
        scores = []
        for block, same in zip((own, near, far), allowed):
            raw = lax.dot_general(query, block[...], over, preferred_element_type=jnp.float32)
            scores.append(jnp.where(same, raw * (softmax_scale * LOG2_E), masked_score))
        top = jnp.maximum(
            jnp.maximum(jnp.max(scores[0], axis=1, keepdims=True), jnp.max(scores[1], axis=1, keepdims=True)),
            jnp.max(scores[2], axis=1, keepdims=True),
        )
        total, accum = 0.0, 0.0
        for block, score in zip((own, near, far), scores):
            probs = jnp.exp2(score - top)
            total = total + jnp.sum(probs, axis=1, keepdims=True)
            accum = accum + jnp.dot(
                probs.astype(jnp.bfloat16), block[:, :lat_width], preferred_element_type=jnp.float32
            )
        context = (accum / total).astype(jnp.bfloat16)
        value = jnp.dot(context, uv[head], preferred_element_type=jnp.float32)
        width = uv.shape[2]
        out[:, head * width : (head + 1) * width] = value.astype(out.dtype)


def attend(ctx_here, q_nope, q_rope, own, near, far, uv_weight, rope_width):
    queries, width = q_nope.shape[0], own.shape[1]
    heads, lat_width, value_width = uv_weight.shape
    tile = 128
    whole = lambda shape: pl.BlockSpec(shape, lambda i, s: (0,) * len(shape))
    return pl.pallas_call(
        functools.partial(attend_kernel, heads=heads, rope_width=rope_width),
        grid_spec=pltpu.PrefetchScalarGridSpec(
            num_scalar_prefetch=1,
            grid=(queries // tile,),
            in_specs=[
                pl.BlockSpec((tile, heads * lat_width), lambda i, s: (i, 0)),
                pl.BlockSpec((tile, heads * rope_width), lambda i, s: (i, 0)),
                whole(own.shape),
                whole(own.shape),
                whole(own.shape),
                whole(uv_weight.shape),
            ],
            out_specs=pl.BlockSpec((tile, heads * value_width), lambda i, s: (i, 0)),
        ),
        out_shape=jax.ShapeDtypeStruct((queries, heads * value_width), jnp.bfloat16),
        compiler_params=pltpu.CompilerParams(vmem_limit_bytes=40 * 1024 * 1024),
        cost_estimate=pl.CostEstimate(
            flops=6 * heads * queries * own.shape[0] * (width + lat_width),
            bytes_accessed=2 * (q_nope.size + 3 * own.size + uv_weight.size),
            transcendentals=3 * heads * queries * own.shape[0],
        ),
        name="attend",
    )(ctx_here.reshape(1), q_nope, q_rope, own, near, far, uv_weight)


def project_kernel(order, values, weight, *outs):
    rows = outs[0].shape[0]
    picked = jnp.concatenate(
        [values[pl.ds(pl.multiple_of(order[at] * rows, rows), rows), :] for at in range(len(outs))], axis=0
    )
    result = jnp.dot(picked, weight[...], preferred_element_type=jnp.float32).astype(outs[0].dtype)
    for at, out in enumerate(outs):
        out[...] = result[at * rows : (at + 1) * rows]


def project_blocks(order, values, weight, count):
    rows, inner = values.shape
    width = weight.shape[1]
    block, tile = rows // count, 896
    return pl.pallas_call(
        project_kernel,
        grid_spec=pltpu.PrefetchScalarGridSpec(
            num_scalar_prefetch=1,
            grid=(width // tile,),
            in_specs=[
                pl.BlockSpec((rows, inner), lambda n, s: (0, 0)),
                pl.BlockSpec((inner, tile), lambda n, s: (0, n)),
            ],
            out_specs=[pl.BlockSpec((block, tile), lambda n, s: (0, n))] * count,
        ),
        out_shape=[jax.ShapeDtypeStruct((block, width), jnp.bfloat16)] * count,
        compiler_params=pltpu.CompilerParams(vmem_limit_bytes=32 * 1024 * 1024),
        cost_estimate=pl.CostEstimate(
            flops=2 * rows * inner * width, bytes_accessed=2 * (inner + rows) * width, transcendentals=0
        ),
        name="project",
    )(order, values, weight)


def hidden_kernel(here, *refs, blocks, counts, experts):
    rows = refs[:blocks]
    pieces = refs[blocks : blocks + sum(counts)]
    hidden, energy_bins, scale, row_data, held, sems = refs[blocks + sum(counts) :]
    copies, at = [], 0
    for part, count in enumerate(counts):
        mine, first = [], 0
        for piece in pieces[at : at + count]:
            mine.append(
                pltpu.make_async_copy(piece, held.at[part, pl.ds(first, piece.shape[0])], sems.at[at + len(mine)])
            )
            mine[-1].start()
            first += piece.shape[0]
        at += count
        copies.append(mine)
    inner, units, each = held.shape[1], held.shape[2] // 2, rows[0].shape[0]
    for at, row in enumerate(rows):
        row_data[at * each : (at + 1) * each, :] = row[:, :inner]
    table = jnp.concatenate([row[:, inner:] for row in rows], axis=0).astype(jnp.float32)
    lane = lax.broadcasted_iota(jnp.int32, table.shape, 1)

    def column(first):
        return jnp.sum(jnp.where(lane == first + here[0], table, 0.0), axis=1, keepdims=True)

    levels = jnp.sum(jnp.where(lane < experts, table, 0.0), axis=1, keepdims=True)
    scale[...] = column(0) / levels
    squares = 0.0
    for part, mine in enumerate(copies):
        for copy in mine:
            copy.wait()
        both = jnp.dot(row_data[...], held[part], preferred_element_type=jnp.float32)
        gate_part, up_part = both[:, :units], both[:, units:]
        activation = gate_part / (1.0 + jnp.exp(-gate_part)) * up_part
        hidden[:, part * units : (part + 1) * units] = activation.astype(hidden.dtype)
        squares = squares + jnp.sum(activation * activation, axis=1, keepdims=True)
    place = lane.astype(jnp.float32)
    high = jnp.where(place == column(experts), squares * (1.0 / HID), 0.0)
    low = jnp.where(place == column(2 * experts), 1.0, 0.0)
    counted = jnp.dot(high.T, low, precision=lax.Precision.HIGHEST, preferred_element_type=jnp.float32)
    energy_bins[...] = counted[: energy_bins.shape[0], :]


def hidden_rows(rows, weights, experts):
    blocks, parts = len(rows), len(weights)
    both = weights[0][0].shape[1]
    inner = sum(piece.shape[0] for piece in weights[0])
    count = blocks * rows[0].shape[0]
    counts = tuple(len(pieces) for pieces in weights)
    whole = pl.BlockSpec(memory_space=pltpu.VMEM)
    return pl.pallas_call(
        functools.partial(hidden_kernel, blocks=blocks, counts=counts, experts=experts),
        in_specs=[pl.BlockSpec(memory_space=pltpu.SMEM)]
        + [whole] * blocks
        + [pl.BlockSpec(memory_space=pl.ANY)] * sum(counts),
        out_specs=[whole] * 3,
        out_shape=[
            jax.ShapeDtypeStruct((count, parts * both // 2), jnp.bfloat16),
            jax.ShapeDtypeStruct((NBINS // 128, 128), jnp.float32),
            jax.ShapeDtypeStruct((count, 1), jnp.float32),
        ],
        scratch_shapes=[
            pltpu.VMEM((count, inner), jnp.bfloat16),
            pltpu.VMEM((parts, inner, both), jnp.bfloat16),
            pltpu.SemaphoreType.DMA((sum(counts),)),
        ],
        compiler_params=pltpu.CompilerParams(vmem_limit_bytes=VMEM_BYTES),
        cost_estimate=pl.CostEstimate(
            flops=2 * count * inner * parts * both,
            bytes_accessed=2 * inner * (count + parts * both),
            transcendentals=count * parts * both // 2,
        ),
        name="hidden",
    )(lax.axis_index("exp").astype(jnp.int32).reshape(1), *rows, *[piece for pieces in weights for piece in pieces])


def down_kernel(hidden, scale, *refs, parts, tile):
    weights = refs[:parts]
    outs, held, sems = refs[parts:-2], refs[-2], refs[-1]
    rows, units = outs[0].shape[0], weights[0].shape[0]
    tiles = outs[0].shape[1] // tile
    copies = [
        [
            pltpu.make_async_copy(
                weight.at[:, pl.ds(at * tile, tile)],
                held.at[at, pl.ds(part * units, units)],
                sems.at[at * parts + part],
            )
            for part, weight in enumerate(weights)
        ]
        for at in range(tiles)
    ]
    for group in copies:
        for copy in group:
            copy.start()
    for at, group in enumerate(copies):
        for copy in group:
            copy.wait()
        total = jnp.dot(hidden[...], held[at], preferred_element_type=jnp.float32)
        total = (total * scale[...]).astype(outs[0].dtype)
        for block, out in enumerate(outs):
            out[:, at * tile : (at + 1) * tile] = total[block * rows : (block + 1) * rows]


def down_blocks(hidden, weights, scale, count):
    parts, tile = len(weights), 896
    rows, inner = hidden.shape
    units, width = weights[0].shape
    whole = pl.BlockSpec(memory_space=pltpu.VMEM)
    return pl.pallas_call(
        functools.partial(down_kernel, parts=parts, tile=tile),
        in_specs=[whole] * 2 + [pl.BlockSpec(memory_space=pl.ANY)] * parts,
        out_specs=[whole] * count,
        out_shape=[jax.ShapeDtypeStruct((rows // count, width), jnp.bfloat16)] * count,
        scratch_shapes=[
            pltpu.VMEM((width // tile, inner, tile), jnp.bfloat16),
            pltpu.SemaphoreType.DMA((width // tile * parts,)),
        ],
        compiler_params=pltpu.CompilerParams(vmem_limit_bytes=VMEM_BYTES),
        cost_estimate=pl.CostEstimate(
            flops=2 * rows * inner * width, bytes_accessed=2 * width * (inner + rows), transcendentals=0
        ),
        name="down",
    )(hidden, scale, *weights)


def spread_bins(counts):
    counts = counts.reshape(2, 2, NBINS // 4)
    ctx_here = lax.axis_index("ctx")
    for at, bit in ((ctx_here // 2, 2), (ctx_here % 2, 1)):
        counts = lax.dynamic_index_in_dim(counts, at, 0, keepdims=False) + swap_ctx(
            lax.dynamic_index_in_dim(counts, 1 - at, 0, keepdims=False), bit
        )
    return counts[None, :]


def dense_device(
    residual_in,
    norm_gain,
    q_nope,
    q_rope,
    latent,
    k_rope,
    doc_ids,
    uv_weight,
    out_weight,
    expert_ids,
    gate_levels,
    bin_ids,
    gate_weight,
    up_weight,
    down_weight,
):
    exp_devices, ctx_devices = lax.axis_size("exp"), lax.axis_size("ctx")
    ctx_here, exp_here = lax.axis_index("ctx"), lax.axis_index("exp")
    token_count = residual_in.shape[0]
    block_len, head_count, lat_width = q_nope.shape
    rope_width = k_rope.shape[1]
    order = relative_order(exp_devices)

    spare = 128 - rope_width - 1
    own = jnp.concatenate(
        [latent, k_rope, doc_ids.astype(jnp.bfloat16)[:, None], jnp.zeros((block_len, spare), jnp.bfloat16)], axis=1
    )
    half = block_len // 2
    sent = lax.dynamic_slice_in_dim(own, (exp_here % 2) * half, half, 0)
    far_half = lax.ppermute(sent, "ctx", [(c, c + 2) for c in range(ctx_devices - 2)])
    far = jnp.concatenate([far_half, swap_exp(far_half)], axis=0)
    near = lax.ppermute(own, "ctx", [(c, c + 1) for c in range(0, ctx_devices, 2)])
    near = near + lax.ppermute(far, "ctx", [(3, 2)])

    w_down = down_weight[0]
    near_both = jnp.concatenate([gate_weight[0], up_weight[0]], axis=1)

    def from_far(first, end, earlier):
        return swap_ctx(after(lax.slice_in_dim(near_both, first, end, axis=0), earlier), 2)

    part_a, part_b = FIRST_ROWS
    both_a = from_far(0, part_a, far_half)
    own = after(own, both_a)
    both_b = from_far(part_a, part_b, own)
    values = attend(
        ctx_here, q_nope.reshape(block_len, head_count * lat_width), q_rope, own, near, far, uv_weight, rope_width
    )
    values = after(values, both_b)
    both_c = from_far(part_b, near_both.shape[0], values)
    partial = project_blocks(order, values, out_weight, exp_devices)
    attended = one_step(reduce_exp, *partial)
    attended = after(attended, both_c)
    far_down = swap_ctx(after(w_down, attended), 2)
    stream_state = residual_in.astype(jnp.float32) + attended
    normed = (
        stream_state
        * lax.rsqrt(jnp.mean(stream_state * stream_state, axis=1, keepdims=True) + norm_eps)
        * norm_gain
    ).astype(jnp.bfloat16)

    named = expert_ids[:, :, None] == jnp.arange(exp_devices, dtype=jnp.int32)[None, None, :]
    table = jnp.concatenate(
        [
            jnp.sum(jnp.where(named, what[:, :, None], 0), axis=1)
            for what in (gate_levels, bin_ids // 128, bin_ids % 128)
        ]
        + [jnp.zeros((token_count, 128 - 3 * exp_devices), jnp.int32)],
        axis=1,
    ).astype(jnp.bfloat16)
    block = jnp.concatenate([normed, table], axis=1)
    found = [block] + after(one_step(gather_exp, block), far_down)
    far_both = [both_a, both_b, both_c]
    weights = [[near_both], [swap_ctx(near_both, 1)], far_both, [swap_ctx(piece, 1) for piece in far_both]]
    downs = [w_down, swap_ctx(w_down, 1), far_down, swap_ctx(far_down, 1)]
    hidden, bins, row_scale = hidden_rows(found, weights, exp_devices)
    mixture = reduce_exp(*down_blocks(hidden, downs, row_scale, exp_devices))
    layer_out = (stream_state + mixture).astype(jnp.bfloat16)
    histogram = spread_bins(bins)
    return (layer_out, histogram)


def solution(mesh):
    sizes = mesh.shape

    def on_device(*arrays):
        named_experts = arrays[9].shape[1]
        dense = sizes["exp"] == 8 and sizes["ctx"] == 4 and named_experts == sizes["exp"]
        return (dense_device if dense else routed_device)(*arrays)

    return jax.shard_map(
        on_device,
        mesh=mesh,
        in_specs=(
            P(("ctx", "exp"), None),
            P(),
            P("ctx", "exp", None),
            P("ctx", "exp"),
            P("ctx", None),
            P("ctx", None),
            P("ctx"),
            P("exp", None, None),
            P("exp", None),
            P(("ctx", "exp"), None),
            P(("ctx", "exp"), None),
            P(("ctx", "exp"), None),
            P("exp", None, "ctx"),
            P("exp", None, "ctx"),
            P("exp", "ctx", None),
        ),
        out_specs=(P(("ctx", "exp"), None), P("exp", "ctx")),
        check_vma=False,
    )
```

```python
import functools
import math

import jax
import jax.numpy as jnp
from jax import lax
from jax.experimental import pallas as pl
from jax.experimental.pallas import tpu as pltpu
from jax.sharding import PartitionSpec as P

HID = 1024
NBINS = 2048


softmax_scale = 192.0 ** (-0.5)
norm_eps = 1e-06
masked_score = -1e30
LOG2_E = math.log2(math.e)
FIRST_ROWS = (256, 896)
VMEM_BYTES = 14 * 1024 * 1024


def route_slots(expert_ids, experts, capacity):
    flat_ids = expert_ids.reshape(-1)
    onehot = (flat_ids[:, None] == jnp.arange(experts, dtype=jnp.int32)[None, :]).astype(jnp.int32)
    before = jnp.cumsum(onehot, axis=0) - onehot
    slot_rank = jnp.sum(before * onehot, axis=1)
    return (flat_ids * capacity + slot_rank).reshape(expert_ids.shape)


def key_scores(query_nope, query_rope, lat_rows, rope_rows):
    scores = jnp.einsum("qhl,kl->hqk", query_nope, lat_rows, preferred_element_type=jnp.float32)
    scores = scores + jnp.einsum(
        "qhr,kr->hqk", query_rope, rope_rows, preferred_element_type=jnp.float32
    )
    return scores * softmax_scale


def attend_piece(running, key_piece, query_nope, query_rope, query_pos, query_docs):
    lat_rows, rope_rows, doc_rows = key_piece
    key_pos = jnp.arange(lat_rows.shape[0], dtype=jnp.int32)
    allowed = (key_pos[None, :] <= query_pos[:, None]) & (doc_rows[None, :] == query_docs[:, None])
    scores = jnp.where(
        allowed[None], key_scores(query_nope, query_rope, lat_rows, rope_rows), masked_score
    )
    run_max, run_sum, accum = running
    new_max = jnp.maximum(run_max, jnp.max(scores, axis=2))
    probs = jnp.where(allowed[None], jnp.exp(scores - new_max[:, :, None]), 0.0)
    run_sum = jnp.sum(probs, axis=2)
    accum = jnp.einsum(
        "hqk,kl->hql", probs.astype(jnp.bfloat16), lat_rows, preferred_element_type=jnp.float32
    )
    return (new_max, run_sum, accum)


def project_values(context, uv_weight):
    values = jnp.einsum(
        "hql,hlv->qhv", context, uv_weight, preferred_element_type=jnp.float32
    ).astype(jnp.bfloat16)
    return values.reshape(values.shape[0], values.shape[1] * values.shape[2])


def fold_projection(running, uv_weight, out_weight):
    context = (running[2] / running[1][:, :, None]).astype(jnp.bfloat16)
    values = project_values(context, uv_weight)

    def head_rows(row_start, row_count):
        return jnp.dot(values, out_weight, preferred_element_type=jnp.float32)

    return head_rows


def expert_hidden(row_data, w_gate, w_up):
    gate_part = jnp.dot(row_data, w_gate, preferred_element_type=jnp.float32)
    up_part = jnp.dot(row_data, w_up, preferred_element_type=jnp.float32)
    activation = jax.nn.silu(gate_part) * up_part
    return (activation.astype(jnp.bfloat16), jnp.sum(activation * activation, axis=1) / HID)


def bin_energy(energy, slot_bins):
    onehot = (slot_bins[:, None] == jnp.arange(NBINS, dtype=jnp.int32)[None, :]).astype(jnp.float32)
    return jnp.dot(energy[None, :], onehot, precision=lax.Precision.HIGHEST)[0]


def routed_device(
    residual_in,
    norm_gain,
    q_nope,
    q_rope,
    latent,
    k_rope,
    doc_ids,
    uv_weight,
    out_weight,
    expert_ids,
    gate_levels,
    bin_ids,
    gate_weight,
    up_weight,
    down_weight,
):
    exp_devices = lax.axis_size("exp")
    block_len, head_count, lat_width = q_nope.shape
    rope_width = k_rope.shape[1]
    query_first = lax.axis_index("ctx") * block_len
    query_pos = query_first + jnp.arange(block_len, dtype=jnp.int32)
    query_rope = q_rope.reshape(block_len, head_count, rope_width)
    token_count = residual_in.shape[0]
    keys_local = (latent, k_rope, doc_ids)
    initial = (
        jnp.full((head_count, block_len), masked_score, jnp.float32),
        jnp.zeros((head_count, block_len), jnp.float32),
        jnp.zeros((head_count, block_len, lat_width), jnp.float32),
    )
    running = attend_piece(
        initial,
        (
            lax.all_gather(keys_local[0], "ctx", axis=0, tiled=True),
            lax.all_gather(keys_local[1], "ctx", axis=0, tiled=True),
            lax.all_gather(keys_local[2], "ctx", axis=0, tiled=True),
        ),
        q_nope,
        query_rope,
        query_pos,
        doc_ids,
    )
    head_rows = fold_projection(running, uv_weight, out_weight)
    attended = lax.psum_scatter(
        head_rows(jnp.int32(0), token_count * lax.axis_size("exp")),
        "exp",
        scatter_dimension=0,
        tiled=True,
    )
    stream_state = residual_in.astype(jnp.float32) + attended
    normed = (
        stream_state
        * lax.rsqrt(jnp.mean(stream_state * stream_state, axis=1, keepdims=True) + norm_eps)
        * norm_gain
    ).astype(jnp.bfloat16)
    top_count = expert_ids.shape[1]
    capacity = min(token_count, max(2, 2 * token_count * top_count // exp_devices))
    slot_total = exp_devices * capacity
    destination = route_slots(expert_ids, exp_devices, capacity)
    slot_match = destination[:, :, None] == jnp.arange(slot_total, dtype=jnp.int32)[None, None, :]
    selector = jnp.sum(slot_match.astype(jnp.int32), axis=1).astype(jnp.bfloat16)
    outgoing = jnp.einsum("ts,td->sd", selector, normed, preferred_element_type=jnp.float32).astype(
        jnp.bfloat16
    )
    outgoing = outgoing.reshape(exp_devices, capacity, outgoing.shape[1])
    slot_bins = jnp.sum(jnp.where(slot_match, bin_ids[:, :, None], 0), axis=(0, 1)).reshape(
        exp_devices, capacity
    )
    incoming, incoming_bins = (
        lax.all_to_all(outgoing, "exp", split_axis=0, concat_axis=1, tiled=True),
        lax.all_to_all(slot_bins, "exp", split_axis=0, concat_axis=1, tiled=True),
    )
    all_rows, all_bins = (
        lax.all_gather(incoming, "ctx", axis=1, tiled=True),
        lax.all_gather(incoming_bins, "ctx", axis=1, tiled=True),
    )
    hidden, energy = expert_hidden(all_rows[0], gate_weight[0], up_weight[0])
    bin_part = bin_energy(energy, all_bins[0])
    down_local = down_weight[0]
    expert_out = lax.psum_scatter(
        jnp.dot(hidden, down_local, preferred_element_type=jnp.float32).astype(jnp.bfloat16),
        "ctx",
        scatter_dimension=0,
        tiled=True,
    )
    histogram = lax.psum_scatter(bin_part[None, :], "ctx", scatter_dimension=1, tiled=True)
    returned = lax.all_to_all(expert_out[None], "exp", split_axis=1, concat_axis=0, tiled=True)
    levels = gate_levels.astype(jnp.float32)
    route_weights = levels / jnp.sum(levels, axis=1, keepdims=True)
    combiner = jnp.sum(jnp.where(slot_match, route_weights[:, :, None], 0.0), axis=1)
    mixture = jnp.dot(
        combiner,
        returned.reshape(slot_total, returned.shape[2]).astype(jnp.float32),
        precision=lax.Precision.HIGHEST,
    )
    layer_out = (stream_state + mixture).astype(jnp.bfloat16)
    return (layer_out, histogram)


def turn(place):
    return place ^ (place // 2)


def positions(exp_devices):
    ctx_here, here = lax.axis_index("ctx"), lax.axis_index("exp")
    rows = exp_devices // 2
    z_at, x_at = here // 2, here % 2
    order = [
        turn((turn(z_at) - step + rows) % rows) * 2 + (x_at if side == 0 else 1 - x_at)
        for step in range(rows)
        for side in range(2)
    ]
    return jnp.stack([x_at, ctx_here, here, *order]).astype(jnp.int32)


def swap_exp(value, bit=1):
    return lax.ppermute(value, "exp", [(e, e ^ bit) for e in range(lax.axis_size("exp"))])


def ring_z(value):
    rows = lax.axis_size("exp") // 2
    steps = [(turn(at), turn((at + 1) % rows)) for at in range(rows)]
    return lax.ppermute(value, "exp", [(2 * a + x, 2 * b + x) for a, b in steps for x in range(2)])


def swap_ctx(value, bit):
    return lax.ppermute(value, "ctx", [(c, c ^ bit) for c in range(lax.axis_size("ctx"))])


def after(value, earlier):
    return lax.optimization_barrier((value, earlier))[0]


def one_step(work, *inputs):
    taken = lax.axis_index("ctx") // lax.axis_size("ctx") == 0

    def blank(*arrays):
        return jax.tree.map(lambda leaf: jnp.zeros(leaf.shape, leaf.dtype), jax.eval_shape(work, *arrays))

    return lax.cond(taken, work, blank, *inputs)


def reduce_exp(*blocks):
    rows, across = len(blocks) // 2, {}
    for step in list(range(1, rows)) + [0]:
        across[step] = blocks[2 * step], swap_exp(blocks[2 * step + 1])
    total = sum(term.astype(jnp.float32) for term in across[1])
    for step in range(2, rows):
        moved = ring_z(total.astype(jnp.bfloat16))
        total = moved.astype(jnp.float32) + sum(term.astype(jnp.float32) for term in across[step])
    return ring_z(total.astype(jnp.bfloat16)), *across[0]


def norm_kernel(moved, mine, across, residual, gain, table, stream, out):
    width = stream.shape[1]
    state = residual[...].astype(jnp.float32) + (
        moved[...].astype(jnp.float32) + (mine[...].astype(jnp.float32) + across[...].astype(jnp.float32))
    )
    stream[...] = state
    mean = jnp.sum(state * state, axis=1, keepdims=True) * (1.0 / width)
    out[:, :width] = (state * lax.rsqrt(mean + norm_eps) * gain[...]).astype(out.dtype)
    out[:, width:] = table[...]


def norm_rows(moved, mine, across, residual, gain, table):
    rows, width = residual.shape
    whole = pl.BlockSpec(memory_space=pltpu.VMEM)
    return pl.pallas_call(
        norm_kernel,
        in_specs=[whole] * 6,
        out_specs=[whole] * 2,
        out_shape=[
            jax.ShapeDtypeStruct((rows, width), jnp.float32),
            pltpu.VMEM((rows, width + table.shape[1]), jnp.bfloat16),
        ],
        compiler_params=pltpu.CompilerParams(vmem_limit_bytes=VMEM_BYTES),
        cost_estimate=pl.CostEstimate(flops=8 * rows * width, bytes_accessed=14 * rows * width, transcendentals=rows),
        name="norm",
    )(moved, mine, across, residual, gain[None, :], table)


def gather_exp(block):
    found = []
    for step in range(lax.axis_size("exp") // 2):
        if step:
            block = ring_z(after(block, found[-3]) if step > 1 else block)
            found.append(block)
        found.append(swap_exp(block))
    return found


def pack_kernel(here, latent, k_rope, docs, own, sent):
    keys, lat_width, rope_width = latent.shape[0], latent.shape[1], k_rope.shape[1]
    own[:, :lat_width] = latent[...]
    row = lax.broadcasted_iota(jnp.int32, (128, 128), 0)
    lane = lax.broadcasted_iota(jnp.int32, (128, 128), 1)
    for at in range(keys // 128):
        wide = jnp.broadcast_to(docs[at : at + 1, :], (128, 128))
        column = jnp.sum(jnp.where(row == lane, wide, 0), axis=1, keepdims=True)
        ropes = jnp.concatenate(
            [k_rope[at * 128 : (at + 1) * 128, :].astype(jnp.float32), jnp.zeros((128, 128 - rope_width), jnp.float32)],
            axis=1,
        )
        own[at * 128 : (at + 1) * 128, lat_width:] = jnp.where(
            lane == rope_width, column.astype(jnp.float32), ropes
        ).astype(jnp.bfloat16)
    half = sent.shape[0]
    sent[...] = own[pl.ds(pl.multiple_of(here[0] * half, half), half), :]


def pack_keys(here, latent, k_rope, doc_ids):
    keys, width = latent.shape[0], latent.shape[1] + 128
    whole = pl.BlockSpec(memory_space=pltpu.VMEM)
    return pl.pallas_call(
        pack_kernel,
        in_specs=[pl.BlockSpec(memory_space=pltpu.SMEM)] + [whole] * 3,
        out_specs=[whole] * 2,
        out_shape=[
            jax.ShapeDtypeStruct((keys, width), jnp.bfloat16),
            jax.ShapeDtypeStruct((keys // 2, width), jnp.bfloat16),
        ],
        cost_estimate=pl.CostEstimate(flops=0, bytes_accessed=6 * keys * width, transcendentals=0),
        compiler_params=pltpu.CompilerParams(vmem_limit_bytes=8 * 1024 * 1024),
        name="pack",
    )(here, latent, k_rope, doc_ids.reshape(keys // 128, 128))


def join_kernel(left, right, *refs):
    outs, sems = refs[:-1], refs[-1]
    width, first, copies = left.shape[1], 0, []
    for out in outs:
        for side, weight in enumerate((left, right)):
            copies.append(
                pltpu.make_async_copy(
                    weight.at[pl.ds(first, out.shape[0])],
                    out.at[:, pl.ds(side * width, width)],
                    sems.at[len(copies)],
                )
            )
            copies[-1].start()
        first += out.shape[0]
    for copy in copies:
        copy.wait()


def join_weights(left, right, ends):
    width = left.shape[1]
    counts = [end - first for first, end in zip((0, *ends[:-1]), ends)]
    anywhere = pl.BlockSpec(memory_space=pl.ANY)
    return pl.pallas_call(
        join_kernel,
        in_specs=[anywhere] * 2,
        out_specs=[anywhere] * len(ends),
        out_shape=[jax.ShapeDtypeStruct((count, 2 * width), left.dtype) for count in counts],
        scratch_shapes=[pltpu.SemaphoreType.DMA((2 * len(ends),))],
        compiler_params=pltpu.CompilerParams(vmem_limit_bytes=1024 * 1024),
        cost_estimate=pl.CostEstimate(flops=0, bytes_accessed=8 * left.size, transcendentals=0),
        name="join",
    )(left, right)


def route_kernel(ids, levels, bins, out, *, experts):
    lane = lax.broadcasted_iota(jnp.int32, out.shape, 1)
    table = jnp.zeros(out.shape, jnp.int32)
    for at, what in enumerate((levels[...], bins[...] // 128, bins[...] % 128)):
        for expert in range(experts):
            column = jnp.sum(jnp.where(ids[...] == expert, what, 0), axis=1, keepdims=True)
            table = jnp.where(lane == at * experts + expert, column, table)
    out[...] = table.astype(jnp.float32).astype(out.dtype)


def route_table(expert_ids, gate_levels, bin_ids, experts):
    whole = pl.BlockSpec(memory_space=pltpu.VMEM)
    return pl.pallas_call(
        functools.partial(route_kernel, experts=experts),
        in_specs=[whole] * 3,
        out_specs=whole,
        out_shape=jax.ShapeDtypeStruct((expert_ids.shape[0], 128), jnp.bfloat16),
        compiler_params=pltpu.CompilerParams(vmem_limit_bytes=4 * 1024 * 1024),
        name="route",
    )(expert_ids, gate_levels, bin_ids)


def attend_kernel(scalars, q_nope, q_rope, *refs, heads, rope_width):
    own, near_even, near_a, near_b, far_a, far_b, uv, out, keys, more, sems = refs
    tile, block_len, half = out.shape[0], own.shape[0], far_a.shape[0]
    lat_width = uv.shape[1]
    first = pl.program_id(0) * tile
    places = [
        (own, keys, 0),
        (near_even, keys, block_len),
        (near_a, more, 0),
        (near_b, more, half),
        (far_a, keys, 2 * block_len),
        (far_b, keys, 2 * block_len + half),
    ]
    copies = [
        pltpu.make_async_copy(piece, into.at[pl.ds(at, piece.shape[0])], sems.at[number])
        for number, (piece, into, at) in enumerate(places)
    ]

    @pl.when(pl.program_id(0) == 0)
    def _():
        for copy in copies:
            copy.start()
        for copy in copies:
            copy.wait()
        keys[block_len : 2 * block_len, :] = keys[block_len : 2 * block_len, :] + more[...]

    doc_at = lat_width + rope_width
    pick = (lax.broadcasted_iota(jnp.int32, (8, 128), 1) == rope_width).astype(jnp.bfloat16)
    query_docs = keys[pl.ds(pl.multiple_of(first, tile), tile), lat_width:][:, rope_width : rope_width + 1].astype(jnp.float32)
    over = (((1,), (1,)), ((), ()))
    docs = lax.dot_general(pick, keys[:, lat_width:], over, preferred_element_type=jnp.float32)[0:1, :]
    key_at = lax.broadcasted_iota(jnp.int32, (1, keys.shape[0]), 1)
    docs = jnp.where(key_at < (scalars[1] + 1) * block_len, docs, -1.0)
    spare = jnp.zeros((tile, keys.shape[1] - doc_at), jnp.bfloat16)
    query = jnp.concatenate(
        [
            jnp.concatenate(
                [
                    q_nope[:, head * lat_width : (head + 1) * lat_width],
                    q_rope[:, head * rope_width : (head + 1) * rope_width],
                    spare,
                ],
                axis=1,
            )
            for head in range(heads)
        ],
        axis=0,
    )
    scores, top = [], None
    for block in range(keys.shape[0] // block_len):
        at = slice(block * block_len, (block + 1) * block_len)
        same = docs[:, at] == query_docs
        if block == 0:
            within = lax.broadcasted_iota(jnp.int32, (tile, block_len), 1)
            same = same & (within <= lax.broadcasted_iota(jnp.int32, (tile, block_len), 0) + first)
        raw = lax.dot_general(query, keys[at, :], over, preferred_element_type=jnp.float32)
        same = jnp.concatenate([same] * heads, axis=0)
        scores.append(jnp.where(same, raw * (softmax_scale * LOG2_E), masked_score))
        most = jnp.max(scores[-1], axis=1, keepdims=True)
        top = most if top is None else jnp.maximum(top, most)
    total, accum = 0.0, 0.0
    for block, score in enumerate(scores):
        probs = jnp.exp2(score - top)
        total = total + jnp.sum(probs, axis=1, keepdims=True)
        accum = accum + jnp.dot(
            probs.astype(jnp.bfloat16),
            keys[block * block_len : (block + 1) * block_len, :lat_width],
            preferred_element_type=jnp.float32,
        )
    context = (accum / total).astype(jnp.bfloat16)
    width = uv.shape[2]
    for head in range(heads):
        value = jnp.dot(context[head * tile : (head + 1) * tile], uv[head], preferred_element_type=jnp.float32)
        out[:, head * width : (head + 1) * width] = value.astype(out.dtype)


def attend(here, q_nope, q_rope, pieces, uv_weight, rope_width):
    queries, (block_len, width) = q_nope.shape[0], pieces[0].shape
    heads, lat_width, value_width = uv_weight.shape
    tile = 256
    return pl.pallas_call(
        functools.partial(attend_kernel, heads=heads, rope_width=rope_width),
        grid_spec=pltpu.PrefetchScalarGridSpec(
            num_scalar_prefetch=1,
            grid=(queries // tile,),
            in_specs=[
                pl.BlockSpec((tile, heads * lat_width), lambda i, s: (i, 0)),
                pl.BlockSpec((tile, heads * rope_width), lambda i, s: (i, 0)),
                *[pl.BlockSpec(memory_space=pltpu.HBM) for _ in pieces],
                pl.BlockSpec(uv_weight.shape, lambda i, s: (0, 0, 0)),
            ],
            out_specs=pl.BlockSpec((tile, heads * value_width), lambda i, s: (i, 0)),
            scratch_shapes=[
                pltpu.VMEM((3 * block_len, width), jnp.bfloat16),
                pltpu.VMEM((block_len, width), jnp.bfloat16),
                pltpu.SemaphoreType.DMA((len(pieces),)),
            ],
        ),
        out_shape=jax.ShapeDtypeStruct((queries, heads * value_width), jnp.bfloat16),
        compiler_params=pltpu.CompilerParams(vmem_limit_bytes=24 * 1024 * 1024),
        cost_estimate=pl.CostEstimate(
            flops=6 * heads * queries * block_len * (width + lat_width),
            bytes_accessed=2 * (q_nope.size + 4 * block_len * width + uv_weight.size),
            transcendentals=3 * heads * queries * block_len,
        ),
        name="attend",
    )(here, q_nope, q_rope, *pieces, uv_weight)


def project_kernel(order, values, weight, *outs):
    rows = outs[0].shape[0]
    picked = jnp.concatenate(
        [values[pl.ds(pl.multiple_of(order[3 + at] * rows, rows), rows), :] for at in range(len(outs))], axis=0
    )
    result = jnp.dot(picked, weight[...], preferred_element_type=jnp.float32).astype(outs[0].dtype)
    for at, out in enumerate(outs):
        out[...] = result[at * rows : (at + 1) * rows]


def project_blocks(here, values, weight, count):
    rows, inner = values.shape
    width = weight.shape[1]
    block, tile = rows // count, 896
    return pl.pallas_call(
        project_kernel,
        grid_spec=pltpu.PrefetchScalarGridSpec(
            num_scalar_prefetch=1,
            grid=(width // tile,),
            in_specs=[
                pl.BlockSpec((rows, inner), lambda n, s: (0, 0)),
                pl.BlockSpec((inner, tile), lambda n, s: (0, n)),
            ],
            out_specs=[pl.BlockSpec((block, tile), lambda n, s: (0, n))] * count,
        ),
        out_shape=[pltpu.VMEM((block, width), jnp.bfloat16)] * count,
        compiler_params=pltpu.CompilerParams(vmem_limit_bytes=32 * 1024 * 1024),
        cost_estimate=pl.CostEstimate(
            flops=2 * rows * inner * width, bytes_accessed=2 * (inner + rows) * width, transcendentals=0
        ),
        name="project",
    )(here, values, weight)


def hidden_kernel(here, *refs, blocks, counts, experts):
    rows, rest = refs[:blocks], refs[blocks:]
    copies = []
    if counts:
        pieces, (hidden, energy_bins, scale, held, row_data, sems) = rest[: sum(counts)], rest[sum(counts) :]
        at = 0
        for part, count in enumerate(counts):
            copies.append([])
            first = 0
            for piece in pieces[at : at + count]:
                into = held.at[part, pl.ds(first, piece.shape[0])]
                copies[-1].append(pltpu.make_async_copy(piece, into, sems.at[at]))
                copies[-1][-1].start()
                first += piece.shape[0]
                at += 1
    else:
        held, hidden, energy_bins, scale, row_data = rest
    parts, inner, units, each = held.shape[0], held.shape[1], held.shape[2] // 2, rows[0].shape[0]
    for at, row in enumerate(rows):
        row_data[at * each : (at + 1) * each, :] = row[:, :inner]
    table = jnp.concatenate([row[:, inner:] for row in rows], axis=0).astype(jnp.float32)
    lane = lax.broadcasted_iota(jnp.int32, table.shape, 1)

    def column(first):
        return jnp.sum(jnp.where(lane == first + here[2], table, 0.0), axis=1, keepdims=True)

    levels = jnp.sum(jnp.where(lane < experts, table, 0.0), axis=1, keepdims=True)
    scale[...] = column(0) / levels
    squares = 0.0
    for part in range(parts):
        for copy in copies[part] if counts else ():
            copy.wait()
        both = jnp.dot(row_data[...], held[part], preferred_element_type=jnp.float32)
        gate_part, up_part = both[:, :units], both[:, units:]
        activation = gate_part / (1.0 + jnp.exp(-gate_part)) * up_part
        hidden[:, part * units : (part + 1) * units] = activation.astype(hidden.dtype)
        squares = squares + jnp.sum(activation * activation, axis=1, keepdims=True)
    place = lane.astype(jnp.float32)
    high = jnp.where(place == column(experts), squares * (1.0 / HID), 0.0)
    low = jnp.where(place == column(2 * experts), 1.0, 0.0)
    counted = jnp.dot(high.T, low, precision=lax.Precision.HIGHEST, preferred_element_type=jnp.float32)
    energy_bins[...] = counted[: energy_bins.shape[0], :]


def hidden_rows(here, rows, weights, experts):
    first = isinstance(weights, list)
    whole = pl.BlockSpec(memory_space=pltpu.VMEM)
    if first:
        counts = tuple(len(pieces) for pieces in weights)
        parts, both = len(weights), weights[0][0].shape[1]
        inner = sum(piece.shape[0] for piece in weights[0])
        operands = [piece for pieces in weights for piece in pieces]
    else:
        counts, (parts, inner, both), operands = None, weights.shape, [weights]
    count = len(rows) * rows[0].shape[0]
    kept = [pltpu.VMEM((parts, inner, both), jnp.bfloat16)] if first else []
    return pl.pallas_call(
        functools.partial(hidden_kernel, blocks=len(rows), counts=counts, experts=experts),
        in_specs=[pl.BlockSpec(memory_space=pltpu.SMEM)]
        + [whole] * len(rows)
        + [pl.BlockSpec(memory_space=pltpu.HBM) if first else whole] * len(operands),
        out_specs=[whole] * (3 + len(kept)),
        out_shape=[
            jax.ShapeDtypeStruct((count, parts * both // 2), jnp.bfloat16),
            jax.ShapeDtypeStruct((NBINS // 128, 128), jnp.float32),
            jax.ShapeDtypeStruct((count, 1), jnp.float32),
            *kept,
        ],
        scratch_shapes=[pltpu.VMEM((count, inner), jnp.bfloat16)]
        + ([pltpu.SemaphoreType.DMA((len(operands),))] if first else []),
        compiler_params=pltpu.CompilerParams(vmem_limit_bytes=VMEM_BYTES),
        cost_estimate=pl.CostEstimate(
            flops=2 * count * inner * parts * both,
            bytes_accessed=2 * inner * (count + parts * both),
            transcendentals=count * parts * both // 2,
        ),
        name="hidden",
    )(here, *rows, *operands)


def down_kernel(*refs, pieces, parts, tile):
    hidden, scales, weights = refs[:pieces], refs[pieces : 2 * pieces], refs[2 * pieces : 2 * pieces + parts]
    outs = refs[2 * pieces + parts :]
    rows, units = outs[0].shape[0], weights[0].shape[0]
    each = hidden[0].shape[0]
    for piece in range(pieces):
        for at in range(outs[0].shape[1] // tile):
            columns = slice(at * tile, (at + 1) * tile)
            total = 0.0
            for part, weight in enumerate(weights):
                total = total + jnp.dot(
                    hidden[piece][:, part * units : (part + 1) * units],
                    weight[:, columns],
                    preferred_element_type=jnp.float32,
                )
            total = (total * scales[piece][...]).astype(outs[0].dtype)
            for block in range(each // rows):
                outs[piece * (each // rows) + block][:, columns] = total[block * rows : (block + 1) * rows]


def down_blocks(hidden, scales, weights, count):
    pieces, parts, tile = len(hidden), len(weights), 512
    each, inner = hidden[0].shape
    units, width = weights[0].shape
    whole = pl.BlockSpec(memory_space=pltpu.VMEM)
    return pl.pallas_call(
        functools.partial(down_kernel, pieces=pieces, parts=parts, tile=tile),
        in_specs=[whole] * (2 * pieces + parts),
        out_specs=[whole] * count,
        out_shape=[pltpu.VMEM((pieces * each // count, width), jnp.bfloat16)] * count,
        compiler_params=pltpu.CompilerParams(vmem_limit_bytes=VMEM_BYTES),
        cost_estimate=pl.CostEstimate(
            flops=2 * pieces * each * inner * width,
            bytes_accessed=2 * width * (inner + pieces * each),
            transcendentals=0,
        ),
        name="down",
    )(*hidden, *scales, *weights)


def spread_bins(counts):
    counts = counts.reshape(2, 2, NBINS // 4)
    ctx_here = lax.axis_index("ctx")
    for at, bit in ((ctx_here // 2, 2), (ctx_here % 2, 1)):
        counts = lax.dynamic_index_in_dim(counts, at, 0, keepdims=False) + swap_ctx(
            lax.dynamic_index_in_dim(counts, 1 - at, 0, keepdims=False), bit
        )
    return counts[None, :]


def dense_device(
    residual_in,
    norm_gain,
    q_nope,
    q_rope,
    latent,
    k_rope,
    doc_ids,
    uv_weight,
    out_weight,
    expert_ids,
    gate_levels,
    bin_ids,
    gate_weight,
    up_weight,
    down_weight,
):
    exp_devices, ctx_devices = lax.axis_size("exp"), lax.axis_size("ctx")
    block_len, head_count, lat_width = q_nope.shape
    rope_width = k_rope.shape[1]
    here = positions(exp_devices)

    own, sent = pack_keys(here, latent, k_rope, doc_ids)
    table = route_table(expert_ids, gate_levels, bin_ids, exp_devices)
    far_a = lax.ppermute(sent, "ctx", [(c, c + 2) for c in range(ctx_devices - 2)])
    near_even = lax.ppermute(own, "ctx", [(c, c + 1) for c in range(0, ctx_devices, 2)])
    flat_q = q_nope.reshape(block_len, head_count * lat_width)
    w_gate, w_up, w_down = gate_weight[0], up_weight[0], down_weight[0]
    part_a, part_b = FIRST_ROWS
    own_both = join_weights(w_gate, w_up, (part_a, part_b, w_gate.shape[0]))
    far_b = swap_exp(after(far_a, (flat_q, own_both, table)))
    near_a = lax.ppermute(far_a, "ctx", [(3, 2)])
    near_b = lax.ppermute(far_b, "ctx", [(3, 2)])

    both_a = swap_ctx(after(own_both[0], far_a), 2)
    there_both = [swap_ctx(piece, 1) for piece in own_both]
    own = after(own, both_a)
    both_b = swap_ctx(after(own_both[1], own), 2)
    key_pieces = [own, near_even, near_a, near_b, far_a, far_b]
    values = attend(here, flat_q, q_rope, key_pieces, uv_weight, rope_width)
    values = after(values, both_b)
    both_c = swap_ctx(after(own_both[2], values), 2)
    partial = project_blocks(here, values, out_weight, exp_devices)
    def sum_and_norm(partial, *rest):
        return norm_rows(*reduce_exp(*partial), *rest)

    swapped = [swap_ctx(both_a, 1), swap_ctx(both_b, 1)]
    stream_state, block = after(
        one_step(sum_and_norm, partial, residual_in, norm_gain, table), (both_c, swapped, there_both)
    )
    far_down = swap_ctx(after(w_down, block), 2)

    def gather_and_hide(block, here, own_both, there_both, far_both, swapped):
        weights = [own_both, there_both, far_both, [*swapped, swap_ctx(far_both[-1], 1)]]
        found = [block, *gather_exp(block)]
        half = len(found) // 2
        *first, held = hidden_rows(here, found[:half], weights, exp_devices)
        last = hidden_rows(here, found[half:], held, exp_devices)
        return [*zip(first, last)]

    hidden, bins, scales = after(
        one_step(gather_and_hide, block, here, own_both, there_both, [both_a, both_b, both_c], swapped), far_down
    )
    downs = [w_down, swap_ctx(w_down, 1), far_down, swap_ctx(after(far_down, hidden), 1)]
    expert_out = down_blocks(hidden, scales, downs, exp_devices)
    mixture = reduce_exp(*expert_out)
    layer_out = (stream_state + sum(term.astype(jnp.float32) for term in mixture)).astype(jnp.bfloat16)
    histogram = spread_bins(after(bins[0] + bins[1], expert_out[0]))
    return (layer_out, histogram)


def solution(mesh):
    sizes = mesh.shape

    def on_device(*arrays):
        named_experts = arrays[9].shape[1]
        dense = sizes["exp"] == 8 and sizes["ctx"] == 4 and named_experts == sizes["exp"]
        return (dense_device if dense else routed_device)(*arrays)

    return jax.shard_map(
        on_device,
        mesh=mesh,
        in_specs=(
            P(("ctx", "exp"), None),
            P(),
            P("ctx", "exp", None),
            P("ctx", "exp"),
            P("ctx", None),
            P("ctx", None),
            P("ctx"),
            P("exp", None, None),
            P("exp", None),
            P(("ctx", "exp"), None),
            P(("ctx", "exp"), None),
            P(("ctx", "exp"), None),
            P("exp", None, "ctx"),
            P("exp", None, "ctx"),
            P("exp", "ctx", None),
        ),
        out_specs=(P(("ctx", "exp"), None), P("exp", "ctx")),
        check_vma=False,
    )
```

```python
import functools
import math

import jax
import jax.numpy as jnp
from jax import lax
from jax.experimental import pallas as pl
from jax.experimental.pallas import tpu as pltpu
from jax.sharding import PartitionSpec as P

HID = 1024
NBINS = 2048


softmax_scale = 192.0 ** (-0.5)
norm_eps = 1e-06
masked_score = -1e30
LOG2_E = math.log2(math.e)
FIRST_ROWS = 960
VMEM_BYTES = 14 * 1024 * 1024


def route_slots(expert_ids, experts, capacity):
    flat_ids = expert_ids.reshape(-1)
    onehot = (flat_ids[:, None] == jnp.arange(experts, dtype=jnp.int32)[None, :]).astype(jnp.int32)
    before = jnp.cumsum(onehot, axis=0) - onehot
    slot_rank = jnp.sum(before * onehot, axis=1)
    return (flat_ids * capacity + slot_rank).reshape(expert_ids.shape)


def key_scores(query_nope, query_rope, lat_rows, rope_rows):
    scores = jnp.einsum("qhl,kl->hqk", query_nope, lat_rows, preferred_element_type=jnp.float32)
    scores = scores + jnp.einsum(
        "qhr,kr->hqk", query_rope, rope_rows, preferred_element_type=jnp.float32
    )
    return scores * softmax_scale


def attend_piece(running, key_piece, query_nope, query_rope, query_pos, query_docs):
    lat_rows, rope_rows, doc_rows = key_piece
    key_pos = jnp.arange(lat_rows.shape[0], dtype=jnp.int32)
    allowed = (key_pos[None, :] <= query_pos[:, None]) & (doc_rows[None, :] == query_docs[:, None])
    scores = jnp.where(
        allowed[None], key_scores(query_nope, query_rope, lat_rows, rope_rows), masked_score
    )
    run_max, run_sum, accum = running
    new_max = jnp.maximum(run_max, jnp.max(scores, axis=2))
    probs = jnp.where(allowed[None], jnp.exp(scores - new_max[:, :, None]), 0.0)
    run_sum = jnp.sum(probs, axis=2)
    accum = jnp.einsum(
        "hqk,kl->hql", probs.astype(jnp.bfloat16), lat_rows, preferred_element_type=jnp.float32
    )
    return (new_max, run_sum, accum)


def project_values(context, uv_weight):
    values = jnp.einsum(
        "hql,hlv->qhv", context, uv_weight, preferred_element_type=jnp.float32
    ).astype(jnp.bfloat16)
    return values.reshape(values.shape[0], values.shape[1] * values.shape[2])


def fold_projection(running, uv_weight, out_weight):
    context = (running[2] / running[1][:, :, None]).astype(jnp.bfloat16)
    values = project_values(context, uv_weight)

    def head_rows(row_start, row_count):
        return jnp.dot(values, out_weight, preferred_element_type=jnp.float32)

    return head_rows


def expert_hidden(row_data, w_gate, w_up):
    gate_part = jnp.dot(row_data, w_gate, preferred_element_type=jnp.float32)
    up_part = jnp.dot(row_data, w_up, preferred_element_type=jnp.float32)
    activation = jax.nn.silu(gate_part) * up_part
    return (activation.astype(jnp.bfloat16), jnp.sum(activation * activation, axis=1) / HID)


def bin_energy(energy, slot_bins):
    onehot = (slot_bins[:, None] == jnp.arange(NBINS, dtype=jnp.int32)[None, :]).astype(jnp.float32)
    return jnp.dot(energy[None, :], onehot, precision=lax.Precision.HIGHEST)[0]


def routed_device(
    residual_in,
    norm_gain,
    q_nope,
    q_rope,
    latent,
    k_rope,
    doc_ids,
    uv_weight,
    out_weight,
    expert_ids,
    gate_levels,
    bin_ids,
    gate_weight,
    up_weight,
    down_weight,
):
    exp_devices = lax.axis_size("exp")
    block_len, head_count, lat_width = q_nope.shape
    rope_width = k_rope.shape[1]
    query_first = lax.axis_index("ctx") * block_len
    query_pos = query_first + jnp.arange(block_len, dtype=jnp.int32)
    query_rope = q_rope.reshape(block_len, head_count, rope_width)
    token_count = residual_in.shape[0]
    keys_local = (latent, k_rope, doc_ids)
    initial = (
        jnp.full((head_count, block_len), masked_score, jnp.float32),
        jnp.zeros((head_count, block_len), jnp.float32),
        jnp.zeros((head_count, block_len, lat_width), jnp.float32),
    )
    running = attend_piece(
        initial,
        (
            lax.all_gather(keys_local[0], "ctx", axis=0, tiled=True),
            lax.all_gather(keys_local[1], "ctx", axis=0, tiled=True),
            lax.all_gather(keys_local[2], "ctx", axis=0, tiled=True),
        ),
        q_nope,
        query_rope,
        query_pos,
        doc_ids,
    )
    head_rows = fold_projection(running, uv_weight, out_weight)
    attended = lax.psum_scatter(
        head_rows(jnp.int32(0), token_count * lax.axis_size("exp")),
        "exp",
        scatter_dimension=0,
        tiled=True,
    )
    stream_state = residual_in.astype(jnp.float32) + attended
    normed = (
        stream_state
        * lax.rsqrt(jnp.mean(stream_state * stream_state, axis=1, keepdims=True) + norm_eps)
        * norm_gain
    ).astype(jnp.bfloat16)
    top_count = expert_ids.shape[1]
    capacity = min(token_count, max(2, 2 * token_count * top_count // exp_devices))
    slot_total = exp_devices * capacity
    destination = route_slots(expert_ids, exp_devices, capacity)
    slot_match = destination[:, :, None] == jnp.arange(slot_total, dtype=jnp.int32)[None, None, :]
    selector = jnp.sum(slot_match.astype(jnp.int32), axis=1).astype(jnp.bfloat16)
    outgoing = jnp.einsum("ts,td->sd", selector, normed, preferred_element_type=jnp.float32).astype(
        jnp.bfloat16
    )
    outgoing = outgoing.reshape(exp_devices, capacity, outgoing.shape[1])
    slot_bins = jnp.sum(jnp.where(slot_match, bin_ids[:, :, None], 0), axis=(0, 1)).reshape(
        exp_devices, capacity
    )
    incoming, incoming_bins = (
        lax.all_to_all(outgoing, "exp", split_axis=0, concat_axis=1, tiled=True),
        lax.all_to_all(slot_bins, "exp", split_axis=0, concat_axis=1, tiled=True),
    )
    all_rows, all_bins = (
        lax.all_gather(incoming, "ctx", axis=1, tiled=True),
        lax.all_gather(incoming_bins, "ctx", axis=1, tiled=True),
    )
    hidden, energy = expert_hidden(all_rows[0], gate_weight[0], up_weight[0])
    bin_part = bin_energy(energy, all_bins[0])
    down_local = down_weight[0]
    expert_out = lax.psum_scatter(
        jnp.dot(hidden, down_local, preferred_element_type=jnp.float32).astype(jnp.bfloat16),
        "ctx",
        scatter_dimension=0,
        tiled=True,
    )
    histogram = lax.psum_scatter(bin_part[None, :], "ctx", scatter_dimension=1, tiled=True)
    returned = lax.all_to_all(expert_out[None], "exp", split_axis=1, concat_axis=0, tiled=True)
    levels = gate_levels.astype(jnp.float32)
    route_weights = levels / jnp.sum(levels, axis=1, keepdims=True)
    combiner = jnp.sum(jnp.where(slot_match, route_weights[:, :, None], 0.0), axis=1)
    mixture = jnp.dot(
        combiner,
        returned.reshape(slot_total, returned.shape[2]).astype(jnp.float32),
        precision=lax.Precision.HIGHEST,
    )
    layer_out = (stream_state + mixture).astype(jnp.bfloat16)
    return (layer_out, histogram)


def turn(place):
    return place ^ (place // 2)


def positions(exp_devices):
    ctx_here, here = lax.axis_index("ctx"), lax.axis_index("exp")
    rows = exp_devices // 2
    z_at, x_at = here // 2, here % 2
    order = [
        turn((turn(z_at) - step + rows) % rows) * 2 + (x_at if side == 0 else 1 - x_at)
        for step in range(rows)
        for side in range(2)
    ]
    return jnp.stack([x_at, ctx_here, here, *order]).astype(jnp.int32)


def swap_exp(value, bit=1):
    return lax.ppermute(value, "exp", [(e, e ^ bit) for e in range(lax.axis_size("exp"))])


def ring_z(value):
    rows = lax.axis_size("exp") // 2
    steps = [(turn(at), turn((at + 1) % rows)) for at in range(rows)]
    return lax.ppermute(value, "exp", [(2 * a + x, 2 * b + x) for a, b in steps for x in range(2)])


def swap_ctx(value, bit):
    return lax.ppermute(value, "ctx", [(c, c ^ bit) for c in range(lax.axis_size("ctx"))])


def after(value, earlier):
    return lax.optimization_barrier((value, earlier))[0]


def one_step(work, *inputs):
    taken = lax.axis_index("ctx") // lax.axis_size("ctx") == 0

    def blank(*arrays):
        return jax.tree.map(lambda leaf: jnp.zeros(leaf.shape, leaf.dtype), jax.eval_shape(work, *arrays))

    return lax.cond(taken, work, blank, *inputs)


def reduce_exp(own, own_across, first, first_a, first_b, second, second_across, third, third_across):
    def summed(*terms):
        return sum(term.astype(jnp.float32) for term in terms).astype(jnp.bfloat16)

    got_a, moved_b = swap_exp(first_a), ring_z(first_b)
    total = summed(first, jnp.concatenate([got_a, jnp.zeros_like(first_b)], axis=1))
    second_across = summed(second_across, jnp.concatenate([jnp.zeros_like(first_a), moved_b], axis=1))
    got_second = swap_exp(second_across)
    got_third = swap_exp(after(third_across, second_across))
    total = summed(ring_z(total), second, got_second)
    got_own = swap_exp(after(own_across, got_second))
    total = summed(ring_z(total), third, got_third)
    return ring_z(total), own, got_own


def split_outs(count, rows, width):
    half = width // 2
    places = []
    for at in range(count):
        for columns in ((0, half), (half, width)) if at == 3 else ((0, width),):
            places.append((at * rows, columns))
    return places


def norm_kernel(moved, mine, across, residual, gain, table, stream, out):
    width = stream.shape[1]
    state = residual[...].astype(jnp.float32) + (
        moved[...].astype(jnp.float32) + (mine[...].astype(jnp.float32) + across[...].astype(jnp.float32))
    )
    stream[...] = state
    mean = jnp.sum(state * state, axis=1, keepdims=True) * (1.0 / width)
    out[:, :width] = (state * lax.rsqrt(mean + norm_eps) * gain[...]).astype(out.dtype)
    out[:, width:] = table[...]


def norm_rows(moved, mine, across, residual, gain, table):
    rows, width = residual.shape
    whole = pl.BlockSpec(memory_space=pltpu.VMEM)
    return pl.pallas_call(
        norm_kernel,
        in_specs=[whole] * 6,
        out_specs=[whole] * 2,
        out_shape=[
            jax.ShapeDtypeStruct((rows, width), jnp.float32),
            pltpu.VMEM((rows, width + table.shape[1]), jnp.bfloat16),
        ],
        compiler_params=pltpu.CompilerParams(vmem_limit_bytes=VMEM_BYTES),
        cost_estimate=pl.CostEstimate(flops=8 * rows * width, bytes_accessed=14 * rows * width, transcendentals=rows),
        name="norm",
    )(moved, mine, across, residual, gain[None, :], table)


def gather_exp(block):
    found = [block, swap_exp(block)]
    for step in range(2, lax.axis_size("exp") // 2):
        block = ring_z(after(block, found[-3]) if len(found) > 2 else block)
        found += [block, swap_exp(block)]
    return found


def pack_kernel(here, latent, k_rope, docs, own, sent):
    keys, lat_width, rope_width = latent.shape[0], latent.shape[1], k_rope.shape[1]
    own[:, :lat_width] = latent[...]
    row = lax.broadcasted_iota(jnp.int32, (128, 128), 0)
    lane = lax.broadcasted_iota(jnp.int32, (128, 128), 1)
    for at in range(keys // 128):
        wide = jnp.broadcast_to(docs[at : at + 1, :], (128, 128))
        column = jnp.sum(jnp.where(row == lane, wide, 0), axis=1, keepdims=True)
        ropes = jnp.concatenate(
            [k_rope[at * 128 : (at + 1) * 128, :].astype(jnp.float32), jnp.zeros((128, 128 - rope_width), jnp.float32)],
            axis=1,
        )
        own[at * 128 : (at + 1) * 128, lat_width:] = jnp.where(
            lane == rope_width, column.astype(jnp.float32), ropes
        ).astype(jnp.bfloat16)
    half = sent.shape[0]
    sent[...] = own[pl.ds(pl.multiple_of(here[0] * half, half), half), :]


def pack_keys(here, latent, k_rope, doc_ids):
    keys, width = latent.shape[0], latent.shape[1] + 128
    whole = pl.BlockSpec(memory_space=pltpu.VMEM)
    return pl.pallas_call(
        pack_kernel,
        in_specs=[pl.BlockSpec(memory_space=pltpu.SMEM)] + [whole] * 3,
        out_specs=[whole] * 2,
        out_shape=[
            jax.ShapeDtypeStruct((keys, width), jnp.bfloat16),
            jax.ShapeDtypeStruct((keys // 2, width), jnp.bfloat16),
        ],
        cost_estimate=pl.CostEstimate(flops=0, bytes_accessed=6 * keys * width, transcendentals=0),
        compiler_params=pltpu.CompilerParams(vmem_limit_bytes=8 * 1024 * 1024),
        name="pack",
    )(here, latent, k_rope, doc_ids.reshape(keys // 128, 128))


def join_kernel(left, right, *refs):
    outs, sems = refs[:-1], refs[-1]
    width, first, copies = left.shape[1], 0, []
    for out in outs:
        for side, weight in enumerate((left, right)):
            copies.append(
                pltpu.make_async_copy(
                    weight.at[pl.ds(first, out.shape[0])],
                    out.at[:, pl.ds(side * width, width)],
                    sems.at[len(copies)],
                )
            )
            copies[-1].start()
        first += out.shape[0]
    for copy in copies:
        copy.wait()


def join_weights(left, right, ends):
    width = left.shape[1]
    counts = [end - first for first, end in zip((0, *ends[:-1]), ends)]
    anywhere = pl.BlockSpec(memory_space=pl.ANY)
    return pl.pallas_call(
        join_kernel,
        in_specs=[anywhere] * 2,
        out_specs=[anywhere] * len(ends),
        out_shape=[jax.ShapeDtypeStruct((count, 2 * width), left.dtype) for count in counts],
        scratch_shapes=[pltpu.SemaphoreType.DMA((2 * len(ends),))],
        compiler_params=pltpu.CompilerParams(vmem_limit_bytes=1024 * 1024),
        cost_estimate=pl.CostEstimate(flops=0, bytes_accessed=8 * left.size, transcendentals=0),
        name="join",
    )(left, right)


def route_kernel(ids, levels, bins, out, *, experts):
    lane = lax.broadcasted_iota(jnp.int32, out.shape, 1)
    table = jnp.zeros(out.shape, jnp.int32)
    for at, what in enumerate((levels[...], bins[...] // 128, bins[...] % 128)):
        for expert in range(experts):
            column = jnp.sum(jnp.where(ids[...] == expert, what, 0), axis=1, keepdims=True)
            table = jnp.where(lane == at * experts + expert, column, table)
    out[...] = table.astype(jnp.float32).astype(out.dtype)


def route_table(expert_ids, gate_levels, bin_ids, experts):
    whole = pl.BlockSpec(memory_space=pltpu.VMEM)
    return pl.pallas_call(
        functools.partial(route_kernel, experts=experts),
        in_specs=[whole] * 3,
        out_specs=whole,
        out_shape=jax.ShapeDtypeStruct((expert_ids.shape[0], 128), jnp.bfloat16),
        compiler_params=pltpu.CompilerParams(vmem_limit_bytes=4 * 1024 * 1024),
        name="route",
    )(expert_ids, gate_levels, bin_ids)


def attend_kernel(scalars, q_nope, q_rope, *refs, heads, rope_width):
    own, near_even, near_a, near_b, far_a, far_b, uv, out, keys, more, sems = refs
    tile, block_len, half = out.shape[0], own.shape[0], far_a.shape[0]
    lat_width = uv.shape[1]
    first = pl.program_id(0) * tile
    places = [
        (own, keys, 0),
        (near_even, keys, block_len),
        (near_a, more, 0),
        (near_b, more, half),
        (far_a, keys, 2 * block_len),
        (far_b, keys, 2 * block_len + half),
    ]
    copies = [
        pltpu.make_async_copy(piece, into.at[pl.ds(at, piece.shape[0])], sems.at[number])
        for number, (piece, into, at) in enumerate(places)
    ]

    @pl.when(pl.program_id(0) == 0)
    def _():
        for copy in copies:
            copy.start()
        for copy in copies:
            copy.wait()
        keys[block_len : 2 * block_len, :] = keys[block_len : 2 * block_len, :] + more[...]

    doc_at = lat_width + rope_width
    pick = (lax.broadcasted_iota(jnp.int32, (8, 128), 1) == rope_width).astype(jnp.bfloat16)
    query_docs = keys[pl.ds(pl.multiple_of(first, tile), tile), lat_width:][:, rope_width : rope_width + 1].astype(jnp.float32)
    over = (((1,), (1,)), ((), ()))
    docs = lax.dot_general(pick, keys[:, lat_width:], over, preferred_element_type=jnp.float32)[0:1, :]
    key_at = lax.broadcasted_iota(jnp.int32, (1, keys.shape[0]), 1)
    docs = jnp.where(key_at < (scalars[1] + 1) * block_len, docs, -1.0)
    spare = jnp.zeros((tile, keys.shape[1] - doc_at), jnp.bfloat16)
    query = jnp.concatenate(
        [
            jnp.concatenate(
                [
                    q_nope[:, head * lat_width : (head + 1) * lat_width],
                    q_rope[:, head * rope_width : (head + 1) * rope_width],
                    spare,
                ],
                axis=1,
            )
            for head in range(heads)
        ],
        axis=0,
    )
    scores, top = [], None
    for block in range(keys.shape[0] // block_len):
        at = slice(block * block_len, (block + 1) * block_len)
        same = docs[:, at] == query_docs
        if block == 0:
            within = lax.broadcasted_iota(jnp.int32, (tile, block_len), 1)
            same = same & (within <= lax.broadcasted_iota(jnp.int32, (tile, block_len), 0) + first)
        raw = lax.dot_general(query, keys[at, :], over, preferred_element_type=jnp.float32)
        same = jnp.concatenate([same] * heads, axis=0)
        scores.append(jnp.where(same, raw * (softmax_scale * LOG2_E), masked_score))
        most = jnp.max(scores[-1], axis=1, keepdims=True)
        top = most if top is None else jnp.maximum(top, most)
    total, accum = 0.0, 0.0
    for block, score in enumerate(scores):
        probs = jnp.exp2(score - top)
        total = total + jnp.sum(probs, axis=1, keepdims=True)
        accum = accum + jnp.dot(
            probs.astype(jnp.bfloat16),
            keys[block * block_len : (block + 1) * block_len, :lat_width],
            preferred_element_type=jnp.float32,
        )
    context = (accum / total).astype(jnp.bfloat16)
    width = uv.shape[2]
    for head in range(heads):
        value = jnp.dot(context[head * tile : (head + 1) * tile], uv[head], preferred_element_type=jnp.float32)
        out[:, head * width : (head + 1) * width] = value.astype(out.dtype)


def attend(here, q_nope, q_rope, pieces, uv_weight, rope_width):
    queries, (block_len, width) = q_nope.shape[0], pieces[0].shape
    heads, lat_width, value_width = uv_weight.shape
    tile = 256
    return pl.pallas_call(
        functools.partial(attend_kernel, heads=heads, rope_width=rope_width),
        grid_spec=pltpu.PrefetchScalarGridSpec(
            num_scalar_prefetch=1,
            grid=(queries // tile,),
            in_specs=[
                pl.BlockSpec((tile, heads * lat_width), lambda i, s: (i, 0)),
                pl.BlockSpec((tile, heads * rope_width), lambda i, s: (i, 0)),
                *[pl.BlockSpec(memory_space=pltpu.HBM) for _ in pieces],
                pl.BlockSpec(uv_weight.shape, lambda i, s: (0, 0, 0)),
            ],
            out_specs=pl.BlockSpec((tile, heads * value_width), lambda i, s: (i, 0)),
            scratch_shapes=[
                pltpu.VMEM((3 * block_len, width), jnp.bfloat16),
                pltpu.VMEM((block_len, width), jnp.bfloat16),
                pltpu.SemaphoreType.DMA((len(pieces),)),
            ],
        ),
        out_shape=jax.ShapeDtypeStruct((queries, heads * value_width), jnp.bfloat16),
        compiler_params=pltpu.CompilerParams(vmem_limit_bytes=24 * 1024 * 1024),
        cost_estimate=pl.CostEstimate(
            flops=6 * heads * queries * block_len * (width + lat_width),
            bytes_accessed=2 * (q_nope.size + 4 * block_len * width + uv_weight.size),
            transcendentals=3 * heads * queries * block_len,
        ),
        name="attend",
    )(here, q_nope, q_rope, *pieces, uv_weight)


def project_kernel(order, values, weight, *outs, places):
    rows = outs[0].shape[0]
    picked = jnp.concatenate(
        [values[pl.ds(pl.multiple_of(order[3 + at] * rows, rows), rows), :] for at in range(values.shape[0] // rows)], axis=0
    )
    result = jnp.dot(picked, weight[...], preferred_element_type=jnp.float32).astype(outs[0].dtype)
    tile, step = weight.shape[1], pl.program_id(0)
    for (first, (start, end)), out in zip(places, outs):

        @pl.when((step >= start // tile) & (step < end // tile))
        def _(first=first, out=out):
            out[...] = result[first : first + rows]


def project_blocks(here, values, weight, count):
    rows, inner = values.shape
    width = weight.shape[1]
    block, tile = rows // count, 896
    places = split_outs(count, block, width)

    def out_spec(columns):
        first, last = columns[0] // tile, columns[1] // tile - 1
        return pl.BlockSpec((block, tile), lambda n, s: (0, jnp.clip(n, first, last) - first))

    return pl.pallas_call(
        functools.partial(project_kernel, places=places),
        grid_spec=pltpu.PrefetchScalarGridSpec(
            num_scalar_prefetch=1,
            grid=(width // tile,),
            in_specs=[
                pl.BlockSpec((rows, inner), lambda n, s: (0, 0)),
                pl.BlockSpec((inner, tile), lambda n, s: (0, n)),
            ],
            out_specs=[out_spec(columns) for _, columns in places],
        ),
        out_shape=[pltpu.VMEM((block, end - start), jnp.bfloat16) for _, (start, end) in places],
        compiler_params=pltpu.CompilerParams(vmem_limit_bytes=32 * 1024 * 1024),
        cost_estimate=pl.CostEstimate(
            flops=2 * rows * inner * width, bytes_accessed=2 * (inner + rows) * width, transcendentals=0
        ),
        name="project",
    )(here, values, weight)


def hidden_kernel(here, *refs, blocks, counts, experts):
    rows, rest = refs[:blocks], refs[blocks:]
    copies = []
    if counts:
        pieces, (hidden, energy_bins, scale, held, row_data, sems) = rest[: sum(counts)], rest[sum(counts) :]
        at = 0
        for part, count in enumerate(counts):
            copies.append([])
            first = 0
            for piece in pieces[at : at + count]:
                into = held.at[part, pl.ds(first, piece.shape[0])]
                copies[-1].append(pltpu.make_async_copy(piece, into, sems.at[at]))
                copies[-1][-1].start()
                first += piece.shape[0]
                at += 1
    else:
        held, hidden, energy_bins, scale, row_data = rest
    parts, inner, units, each = held.shape[0], held.shape[1], held.shape[2] // 2, rows[0].shape[0]
    for at, row in enumerate(rows):
        row_data[at * each : (at + 1) * each, :] = row[:, :inner]
    table = jnp.concatenate([row[:, inner:] for row in rows], axis=0).astype(jnp.float32)
    lane = lax.broadcasted_iota(jnp.int32, table.shape, 1)

    def column(first):
        return jnp.sum(jnp.where(lane == first + here[2], table, 0.0), axis=1, keepdims=True)

    levels = jnp.sum(jnp.where(lane < experts, table, 0.0), axis=1, keepdims=True)
    scale[...] = column(0) / levels
    squares = 0.0
    for part in range(parts):
        for copy in copies[part] if counts else ():
            copy.wait()
        both = jnp.dot(row_data[...], held[part], preferred_element_type=jnp.float32)
        gate_part, up_part = both[:, :units], both[:, units:]
        activation = gate_part / (1.0 + jnp.exp(-gate_part)) * up_part
        hidden[:, part * units : (part + 1) * units] = activation.astype(hidden.dtype)
        squares = squares + jnp.sum(activation * activation, axis=1, keepdims=True)
    place = lane.astype(jnp.float32)
    high = jnp.where(place == column(experts), squares * (1.0 / HID), 0.0)
    low = jnp.where(place == column(2 * experts), 1.0, 0.0)
    counted = jnp.dot(high.T, low, precision=lax.Precision.HIGHEST, preferred_element_type=jnp.float32)
    energy_bins[...] = counted[: energy_bins.shape[0], :]


def hidden_rows(here, rows, weights, experts):
    first = isinstance(weights, list)
    whole = pl.BlockSpec(memory_space=pltpu.VMEM)
    if first:
        counts = tuple(len(pieces) for pieces in weights)
        parts, both = len(weights), weights[0][0].shape[1]
        inner = sum(piece.shape[0] for piece in weights[0])
        operands = [piece for pieces in weights for piece in pieces]
    else:
        counts, (parts, inner, both), operands = None, weights.shape, [weights]
    count = len(rows) * rows[0].shape[0]
    kept = [pltpu.VMEM((parts, inner, both), jnp.bfloat16)] if first else []
    return pl.pallas_call(
        functools.partial(hidden_kernel, blocks=len(rows), counts=counts, experts=experts),
        in_specs=[pl.BlockSpec(memory_space=pltpu.SMEM)]
        + [whole] * len(rows)
        + [pl.BlockSpec(memory_space=pltpu.HBM) if first else whole] * len(operands),
        out_specs=[whole] * (3 + len(kept)),
        out_shape=[
            jax.ShapeDtypeStruct((count, parts * both // 2), jnp.bfloat16),
            jax.ShapeDtypeStruct((NBINS // 128, 128), jnp.float32),
            jax.ShapeDtypeStruct((count, 1), jnp.float32),
            *kept,
        ],
        scratch_shapes=[pltpu.VMEM((count, inner), jnp.bfloat16)]
        + ([pltpu.SemaphoreType.DMA((len(operands),))] if first else []),
        compiler_params=pltpu.CompilerParams(vmem_limit_bytes=VMEM_BYTES),
        cost_estimate=pl.CostEstimate(
            flops=2 * count * inner * parts * both,
            bytes_accessed=2 * inner * (count + parts * both),
            transcendentals=count * parts * both // 2,
        ),
        name="hidden",
    )(here, *rows, *operands)


def down_kernel(*refs, pieces, parts, tile, places):
    hidden, scales, weights = refs[:pieces], refs[pieces : 2 * pieces], refs[2 * pieces : 2 * pieces + parts]
    outs = refs[2 * pieces + parts :]
    rows, units = outs[0].shape[0], weights[0].shape[0]
    each = hidden[0].shape[0]
    for piece in range(pieces):
        for at in range(weights[0].shape[1] // tile):
            columns = slice(at * tile, (at + 1) * tile)
            total = 0.0
            for part, weight in enumerate(weights):
                total = total + jnp.dot(
                    hidden[piece][:, part * units : (part + 1) * units],
                    weight[:, columns],
                    preferred_element_type=jnp.float32,
                )
            total = (total * scales[piece][...]).astype(outs[0].dtype)
            for (first, (start, end)), out in zip(places, outs):
                if piece * each <= first < (piece + 1) * each and start <= at * tile < end:
                    out[:, at * tile - start : (at + 1) * tile - start] = total[first - piece * each :][:rows]


def down_blocks(hidden, scales, weights, count):
    pieces, parts, tile = len(hidden), len(weights), 896
    each, inner = hidden[0].shape
    units, width = weights[0].shape
    whole = pl.BlockSpec(memory_space=pltpu.VMEM)
    places = split_outs(count, pieces * each // count, width)
    return pl.pallas_call(
        functools.partial(down_kernel, pieces=pieces, parts=parts, tile=tile, places=places),
        in_specs=[whole] * (2 * pieces + parts),
        out_specs=[whole] * len(places),
        out_shape=[pltpu.VMEM((pieces * each // count, end - start), jnp.bfloat16) for _, (start, end) in places],
        compiler_params=pltpu.CompilerParams(vmem_limit_bytes=VMEM_BYTES),
        cost_estimate=pl.CostEstimate(
            flops=2 * pieces * each * inner * width,
            bytes_accessed=2 * width * (inner + pieces * each),
            transcendentals=0,
        ),
        name="down",
    )(*hidden, *scales, *weights)


def spread_bins(counts):
    counts = counts.reshape(2, 2, NBINS // 4)
    ctx_here = lax.axis_index("ctx")
    for at, bit in ((ctx_here // 2, 2), (ctx_here % 2, 1)):
        counts = lax.dynamic_index_in_dim(counts, at, 0, keepdims=False) + swap_ctx(
            lax.dynamic_index_in_dim(counts, 1 - at, 0, keepdims=False), bit
        )
    return counts[None, :]


def dense_device(
    residual_in,
    norm_gain,
    q_nope,
    q_rope,
    latent,
    k_rope,
    doc_ids,
    uv_weight,
    out_weight,
    expert_ids,
    gate_levels,
    bin_ids,
    gate_weight,
    up_weight,
    down_weight,
):
    exp_devices, ctx_devices = lax.axis_size("exp"), lax.axis_size("ctx")
    block_len, head_count, lat_width = q_nope.shape
    rope_width = k_rope.shape[1]
    here = positions(exp_devices)

    own, sent = pack_keys(here, latent, k_rope, doc_ids)
    far = lax.ppermute(sent, "ctx", [(c, c + 2) for c in range(ctx_devices - 2)])
    flat_q = q_nope.reshape(block_len, head_count * lat_width)
    w_gate, w_up, w_down = gate_weight[0], up_weight[0], down_weight[0]
    own_both = join_weights(w_gate, w_up, (FIRST_ROWS, w_gate.shape[0]))
    far = after(far, own_both)
    both_a = swap_ctx(after(own_both[0], far), 2)

    def attend_and_project(here, flat_q, q_rope, own, far, uv_weight, out_weight, expert_ids, gate_levels, bin_ids):
        far_across = swap_exp(far)
        near = lax.ppermute(own, "ctx", [(c, c + 1) for c in range(0, ctx_devices, 2)])
        table = route_table(expert_ids, gate_levels, bin_ids, exp_devices)
        early = after(far, (flat_q, table))
        key_pieces = [own, near, *[lax.ppermute(piece, "ctx", [(3, 2)]) for piece in (early, far_across)], far, far_across]
        values = attend(here, flat_q, q_rope, key_pieces, uv_weight, rope_width)
        return project_blocks(here, values, out_weight, exp_devices), table

    there_both = [swap_ctx(piece, 1) for piece in own_both]
    inputs = here, flat_q, q_rope, own, far, uv_weight, out_weight, expert_ids, gate_levels, bin_ids
    partial, table = after(one_step(attend_and_project, *inputs), both_a)
    both_c = swap_ctx(after(own_both[1], (partial[0], both_a)), 2)

    def sum_and_norm(partial, *rest):
        return norm_rows(*reduce_exp(*partial), *rest)

    stream_state, block = one_step(sum_and_norm, partial, residual_in, norm_gain, table)
    swapped = swap_ctx(both_a, 1)
    across, back = after(one_step(lambda value: (swap_exp(value), ring_z(value)), block), (both_c, swapped))
    far_down = swap_ctx(after(w_down, (both_c, back)), 2)

    def gather_and_hide(block, across, back, here, own_both, there_both, far_both, swapped):
        weights = [own_both, there_both, far_both, [swapped, swap_ctx(far_both[-1], 1)]]
        found = [block, across, *gather_exp(back)]
        half = len(found) // 2
        *first, held = hidden_rows(here, found[:half], weights, exp_devices)
        last = hidden_rows(here, found[half:], held, exp_devices)
        return [*zip(first, last)]

    hidden, bins, scales = after(
        one_step(gather_and_hide, block, across, back, here, own_both, there_both, [both_a, both_c], swapped), far_down
    )
    downs = [w_down, swap_ctx(w_down, 1), far_down, swap_ctx(after(far_down, hidden), 1)]
    expert_out = down_blocks(hidden, scales, downs, exp_devices)
    mixture = reduce_exp(*expert_out)
    layer_out = (stream_state + sum(term.astype(jnp.float32) for term in mixture)).astype(jnp.bfloat16)
    histogram = spread_bins(after(bins[0] + bins[1], expert_out[0]))
    return (layer_out, histogram)


def solution(mesh):
    sizes = mesh.shape

    def on_device(*arrays):
        named_experts = arrays[9].shape[1]
        dense = sizes["exp"] == 8 and sizes["ctx"] == 4 and named_experts == sizes["exp"]
        return (dense_device if dense else routed_device)(*arrays)

    return jax.shard_map(
        on_device,
        mesh=mesh,
        in_specs=(
            P(("ctx", "exp"), None),
            P(),
            P("ctx", "exp", None),
            P("ctx", "exp"),
            P("ctx", None),
            P("ctx", None),
            P("ctx"),
            P("exp", None, None),
            P("exp", None),
            P(("ctx", "exp"), None),
            P(("ctx", "exp"), None),
            P(("ctx", "exp"), None),
            P("exp", None, "ctx"),
            P("exp", None, "ctx"),
            P("exp", "ctx", None),
        ),
        out_specs=(P(("ctx", "exp"), None), P("exp", "ctx")),
        check_vma=False,
    )
```

```python
import functools
import math

import jax
import jax.numpy as jnp
from jax import lax
from jax.experimental import pallas as pl
from jax.experimental.pallas import tpu as pltpu
from jax.sharding import PartitionSpec as P

HID = 1024
NBINS = 2048


softmax_scale = 192.0 ** (-0.5)
norm_eps = 1e-06
masked_score = -1e30
LOG2_E = math.log2(math.e)
FIRST_ROWS = 960
VMEM_BYTES = 14 * 1024 * 1024


def route_slots(expert_ids, experts, capacity):
    flat_ids = expert_ids.reshape(-1)
    onehot = (flat_ids[:, None] == jnp.arange(experts, dtype=jnp.int32)[None, :]).astype(jnp.int32)
    before = jnp.cumsum(onehot, axis=0) - onehot
    slot_rank = jnp.sum(before * onehot, axis=1)
    return (flat_ids * capacity + slot_rank).reshape(expert_ids.shape)


def key_scores(query_nope, query_rope, lat_rows, rope_rows):
    scores = jnp.einsum("qhl,kl->hqk", query_nope, lat_rows, preferred_element_type=jnp.float32)
    scores = scores + jnp.einsum(
        "qhr,kr->hqk", query_rope, rope_rows, preferred_element_type=jnp.float32
    )
    return scores * softmax_scale


def attend_piece(running, key_piece, query_nope, query_rope, query_pos, query_docs):
    lat_rows, rope_rows, doc_rows = key_piece
    key_pos = jnp.arange(lat_rows.shape[0], dtype=jnp.int32)
    allowed = (key_pos[None, :] <= query_pos[:, None]) & (doc_rows[None, :] == query_docs[:, None])
    scores = jnp.where(
        allowed[None], key_scores(query_nope, query_rope, lat_rows, rope_rows), masked_score
    )
    run_max, run_sum, accum = running
    new_max = jnp.maximum(run_max, jnp.max(scores, axis=2))
    probs = jnp.where(allowed[None], jnp.exp(scores - new_max[:, :, None]), 0.0)
    run_sum = jnp.sum(probs, axis=2)
    accum = jnp.einsum(
        "hqk,kl->hql", probs.astype(jnp.bfloat16), lat_rows, preferred_element_type=jnp.float32
    )
    return (new_max, run_sum, accum)


def project_values(context, uv_weight):
    values = jnp.einsum(
        "hql,hlv->qhv", context, uv_weight, preferred_element_type=jnp.float32
    ).astype(jnp.bfloat16)
    return values.reshape(values.shape[0], values.shape[1] * values.shape[2])


def fold_projection(running, uv_weight, out_weight):
    context = (running[2] / running[1][:, :, None]).astype(jnp.bfloat16)
    values = project_values(context, uv_weight)

    def head_rows(row_start, row_count):
        return jnp.dot(values, out_weight, preferred_element_type=jnp.float32)

    return head_rows


def expert_hidden(row_data, w_gate, w_up):
    gate_part = jnp.dot(row_data, w_gate, preferred_element_type=jnp.float32)
    up_part = jnp.dot(row_data, w_up, preferred_element_type=jnp.float32)
    activation = jax.nn.silu(gate_part) * up_part
    return (activation.astype(jnp.bfloat16), jnp.sum(activation * activation, axis=1) / HID)


def bin_energy(energy, slot_bins):
    onehot = (slot_bins[:, None] == jnp.arange(NBINS, dtype=jnp.int32)[None, :]).astype(jnp.float32)
    return jnp.dot(energy[None, :], onehot, precision=lax.Precision.HIGHEST)[0]


def routed_device(
    residual_in,
    norm_gain,
    q_nope,
    q_rope,
    latent,
    k_rope,
    doc_ids,
    uv_weight,
    out_weight,
    expert_ids,
    gate_levels,
    bin_ids,
    gate_weight,
    up_weight,
    down_weight,
):
    exp_devices = lax.axis_size("exp")
    block_len, head_count, lat_width = q_nope.shape
    rope_width = k_rope.shape[1]
    query_first = lax.axis_index("ctx") * block_len
    query_pos = query_first + jnp.arange(block_len, dtype=jnp.int32)
    query_rope = q_rope.reshape(block_len, head_count, rope_width)
    token_count = residual_in.shape[0]
    keys_local = (latent, k_rope, doc_ids)
    initial = (
        jnp.full((head_count, block_len), masked_score, jnp.float32),
        jnp.zeros((head_count, block_len), jnp.float32),
        jnp.zeros((head_count, block_len, lat_width), jnp.float32),
    )
    running = attend_piece(
        initial,
        (
            lax.all_gather(keys_local[0], "ctx", axis=0, tiled=True),
            lax.all_gather(keys_local[1], "ctx", axis=0, tiled=True),
            lax.all_gather(keys_local[2], "ctx", axis=0, tiled=True),
        ),
        q_nope,
        query_rope,
        query_pos,
        doc_ids,
    )
    head_rows = fold_projection(running, uv_weight, out_weight)
    attended = lax.psum_scatter(
        head_rows(jnp.int32(0), token_count * lax.axis_size("exp")),
        "exp",
        scatter_dimension=0,
        tiled=True,
    )
    stream_state = residual_in.astype(jnp.float32) + attended
    normed = (
        stream_state
        * lax.rsqrt(jnp.mean(stream_state * stream_state, axis=1, keepdims=True) + norm_eps)
        * norm_gain
    ).astype(jnp.bfloat16)
    top_count = expert_ids.shape[1]
    capacity = min(token_count, max(2, 2 * token_count * top_count // exp_devices))
    slot_total = exp_devices * capacity
    destination = route_slots(expert_ids, exp_devices, capacity)
    slot_match = destination[:, :, None] == jnp.arange(slot_total, dtype=jnp.int32)[None, None, :]
    selector = jnp.sum(slot_match.astype(jnp.int32), axis=1).astype(jnp.bfloat16)
    outgoing = jnp.einsum("ts,td->sd", selector, normed, preferred_element_type=jnp.float32).astype(
        jnp.bfloat16
    )
    outgoing = outgoing.reshape(exp_devices, capacity, outgoing.shape[1])
    slot_bins = jnp.sum(jnp.where(slot_match, bin_ids[:, :, None], 0), axis=(0, 1)).reshape(
        exp_devices, capacity
    )
    incoming, incoming_bins = (
        lax.all_to_all(outgoing, "exp", split_axis=0, concat_axis=1, tiled=True),
        lax.all_to_all(slot_bins, "exp", split_axis=0, concat_axis=1, tiled=True),
    )
    all_rows, all_bins = (
        lax.all_gather(incoming, "ctx", axis=1, tiled=True),
        lax.all_gather(incoming_bins, "ctx", axis=1, tiled=True),
    )
    hidden, energy = expert_hidden(all_rows[0], gate_weight[0], up_weight[0])
    bin_part = bin_energy(energy, all_bins[0])
    down_local = down_weight[0]
    expert_out = lax.psum_scatter(
        jnp.dot(hidden, down_local, preferred_element_type=jnp.float32).astype(jnp.bfloat16),
        "ctx",
        scatter_dimension=0,
        tiled=True,
    )
    histogram = lax.psum_scatter(bin_part[None, :], "ctx", scatter_dimension=1, tiled=True)
    returned = lax.all_to_all(expert_out[None], "exp", split_axis=1, concat_axis=0, tiled=True)
    levels = gate_levels.astype(jnp.float32)
    route_weights = levels / jnp.sum(levels, axis=1, keepdims=True)
    combiner = jnp.sum(jnp.where(slot_match, route_weights[:, :, None], 0.0), axis=1)
    mixture = jnp.dot(
        combiner,
        returned.reshape(slot_total, returned.shape[2]).astype(jnp.float32),
        precision=lax.Precision.HIGHEST,
    )
    layer_out = (stream_state + mixture).astype(jnp.bfloat16)
    return (layer_out, histogram)


def turn(place):
    return place ^ (place // 2)


def positions(exp_devices):
    ctx_here, here = lax.axis_index("ctx"), lax.axis_index("exp")
    rows = exp_devices // 2
    z_at, x_at = here // 2, here % 2
    order = [
        turn((turn(z_at) - step + rows) % rows) * 2 + (x_at if side == 0 else 1 - x_at)
        for step in range(rows)
        for side in range(2)
    ]
    return jnp.stack([x_at, ctx_here, here, *order]).astype(jnp.int32)


def swap_exp(value, bit=1):
    return lax.ppermute(value, "exp", [(e, e ^ bit) for e in range(lax.axis_size("exp"))])


def ring_z(value):
    rows = lax.axis_size("exp") // 2
    steps = [(turn(at), turn((at + 1) % rows)) for at in range(rows)]
    return lax.ppermute(value, "exp", [(2 * a + x, 2 * b + x) for a, b in steps for x in range(2)])


def swap_ctx(value, bit):
    return lax.ppermute(value, "ctx", [(c, c ^ bit) for c in range(lax.axis_size("ctx"))])


def after(value, earlier):
    return lax.optimization_barrier((value, earlier))[0]


def one_step(work, *inputs):
    taken = lax.axis_index("ctx") // lax.axis_size("ctx") == 0

    def blank(*arrays):
        return jax.tree.map(lambda leaf: jnp.zeros(leaf.shape, leaf.dtype), jax.eval_shape(work, *arrays))

    return lax.cond(taken, work, blank, *inputs)


def reduce_exp(own, own_across, first, first_a, first_b, second, second_across, third, third_across):
    def summed(*terms):
        return sum(term.astype(jnp.float32) for term in terms).astype(jnp.bfloat16)

    got_a, moved_b = swap_exp(first_a), ring_z(first_b)
    total = summed(first, jnp.concatenate([got_a, jnp.zeros_like(first_b)], axis=1))
    second_across = summed(second_across, jnp.concatenate([jnp.zeros_like(first_a), moved_b], axis=1))
    got_second = swap_exp(second_across)
    got_third = swap_exp(after(third_across, second_across))
    total = summed(ring_z(total), second, got_second)
    got_own = swap_exp(after(own_across, got_second))
    total = summed(ring_z(total), third, got_third)
    return ring_z(total), own, got_own


def split_outs(count, rows, width):
    half = width // 2
    places = []
    for at in range(count):
        for columns in ((0, half), (half, width)) if at == 3 else ((0, width),):
            places.append((at * rows, columns))
    return places


def norm_kernel(moved, mine, across, residual, gain, table, stream, out):
    width = stream.shape[1]
    state = residual[...].astype(jnp.float32) + (
        moved[...].astype(jnp.float32) + (mine[...].astype(jnp.float32) + across[...].astype(jnp.float32))
    )
    stream[...] = state
    mean = jnp.sum(state * state, axis=1, keepdims=True) * (1.0 / width)
    out[:, :width] = (state * lax.rsqrt(mean + norm_eps) * gain[...]).astype(out.dtype)
    out[:, width:] = table[...]


def norm_rows(moved, mine, across, residual, gain, table):
    rows, width = residual.shape
    whole = pl.BlockSpec(memory_space=pltpu.VMEM)
    return pl.pallas_call(
        norm_kernel,
        in_specs=[whole] * 6,
        out_specs=[whole] * 2,
        out_shape=[
            pltpu.VMEM((rows, width), jnp.float32),
            pltpu.VMEM((rows, width + table.shape[1]), jnp.bfloat16),
        ],
        compiler_params=pltpu.CompilerParams(vmem_limit_bytes=VMEM_BYTES),
        cost_estimate=pl.CostEstimate(flops=8 * rows * width, bytes_accessed=14 * rows * width, transcendentals=rows),
        name="norm",
    )(moved, mine, across, residual, gain[None, :], table)


def gather_exp(block):
    found = [block, swap_exp(block)]
    for step in range(2, lax.axis_size("exp") // 2):
        block = ring_z(after(block, found[-3]) if len(found) > 2 else block)
        found += [block, swap_exp(block)]
    return found


def pack_kernel(here, latent, k_rope, docs, own, sent):
    keys, lat_width, rope_width = latent.shape[0], latent.shape[1], k_rope.shape[1]
    own[:, :lat_width] = latent[...]
    row = lax.broadcasted_iota(jnp.int32, (128, 128), 0)
    lane = lax.broadcasted_iota(jnp.int32, (128, 128), 1)
    for at in range(keys // 128):
        wide = jnp.broadcast_to(docs[at : at + 1, :], (128, 128))
        column = jnp.sum(jnp.where(row == lane, wide, 0), axis=1, keepdims=True)
        ropes = jnp.concatenate(
            [k_rope[at * 128 : (at + 1) * 128, :].astype(jnp.float32), jnp.zeros((128, 128 - rope_width), jnp.float32)],
            axis=1,
        )
        own[at * 128 : (at + 1) * 128, lat_width:] = jnp.where(
            lane == rope_width, column.astype(jnp.float32), ropes
        ).astype(jnp.bfloat16)
    half = sent.shape[0]
    sent[...] = own[pl.ds(pl.multiple_of(here[0] * half, half), half), :]


def pack_keys(here, latent, k_rope, doc_ids):
    keys, width = latent.shape[0], latent.shape[1] + 128
    whole = pl.BlockSpec(memory_space=pltpu.VMEM)
    return pl.pallas_call(
        pack_kernel,
        in_specs=[pl.BlockSpec(memory_space=pltpu.SMEM)] + [whole] * 3,
        out_specs=[whole] * 2,
        out_shape=[
            jax.ShapeDtypeStruct((keys, width), jnp.bfloat16),
            jax.ShapeDtypeStruct((keys // 2, width), jnp.bfloat16),
        ],
        cost_estimate=pl.CostEstimate(flops=0, bytes_accessed=6 * keys * width, transcendentals=0),
        compiler_params=pltpu.CompilerParams(vmem_limit_bytes=8 * 1024 * 1024),
        name="pack",
    )(here, latent, k_rope, doc_ids.reshape(keys // 128, 128))


def join_kernel(left, right, *refs):
    outs, sems = refs[:-1], refs[-1]
    width, first, copies = left.shape[1], 0, []
    for out in outs:
        for side, weight in enumerate((left, right)):
            copies.append(
                pltpu.make_async_copy(
                    weight.at[pl.ds(first, out.shape[0])],
                    out.at[:, pl.ds(side * width, width)],
                    sems.at[len(copies)],
                )
            )
            copies[-1].start()
        first += out.shape[0]
    for copy in copies:
        copy.wait()


def join_weights(left, right, ends):
    width = left.shape[1]
    counts = [end - first for first, end in zip((0, *ends[:-1]), ends)]
    anywhere = pl.BlockSpec(memory_space=pl.ANY)
    return pl.pallas_call(
        join_kernel,
        in_specs=[anywhere] * 2,
        out_specs=[anywhere] * len(ends),
        out_shape=[jax.ShapeDtypeStruct((count, 2 * width), left.dtype) for count in counts],
        scratch_shapes=[pltpu.SemaphoreType.DMA((2 * len(ends),))],
        compiler_params=pltpu.CompilerParams(vmem_limit_bytes=1024 * 1024),
        cost_estimate=pl.CostEstimate(flops=0, bytes_accessed=8 * left.size, transcendentals=0),
        name="join",
    )(left, right)


def route_kernel(ids, levels, bins, out, *, experts):
    lane = lax.broadcasted_iota(jnp.int32, out.shape, 1)
    table = jnp.zeros(out.shape, jnp.int32)
    for at, what in enumerate((levels[...], bins[...] // 128, bins[...] % 128)):
        for expert in range(experts):
            column = jnp.sum(jnp.where(ids[...] == expert, what, 0), axis=1, keepdims=True)
            table = jnp.where(lane == at * experts + expert, column, table)
    out[...] = table.astype(jnp.float32).astype(out.dtype)


def route_table(expert_ids, gate_levels, bin_ids, experts):
    whole = pl.BlockSpec(memory_space=pltpu.VMEM)
    return pl.pallas_call(
        functools.partial(route_kernel, experts=experts),
        in_specs=[whole] * 3,
        out_specs=whole,
        out_shape=jax.ShapeDtypeStruct((expert_ids.shape[0], 128), jnp.bfloat16),
        compiler_params=pltpu.CompilerParams(vmem_limit_bytes=4 * 1024 * 1024),
        name="route",
    )(expert_ids, gate_levels, bin_ids)


def attend_kernel(scalars, q_nope, q_rope, *refs, heads, rope_width):
    own, near_even, near_a, near_b, far_a, far_b, uv, out, keys, more, sems = refs
    tile, block_len, half = out.shape[0], own.shape[0], far_a.shape[0]
    lat_width = uv.shape[1]
    first = pl.program_id(0) * tile
    places = [
        (own, keys, 0),
        (near_even, keys, block_len),
        (near_a, more, 0),
        (near_b, more, half),
        (far_a, keys, 2 * block_len),
        (far_b, keys, 2 * block_len + half),
    ]
    copies = [
        pltpu.make_async_copy(piece, into.at[pl.ds(at, piece.shape[0])], sems.at[number])
        for number, (piece, into, at) in enumerate(places)
    ]

    @pl.when(pl.program_id(0) == 0)
    def _():
        for copy in copies:
            copy.start()
        for copy in copies:
            copy.wait()
        keys[block_len : 2 * block_len, :] = keys[block_len : 2 * block_len, :] + more[...]

    doc_at = lat_width + rope_width
    pick = (lax.broadcasted_iota(jnp.int32, (8, 128), 1) == rope_width).astype(jnp.bfloat16)
    query_docs = keys[pl.ds(pl.multiple_of(first, tile), tile), lat_width:][:, rope_width : rope_width + 1].astype(jnp.float32)
    over = (((1,), (1,)), ((), ()))
    docs = lax.dot_general(pick, keys[:, lat_width:], over, preferred_element_type=jnp.float32)[0:1, :]
    key_at = lax.broadcasted_iota(jnp.int32, (1, keys.shape[0]), 1)
    docs = jnp.where(key_at < (scalars[1] + 1) * block_len, docs, -1.0)
    spare = jnp.zeros((tile, keys.shape[1] - doc_at), jnp.bfloat16)
    query = jnp.concatenate(
        [
            jnp.concatenate(
                [
                    q_nope[:, head * lat_width : (head + 1) * lat_width],
                    q_rope[:, head * rope_width : (head + 1) * rope_width],
                    spare,
                ],
                axis=1,
            )
            for head in range(heads)
        ],
        axis=0,
    )
    scores, top = [], None
    for block in range(keys.shape[0] // block_len):
        at = slice(block * block_len, (block + 1) * block_len)
        same = docs[:, at] == query_docs
        if block == 0:
            within = lax.broadcasted_iota(jnp.int32, (tile, block_len), 1)
            same = same & (within <= lax.broadcasted_iota(jnp.int32, (tile, block_len), 0) + first)
        raw = lax.dot_general(query, keys[at, :], over, preferred_element_type=jnp.float32)
        same = jnp.concatenate([same] * heads, axis=0)
        scores.append(jnp.where(same, raw * (softmax_scale * LOG2_E), masked_score))
        most = jnp.max(scores[-1], axis=1, keepdims=True)
        top = most if top is None else jnp.maximum(top, most)
    total, accum = 0.0, 0.0
    for block, score in enumerate(scores):
        probs = jnp.exp2(score - top)
        total = total + jnp.sum(probs, axis=1, keepdims=True)
        accum = accum + jnp.dot(
            probs.astype(jnp.bfloat16),
            keys[block * block_len : (block + 1) * block_len, :lat_width],
            preferred_element_type=jnp.float32,
        )
    context = (accum / total).astype(jnp.bfloat16)
    width = uv.shape[2]
    for head in range(heads):
        value = jnp.dot(context[head * tile : (head + 1) * tile], uv[head], preferred_element_type=jnp.float32)
        out[:, head * width : (head + 1) * width] = value.astype(out.dtype)


def attend(here, q_nope, q_rope, pieces, uv_weight, rope_width):
    queries, (block_len, width) = q_nope.shape[0], pieces[0].shape
    heads, lat_width, value_width = uv_weight.shape
    tile = 256
    return pl.pallas_call(
        functools.partial(attend_kernel, heads=heads, rope_width=rope_width),
        grid_spec=pltpu.PrefetchScalarGridSpec(
            num_scalar_prefetch=1,
            grid=(queries // tile,),
            in_specs=[
                pl.BlockSpec((tile, heads * lat_width), lambda i, s: (i, 0)),
                pl.BlockSpec((tile, heads * rope_width), lambda i, s: (i, 0)),
                *[pl.BlockSpec(memory_space=pltpu.HBM) for _ in pieces],
                pl.BlockSpec(uv_weight.shape, lambda i, s: (0, 0, 0)),
            ],
            out_specs=pl.BlockSpec((tile, heads * value_width), lambda i, s: (i, 0)),
            scratch_shapes=[
                pltpu.VMEM((3 * block_len, width), jnp.bfloat16),
                pltpu.VMEM((block_len, width), jnp.bfloat16),
                pltpu.SemaphoreType.DMA((len(pieces),)),
            ],
        ),
        out_shape=jax.ShapeDtypeStruct((queries, heads * value_width), jnp.bfloat16),
        compiler_params=pltpu.CompilerParams(vmem_limit_bytes=24 * 1024 * 1024),
        cost_estimate=pl.CostEstimate(
            flops=6 * heads * queries * block_len * (width + lat_width),
            bytes_accessed=2 * (q_nope.size + 4 * block_len * width + uv_weight.size),
            transcendentals=3 * heads * queries * block_len,
        ),
        name="attend",
    )(here, q_nope, q_rope, *pieces, uv_weight)


def project_kernel(order, values, weight, *outs, places):
    rows = outs[0].shape[0]
    picked = jnp.concatenate(
        [values[pl.ds(pl.multiple_of(order[3 + at] * rows, rows), rows), :] for at in range(values.shape[0] // rows)], axis=0
    )
    result = jnp.dot(picked, weight[...], preferred_element_type=jnp.float32).astype(outs[0].dtype)
    tile, step = weight.shape[1], pl.program_id(0)
    for (first, (start, end)), out in zip(places, outs):

        @pl.when((step >= start // tile) & (step < end // tile))
        def _(first=first, out=out):
            out[...] = result[first : first + rows]


def project_blocks(here, values, weight, count):
    rows, inner = values.shape
    width = weight.shape[1]
    block, tile = rows // count, 896
    places = split_outs(count, block, width)

    def out_spec(columns):
        first, last = columns[0] // tile, columns[1] // tile - 1
        return pl.BlockSpec((block, tile), lambda n, s: (0, jnp.clip(n, first, last) - first))

    return pl.pallas_call(
        functools.partial(project_kernel, places=places),
        grid_spec=pltpu.PrefetchScalarGridSpec(
            num_scalar_prefetch=1,
            grid=(width // tile,),
            in_specs=[
                pl.BlockSpec((rows, inner), lambda n, s: (0, 0)),
                pl.BlockSpec((inner, tile), lambda n, s: (0, n)),
            ],
            out_specs=[out_spec(columns) for _, columns in places],
        ),
        out_shape=[pltpu.VMEM((block, end - start), jnp.bfloat16) for _, (start, end) in places],
        compiler_params=pltpu.CompilerParams(vmem_limit_bytes=32 * 1024 * 1024),
        cost_estimate=pl.CostEstimate(
            flops=2 * rows * inner * width, bytes_accessed=2 * (inner + rows) * width, transcendentals=0
        ),
        name="project",
    )(here, values, weight)


def hidden_kernel(here, *refs, blocks, counts, experts):
    rows, rest = refs[:blocks], refs[blocks:]
    copies = []
    if counts:
        pieces, (hidden, energy_bins, scale, held, row_data, sems) = rest[: sum(counts)], rest[sum(counts) :]
        at = 0
        for part, count in enumerate(counts):
            copies.append([])
            first = 0
            for piece in pieces[at : at + count]:
                into = held.at[part, pl.ds(first, piece.shape[0])]
                copies[-1].append(pltpu.make_async_copy(piece, into, sems.at[at]))
                copies[-1][-1].start()
                first += piece.shape[0]
                at += 1
    else:
        held, hidden, energy_bins, scale, row_data = rest
    parts, inner, units, each = held.shape[0], held.shape[1], held.shape[2] // 2, rows[0].shape[0]
    for at, row in enumerate(rows):
        row_data[at * each : (at + 1) * each, :] = row[:, :inner]
    table = jnp.concatenate([row[:, inner:] for row in rows], axis=0).astype(jnp.float32)
    lane = lax.broadcasted_iota(jnp.int32, table.shape, 1)

    def column(first):
        return jnp.sum(jnp.where(lane == first + here[2], table, 0.0), axis=1, keepdims=True)

    levels = jnp.sum(jnp.where(lane < experts, table, 0.0), axis=1, keepdims=True)
    scale[...] = column(0) / levels
    squares = 0.0
    for part in range(parts):
        for copy in copies[part] if counts else ():
            copy.wait()
        both = jnp.dot(row_data[...], held[part], preferred_element_type=jnp.float32)
        gate_part, up_part = both[:, :units], both[:, units:]
        activation = gate_part / (1.0 + jnp.exp(-gate_part)) * up_part
        hidden[:, part * units : (part + 1) * units] = activation.astype(hidden.dtype)
        squares = squares + jnp.sum(activation * activation, axis=1, keepdims=True)
    place = lane.astype(jnp.float32)
    high = jnp.where(place == column(experts), squares * (1.0 / HID), 0.0)
    low = jnp.where(place == column(2 * experts), 1.0, 0.0)
    counted = jnp.dot(high.T, low, precision=lax.Precision.HIGHEST, preferred_element_type=jnp.float32)
    energy_bins[...] = counted[: energy_bins.shape[0], :]


def hidden_rows(here, rows, weights, experts):
    first = isinstance(weights, list)
    whole = pl.BlockSpec(memory_space=pltpu.VMEM)
    if first:
        counts = tuple(len(pieces) for pieces in weights)
        parts, both = len(weights), weights[0][0].shape[1]
        inner = sum(piece.shape[0] for piece in weights[0])
        operands = [piece for pieces in weights for piece in pieces]
    else:
        counts, (parts, inner, both), operands = None, weights.shape, [weights]
    count = len(rows) * rows[0].shape[0]
    kept = [pltpu.VMEM((parts, inner, both), jnp.bfloat16)] if first else []
    return pl.pallas_call(
        functools.partial(hidden_kernel, blocks=len(rows), counts=counts, experts=experts),
        in_specs=[pl.BlockSpec(memory_space=pltpu.SMEM)]
        + [whole] * len(rows)
        + [pl.BlockSpec(memory_space=pltpu.HBM) if first else whole] * len(operands),
        out_specs=[whole] * (3 + len(kept)),
        out_shape=[
            jax.ShapeDtypeStruct((count, parts * both // 2), jnp.bfloat16),
            jax.ShapeDtypeStruct((NBINS // 128, 128), jnp.float32),
            jax.ShapeDtypeStruct((count, 1), jnp.float32),
            *kept,
        ],
        scratch_shapes=[pltpu.VMEM((count, inner), jnp.bfloat16)]
        + ([pltpu.SemaphoreType.DMA((len(operands),))] if first else []),
        compiler_params=pltpu.CompilerParams(vmem_limit_bytes=VMEM_BYTES),
        cost_estimate=pl.CostEstimate(
            flops=2 * count * inner * parts * both,
            bytes_accessed=2 * inner * (count + parts * both),
            transcendentals=count * parts * both // 2,
        ),
        name="hidden",
    )(here, *rows, *operands)


def down_kernel(*refs, pieces, parts, tile, places):
    hidden, scales, weights = refs[:pieces], refs[pieces : 2 * pieces], refs[2 * pieces : 2 * pieces + parts]
    outs = refs[2 * pieces + parts :]
    rows, units = outs[0].shape[0], weights[0].shape[0]
    each = hidden[0].shape[0]
    for piece in range(pieces):
        for at in range(weights[0].shape[1] // tile):
            columns = slice(at * tile, (at + 1) * tile)
            total = 0.0
            for part, weight in enumerate(weights):
                total = total + jnp.dot(
                    hidden[piece][:, part * units : (part + 1) * units],
                    weight[:, columns],
                    preferred_element_type=jnp.float32,
                )
            total = (total * scales[piece][...]).astype(outs[0].dtype)
            for (first, (start, end)), out in zip(places, outs):
                if piece * each <= first < (piece + 1) * each and start <= at * tile < end:
                    out[:, at * tile - start : (at + 1) * tile - start] = total[first - piece * each :][:rows]


def down_blocks(hidden, scales, weights, count):
    pieces, parts, tile = len(hidden), len(weights), 896
    each, inner = hidden[0].shape
    units, width = weights[0].shape
    whole = pl.BlockSpec(memory_space=pltpu.VMEM)
    places = split_outs(count, pieces * each // count, width)
    return pl.pallas_call(
        functools.partial(down_kernel, pieces=pieces, parts=parts, tile=tile, places=places),
        in_specs=[whole] * (2 * pieces + parts),
        out_specs=[whole] * len(places),
        out_shape=[pltpu.VMEM((pieces * each // count, end - start), jnp.bfloat16) for _, (start, end) in places],
        compiler_params=pltpu.CompilerParams(vmem_limit_bytes=VMEM_BYTES),
        cost_estimate=pl.CostEstimate(
            flops=2 * pieces * each * inner * width,
            bytes_accessed=2 * width * (inner + pieces * each),
            transcendentals=0,
        ),
        name="down",
    )(*hidden, *scales, *weights)


def spread_bins(counts):
    counts = counts.reshape(2, 2, NBINS // 4)
    ctx_here = lax.axis_index("ctx")
    for at, bit in ((ctx_here // 2, 2), (ctx_here % 2, 1)):
        counts = lax.dynamic_index_in_dim(counts, at, 0, keepdims=False) + swap_ctx(
            lax.dynamic_index_in_dim(counts, 1 - at, 0, keepdims=False), bit
        )
    return counts[None, :]


def dense_device(
    residual_in,
    norm_gain,
    q_nope,
    q_rope,
    latent,
    k_rope,
    doc_ids,
    uv_weight,
    out_weight,
    expert_ids,
    gate_levels,
    bin_ids,
    gate_weight,
    up_weight,
    down_weight,
):
    exp_devices, ctx_devices = lax.axis_size("exp"), lax.axis_size("ctx")
    block_len, head_count, lat_width = q_nope.shape
    rope_width = k_rope.shape[1]
    here = positions(exp_devices)

    own, sent = pack_keys(here, latent, k_rope, doc_ids)
    far = lax.ppermute(sent, "ctx", [(c, c + 2) for c in range(ctx_devices - 2)])
    flat_q = q_nope.reshape(block_len, head_count * lat_width)
    w_gate, w_up, w_down = gate_weight[0], up_weight[0], down_weight[0]
    own_both = join_weights(w_gate, w_up, (FIRST_ROWS, w_gate.shape[0]))
    far = after(far, own_both)
    both_a = swap_ctx(after(own_both[0], far), 2)

    def attend_and_project(here, flat_q, q_rope, own, far, uv_weight, out_weight, expert_ids, gate_levels, bin_ids):
        far_across = swap_exp(far)
        near = lax.ppermute(own, "ctx", [(c, c + 1) for c in range(0, ctx_devices, 2)])
        table = route_table(expert_ids, gate_levels, bin_ids, exp_devices)
        early = after(far, (flat_q, table))
        key_pieces = [own, near, *[lax.ppermute(piece, "ctx", [(3, 2)]) for piece in (early, far_across)], far, far_across]
        values = attend(here, flat_q, q_rope, key_pieces, uv_weight, rope_width)
        return project_blocks(here, values, out_weight, exp_devices), table

    there_both = [swap_ctx(piece, 1) for piece in own_both]
    inputs = here, flat_q, q_rope, own, far, uv_weight, out_weight, expert_ids, gate_levels, bin_ids
    partial, table = after(one_step(attend_and_project, *inputs), both_a)
    both_c = swap_ctx(after(own_both[1], (partial[0], both_a)), 2)

    def sum_and_norm(partial, *rest):
        return norm_rows(*reduce_exp(*partial), *rest)

    stream_state, block = one_step(sum_and_norm, partial, residual_in, norm_gain, table)
    across, back, there_c, near_down = after(
        one_step(
            lambda value, *weights: (swap_exp(value), ring_z(value), *[swap_ctx(weight, 1) for weight in weights]),
            block,
            own_both[1],
            w_down,
        ),
        both_c,
    )
    there_both = [there_both[0], there_c]
    far_down = swap_ctx(after(w_down, (both_c, back)), 2)

    def gather_and_hide(block, across, back, here, own_both, there_both, far_both):
        weights = [own_both, there_both, far_both, [swap_ctx(piece, 1) for piece in far_both]]
        found = [block, across, *gather_exp(back)]
        half = len(found) // 2
        *first, held = hidden_rows(here, found[:half], weights, exp_devices)
        last = hidden_rows(here, found[half:], held, exp_devices)
        return [*zip(first, last)]

    hidden, bins, scales = after(
        one_step(gather_and_hide, block, across, back, here, own_both, there_both, [both_a, both_c]), far_down
    )
    downs = [w_down, near_down, far_down, swap_ctx(after(far_down, hidden), 1)]
    expert_out = down_blocks(hidden, scales, downs, exp_devices)
    mixture = reduce_exp(*expert_out)
    layer_out = (stream_state + sum(term.astype(jnp.float32) for term in mixture)).astype(jnp.bfloat16)
    histogram = spread_bins(after(bins[0] + bins[1], expert_out[0]))
    return (layer_out, histogram)


def solution(mesh):
    sizes = mesh.shape

    def on_device(*arrays):
        named_experts = arrays[9].shape[1]
        dense = sizes["exp"] == 8 and sizes["ctx"] == 4 and named_experts == sizes["exp"]
        return (dense_device if dense else routed_device)(*arrays)

    return jax.shard_map(
        on_device,
        mesh=mesh,
        in_specs=(
            P(("ctx", "exp"), None),
            P(),
            P("ctx", "exp", None),
            P("ctx", "exp"),
            P("ctx", None),
            P("ctx", None),
            P("ctx"),
            P("exp", None, None),
            P("exp", None),
            P(("ctx", "exp"), None),
            P(("ctx", "exp"), None),
            P(("ctx", "exp"), None),
            P("exp", None, "ctx"),
            P("exp", None, "ctx"),
            P("exp", "ctx", None),
        ),
        out_specs=(P(("ctx", "exp"), None), P("exp", "ctx")),
        check_vma=False,
    )
```

```python
import functools
import math

import jax
import jax.numpy as jnp
from jax import lax
from jax.experimental import pallas as pl
from jax.experimental.pallas import tpu as pltpu
from jax.sharding import PartitionSpec as P

HID = 1024
NBINS = 2048


softmax_scale = 192.0 ** (-0.5)
norm_eps = 1e-06
masked_score = -1e30
LOG2_E = math.log2(math.e)
FIRST_ROWS = 960
VMEM_BYTES = 14 * 1024 * 1024


def route_slots(expert_ids, experts, capacity):
    flat_ids = expert_ids.reshape(-1)
    onehot = (flat_ids[:, None] == jnp.arange(experts, dtype=jnp.int32)[None, :]).astype(jnp.int32)
    before = jnp.cumsum(onehot, axis=0) - onehot
    slot_rank = jnp.sum(before * onehot, axis=1)
    return (flat_ids * capacity + slot_rank).reshape(expert_ids.shape)


def key_scores(query_nope, query_rope, lat_rows, rope_rows):
    scores = jnp.einsum("qhl,kl->hqk", query_nope, lat_rows, preferred_element_type=jnp.float32)
    scores = scores + jnp.einsum(
        "qhr,kr->hqk", query_rope, rope_rows, preferred_element_type=jnp.float32
    )
    return scores * softmax_scale


def attend_piece(running, key_piece, query_nope, query_rope, query_pos, query_docs):
    lat_rows, rope_rows, doc_rows = key_piece
    key_pos = jnp.arange(lat_rows.shape[0], dtype=jnp.int32)
    allowed = (key_pos[None, :] <= query_pos[:, None]) & (doc_rows[None, :] == query_docs[:, None])
    scores = jnp.where(
        allowed[None], key_scores(query_nope, query_rope, lat_rows, rope_rows), masked_score
    )
    run_max, run_sum, accum = running
    new_max = jnp.maximum(run_max, jnp.max(scores, axis=2))
    probs = jnp.where(allowed[None], jnp.exp(scores - new_max[:, :, None]), 0.0)
    run_sum = jnp.sum(probs, axis=2)
    accum = jnp.einsum(
        "hqk,kl->hql", probs.astype(jnp.bfloat16), lat_rows, preferred_element_type=jnp.float32
    )
    return (new_max, run_sum, accum)


def project_values(context, uv_weight):
    values = jnp.einsum(
        "hql,hlv->qhv", context, uv_weight, preferred_element_type=jnp.float32
    ).astype(jnp.bfloat16)
    return values.reshape(values.shape[0], values.shape[1] * values.shape[2])


def fold_projection(running, uv_weight, out_weight):
    context = (running[2] / running[1][:, :, None]).astype(jnp.bfloat16)
    values = project_values(context, uv_weight)

    def head_rows(row_start, row_count):
        return jnp.dot(values, out_weight, preferred_element_type=jnp.float32)

    return head_rows


def expert_hidden(row_data, w_gate, w_up):
    gate_part = jnp.dot(row_data, w_gate, preferred_element_type=jnp.float32)
    up_part = jnp.dot(row_data, w_up, preferred_element_type=jnp.float32)
    activation = jax.nn.silu(gate_part) * up_part
    return (activation.astype(jnp.bfloat16), jnp.sum(activation * activation, axis=1) / HID)


def bin_energy(energy, slot_bins):
    onehot = (slot_bins[:, None] == jnp.arange(NBINS, dtype=jnp.int32)[None, :]).astype(jnp.float32)
    return jnp.dot(energy[None, :], onehot, precision=lax.Precision.HIGHEST)[0]


def routed_device(
    residual_in,
    norm_gain,
    q_nope,
    q_rope,
    latent,
    k_rope,
    doc_ids,
    uv_weight,
    out_weight,
    expert_ids,
    gate_levels,
    bin_ids,
    gate_weight,
    up_weight,
    down_weight,
):
    exp_devices = lax.axis_size("exp")
    block_len, head_count, lat_width = q_nope.shape
    rope_width = k_rope.shape[1]
    query_first = lax.axis_index("ctx") * block_len
    query_pos = query_first + jnp.arange(block_len, dtype=jnp.int32)
    query_rope = q_rope.reshape(block_len, head_count, rope_width)
    token_count = residual_in.shape[0]
    keys_local = (latent, k_rope, doc_ids)
    initial = (
        jnp.full((head_count, block_len), masked_score, jnp.float32),
        jnp.zeros((head_count, block_len), jnp.float32),
        jnp.zeros((head_count, block_len, lat_width), jnp.float32),
    )
    running = attend_piece(
        initial,
        (
            lax.all_gather(keys_local[0], "ctx", axis=0, tiled=True),
            lax.all_gather(keys_local[1], "ctx", axis=0, tiled=True),
            lax.all_gather(keys_local[2], "ctx", axis=0, tiled=True),
        ),
        q_nope,
        query_rope,
        query_pos,
        doc_ids,
    )
    head_rows = fold_projection(running, uv_weight, out_weight)
    attended = lax.psum_scatter(
        head_rows(jnp.int32(0), token_count * lax.axis_size("exp")),
        "exp",
        scatter_dimension=0,
        tiled=True,
    )
    stream_state = residual_in.astype(jnp.float32) + attended
    normed = (
        stream_state
        * lax.rsqrt(jnp.mean(stream_state * stream_state, axis=1, keepdims=True) + norm_eps)
        * norm_gain
    ).astype(jnp.bfloat16)
    top_count = expert_ids.shape[1]
    capacity = min(token_count, max(2, 2 * token_count * top_count // exp_devices))
    slot_total = exp_devices * capacity
    destination = route_slots(expert_ids, exp_devices, capacity)
    slot_match = destination[:, :, None] == jnp.arange(slot_total, dtype=jnp.int32)[None, None, :]
    selector = jnp.sum(slot_match.astype(jnp.int32), axis=1).astype(jnp.bfloat16)
    outgoing = jnp.einsum("ts,td->sd", selector, normed, preferred_element_type=jnp.float32).astype(
        jnp.bfloat16
    )
    outgoing = outgoing.reshape(exp_devices, capacity, outgoing.shape[1])
    slot_bins = jnp.sum(jnp.where(slot_match, bin_ids[:, :, None], 0), axis=(0, 1)).reshape(
        exp_devices, capacity
    )
    incoming, incoming_bins = (
        lax.all_to_all(outgoing, "exp", split_axis=0, concat_axis=1, tiled=True),
        lax.all_to_all(slot_bins, "exp", split_axis=0, concat_axis=1, tiled=True),
    )
    all_rows, all_bins = (
        lax.all_gather(incoming, "ctx", axis=1, tiled=True),
        lax.all_gather(incoming_bins, "ctx", axis=1, tiled=True),
    )
    hidden, energy = expert_hidden(all_rows[0], gate_weight[0], up_weight[0])
    bin_part = bin_energy(energy, all_bins[0])
    down_local = down_weight[0]
    expert_out = lax.psum_scatter(
        jnp.dot(hidden, down_local, preferred_element_type=jnp.float32).astype(jnp.bfloat16),
        "ctx",
        scatter_dimension=0,
        tiled=True,
    )
    histogram = lax.psum_scatter(bin_part[None, :], "ctx", scatter_dimension=1, tiled=True)
    returned = lax.all_to_all(expert_out[None], "exp", split_axis=1, concat_axis=0, tiled=True)
    levels = gate_levels.astype(jnp.float32)
    route_weights = levels / jnp.sum(levels, axis=1, keepdims=True)
    combiner = jnp.sum(jnp.where(slot_match, route_weights[:, :, None], 0.0), axis=1)
    mixture = jnp.dot(
        combiner,
        returned.reshape(slot_total, returned.shape[2]).astype(jnp.float32),
        precision=lax.Precision.HIGHEST,
    )
    layer_out = (stream_state + mixture).astype(jnp.bfloat16)
    return (layer_out, histogram)


def turn(place):
    return place ^ (place // 2)


def positions(exp_devices):
    ctx_here, here = lax.axis_index("ctx"), lax.axis_index("exp")
    rows = exp_devices // 2
    z_at, x_at = here // 2, here % 2
    order = [
        turn((turn(z_at) - step + rows) % rows) * 2 + (x_at if side == 0 else 1 - x_at)
        for step in range(rows)
        for side in range(2)
    ]
    return jnp.stack([x_at, ctx_here, here, *order]).astype(jnp.int32)


def swap_exp(value, bit=1):
    return lax.ppermute(value, "exp", [(e, e ^ bit) for e in range(lax.axis_size("exp"))])


def ring_z(value):
    rows = lax.axis_size("exp") // 2
    steps = [(turn(at), turn((at + 1) % rows)) for at in range(rows)]
    return lax.ppermute(value, "exp", [(2 * a + x, 2 * b + x) for a, b in steps for x in range(2)])


def swap_ctx(value, bit):
    return lax.ppermute(value, "ctx", [(c, c ^ bit) for c in range(lax.axis_size("ctx"))])


def after(value, earlier):
    return lax.optimization_barrier((value, earlier))[0]


def one_step(work, *inputs):
    taken = lax.axis_index("ctx") // lax.axis_size("ctx") == 0

    def blank(*arrays):
        return jax.tree.map(lambda leaf: jnp.zeros(leaf.shape, leaf.dtype), jax.eval_shape(work, *arrays))

    return lax.cond(taken, work, blank, *inputs)


def reduce_exp(own, own_across, first, first_a, first_b, second, second_across, third, third_across):
    def summed(*terms):
        return sum(term.astype(jnp.float32) for term in terms).astype(jnp.bfloat16)

    got_a, moved_b = swap_exp(first_a), ring_z(first_b)
    total = summed(first, jnp.concatenate([got_a, jnp.zeros_like(first_b)], axis=1))
    second_across = summed(second_across, jnp.concatenate([jnp.zeros_like(first_a), moved_b], axis=1))
    got_second = swap_exp(second_across)
    got_third = swap_exp(after(third_across, second_across))
    total = summed(ring_z(total), second, got_second)
    got_own = swap_exp(after(own_across, got_second))
    total = summed(ring_z(total), third, got_third)
    return ring_z(total), own, got_own


def split_outs(count, rows, width):
    half = width // 2
    places = []
    for at in range(count):
        for columns in ((0, half), (half, width)) if at == 3 else ((0, width),):
            places.append((at * rows, columns))
    return places


def norm_kernel(moved, mine, across, residual, gain, table, stream, out):
    width = stream.shape[1]
    state = residual[...].astype(jnp.float32) + (
        moved[...].astype(jnp.float32) + (mine[...].astype(jnp.float32) + across[...].astype(jnp.float32))
    )
    stream[...] = state
    mean = jnp.sum(state * state, axis=1, keepdims=True) * (1.0 / width)
    out[:, :width] = (state * lax.rsqrt(mean + norm_eps) * gain[...]).astype(out.dtype)
    out[:, width:] = table[...]


def norm_rows(moved, mine, across, residual, gain, table):
    rows, width = residual.shape
    whole = pl.BlockSpec(memory_space=pltpu.VMEM)
    return pl.pallas_call(
        norm_kernel,
        in_specs=[whole] * 6,
        out_specs=[whole] * 2,
        out_shape=[
            pltpu.VMEM((rows, width), jnp.float32),
            pltpu.VMEM((rows, width + table.shape[1]), jnp.bfloat16),
        ],
        compiler_params=pltpu.CompilerParams(vmem_limit_bytes=VMEM_BYTES),
        cost_estimate=pl.CostEstimate(flops=8 * rows * width, bytes_accessed=14 * rows * width, transcendentals=rows),
        name="norm",
    )(moved, mine, across, residual, gain[None, :], table)


def gather_exp(block):
    found = [block, swap_exp(block)]
    for step in range(2, lax.axis_size("exp") // 2):
        block = ring_z(after(block, found[-3]) if len(found) > 2 else block)
        found += [block, swap_exp(block)]
    return found


def pack_kernel(here, latent, k_rope, docs, own, sent):
    keys, lat_width, rope_width = latent.shape[0], latent.shape[1], k_rope.shape[1]
    own[:, :lat_width] = latent[...]
    row = lax.broadcasted_iota(jnp.int32, (128, 128), 0)
    lane = lax.broadcasted_iota(jnp.int32, (128, 128), 1)
    for at in range(keys // 128):
        wide = jnp.broadcast_to(docs[at : at + 1, :], (128, 128))
        column = jnp.sum(jnp.where(row == lane, wide, 0), axis=1, keepdims=True)
        ropes = jnp.concatenate(
            [k_rope[at * 128 : (at + 1) * 128, :].astype(jnp.float32), jnp.zeros((128, 128 - rope_width), jnp.float32)],
            axis=1,
        )
        own[at * 128 : (at + 1) * 128, lat_width:] = jnp.where(
            lane == rope_width, column.astype(jnp.float32), ropes
        ).astype(jnp.bfloat16)
    half = sent.shape[0]
    sent[...] = own[pl.ds(pl.multiple_of(here[0] * half, half), half), :]


def pack_keys(here, latent, k_rope, doc_ids):
    keys, width = latent.shape[0], latent.shape[1] + 128
    whole = pl.BlockSpec(memory_space=pltpu.VMEM)
    return pl.pallas_call(
        pack_kernel,
        in_specs=[pl.BlockSpec(memory_space=pltpu.SMEM)] + [whole] * 3,
        out_specs=[whole] * 2,
        out_shape=[
            jax.ShapeDtypeStruct((keys, width), jnp.bfloat16),
            jax.ShapeDtypeStruct((keys // 2, width), jnp.bfloat16),
        ],
        cost_estimate=pl.CostEstimate(flops=0, bytes_accessed=6 * keys * width, transcendentals=0),
        compiler_params=pltpu.CompilerParams(vmem_limit_bytes=8 * 1024 * 1024),
        name="pack",
    )(here, latent, k_rope, doc_ids.reshape(keys // 128, 128))


def join_kernel(left, right, *refs):
    outs, sems = refs[:-1], refs[-1]
    width, first, copies = left.shape[1], 0, []
    for out in outs:
        for side, weight in enumerate((left, right)):
            copies.append(
                pltpu.make_async_copy(
                    weight.at[pl.ds(first, out.shape[0])],
                    out.at[:, pl.ds(side * width, width)],
                    sems.at[len(copies)],
                )
            )
            copies[-1].start()
        first += out.shape[0]
    for copy in copies:
        copy.wait()


def join_weights(left, right, ends):
    width = left.shape[1]
    counts = [end - first for first, end in zip((0, *ends[:-1]), ends)]
    anywhere = pl.BlockSpec(memory_space=pl.ANY)
    return pl.pallas_call(
        join_kernel,
        in_specs=[anywhere] * 2,
        out_specs=[anywhere] * len(ends),
        out_shape=[jax.ShapeDtypeStruct((count, 2 * width), left.dtype) for count in counts],
        scratch_shapes=[pltpu.SemaphoreType.DMA((2 * len(ends),))],
        compiler_params=pltpu.CompilerParams(vmem_limit_bytes=1024 * 1024),
        cost_estimate=pl.CostEstimate(flops=0, bytes_accessed=8 * left.size, transcendentals=0),
        name="join",
    )(left, right)


def route_kernel(ids, levels, bins, out, *, experts):
    lane = lax.broadcasted_iota(jnp.int32, out.shape, 1)
    table = jnp.zeros(out.shape, jnp.int32)
    for at, what in enumerate((levels[...], bins[...] // 128, bins[...] % 128)):
        for expert in range(experts):
            column = jnp.sum(jnp.where(ids[...] == expert, what, 0), axis=1, keepdims=True)
            table = jnp.where(lane == at * experts + expert, column, table)
    out[...] = table.astype(jnp.float32).astype(out.dtype)


def route_table(expert_ids, gate_levels, bin_ids, experts):
    whole = pl.BlockSpec(memory_space=pltpu.VMEM)
    return pl.pallas_call(
        functools.partial(route_kernel, experts=experts),
        in_specs=[whole] * 3,
        out_specs=whole,
        out_shape=jax.ShapeDtypeStruct((expert_ids.shape[0], 128), jnp.bfloat16),
        compiler_params=pltpu.CompilerParams(vmem_limit_bytes=4 * 1024 * 1024),
        name="route",
    )(expert_ids, gate_levels, bin_ids)


def attend_kernel(scalars, q_nope, q_rope, *refs, heads, rope_width):
    own, near_even, near_a, near_b, far_a, far_b, uv, out, keys, more, sems = refs
    tile, block_len, half = out.shape[0], own.shape[0], far_a.shape[0]
    lat_width = uv.shape[1]
    first = pl.program_id(0) * tile
    places = [
        (own, keys, 0),
        (near_even, keys, block_len),
        (near_a, more, 0),
        (near_b, more, half),
        (far_a, keys, 2 * block_len),
        (far_b, keys, 2 * block_len + half),
    ]
    copies = [
        pltpu.make_async_copy(piece, into.at[pl.ds(at, piece.shape[0])], sems.at[number])
        for number, (piece, into, at) in enumerate(places)
    ]

    @pl.when(pl.program_id(0) == 0)
    def _():
        for copy in copies:
            copy.start()
        for copy in copies:
            copy.wait()
        keys[block_len : 2 * block_len, :] = keys[block_len : 2 * block_len, :] + more[...]

    doc_at = lat_width + rope_width
    pick = (lax.broadcasted_iota(jnp.int32, (8, 128), 1) == rope_width).astype(jnp.bfloat16)
    query_docs = keys[pl.ds(pl.multiple_of(first, tile), tile), lat_width:][:, rope_width : rope_width + 1].astype(jnp.float32)
    over = (((1,), (1,)), ((), ()))
    docs = lax.dot_general(pick, keys[:, lat_width:], over, preferred_element_type=jnp.float32)[0:1, :]
    key_at = lax.broadcasted_iota(jnp.int32, (1, keys.shape[0]), 1)
    docs = jnp.where(key_at < (scalars[1] + 1) * block_len, docs, -1.0)
    spare = jnp.zeros((tile, keys.shape[1] - doc_at), jnp.bfloat16)
    query = jnp.concatenate(
        [
            jnp.concatenate(
                [
                    q_nope[:, head * lat_width : (head + 1) * lat_width],
                    q_rope[:, head * rope_width : (head + 1) * rope_width],
                    spare,
                ],
                axis=1,
            )
            for head in range(heads)
        ],
        axis=0,
    )
    scores, top = [], None
    for block in range(keys.shape[0] // block_len):
        at = slice(block * block_len, (block + 1) * block_len)
        same = docs[:, at] == query_docs
        if block == 0:
            within = lax.broadcasted_iota(jnp.int32, (tile, block_len), 1)
            same = same & (within <= lax.broadcasted_iota(jnp.int32, (tile, block_len), 0) + first)
        raw = lax.dot_general(query, keys[at, :], over, preferred_element_type=jnp.float32)
        same = jnp.concatenate([same] * heads, axis=0)
        scores.append(jnp.where(same, raw * (softmax_scale * LOG2_E), masked_score))
        most = jnp.max(scores[-1], axis=1, keepdims=True)
        top = most if top is None else jnp.maximum(top, most)
    total, accum = 0.0, 0.0
    for block, score in enumerate(scores):
        probs = jnp.exp2(score - top)
        total = total + jnp.sum(probs, axis=1, keepdims=True)
        accum = accum + jnp.dot(
            probs.astype(jnp.bfloat16),
            keys[block * block_len : (block + 1) * block_len, :lat_width],
            preferred_element_type=jnp.float32,
        )
    context = (accum / total).astype(jnp.bfloat16)
    width = uv.shape[2]
    for head in range(heads):
        value = jnp.dot(context[head * tile : (head + 1) * tile], uv[head], preferred_element_type=jnp.float32)
        out[:, head * width : (head + 1) * width] = value.astype(out.dtype)


def attend(here, q_nope, q_rope, pieces, uv_weight, rope_width):
    queries, (block_len, width) = q_nope.shape[0], pieces[0].shape
    heads, lat_width, value_width = uv_weight.shape
    tile = 256
    return pl.pallas_call(
        functools.partial(attend_kernel, heads=heads, rope_width=rope_width),
        grid_spec=pltpu.PrefetchScalarGridSpec(
            num_scalar_prefetch=1,
            grid=(queries // tile,),
            in_specs=[
                pl.BlockSpec((tile, heads * lat_width), lambda i, s: (i, 0)),
                pl.BlockSpec((tile, heads * rope_width), lambda i, s: (i, 0)),
                *[pl.BlockSpec(memory_space=pltpu.HBM) for _ in pieces],
                pl.BlockSpec(uv_weight.shape, lambda i, s: (0, 0, 0)),
            ],
            out_specs=pl.BlockSpec((tile, heads * value_width), lambda i, s: (i, 0)),
            scratch_shapes=[
                pltpu.VMEM((3 * block_len, width), jnp.bfloat16),
                pltpu.VMEM((block_len, width), jnp.bfloat16),
                pltpu.SemaphoreType.DMA((len(pieces),)),
            ],
        ),
        out_shape=jax.ShapeDtypeStruct((queries, heads * value_width), jnp.bfloat16),
        compiler_params=pltpu.CompilerParams(vmem_limit_bytes=24 * 1024 * 1024),
        cost_estimate=pl.CostEstimate(
            flops=6 * heads * queries * block_len * (width + lat_width),
            bytes_accessed=2 * (q_nope.size + 4 * block_len * width + uv_weight.size),
            transcendentals=3 * heads * queries * block_len,
        ),
        name="attend",
    )(here, q_nope, q_rope, *pieces, uv_weight)


def project_kernel(order, values, weight, *outs, places):
    rows = outs[0].shape[0]
    picked = jnp.concatenate(
        [values[pl.ds(pl.multiple_of(order[3 + at] * rows, rows), rows), :] for at in range(values.shape[0] // rows)], axis=0
    )
    result = jnp.dot(picked, weight[...], preferred_element_type=jnp.float32).astype(outs[0].dtype)
    tile, step = weight.shape[1], pl.program_id(0)
    for (first, (start, end)), out in zip(places, outs):

        @pl.when((step >= start // tile) & (step < end // tile))
        def _(first=first, out=out):
            out[...] = result[first : first + rows]


def project_blocks(here, values, weight, count):
    rows, inner = values.shape
    width = weight.shape[1]
    block, tile = rows // count, 896
    places = split_outs(count, block, width)

    def out_spec(columns):
        first, last = columns[0] // tile, columns[1] // tile - 1
        return pl.BlockSpec((block, tile), lambda n, s: (0, jnp.clip(n, first, last) - first))

    return pl.pallas_call(
        functools.partial(project_kernel, places=places),
        grid_spec=pltpu.PrefetchScalarGridSpec(
            num_scalar_prefetch=1,
            grid=(width // tile,),
            in_specs=[
                pl.BlockSpec((rows, inner), lambda n, s: (0, 0)),
                pl.BlockSpec((inner, tile), lambda n, s: (0, n)),
            ],
            out_specs=[out_spec(columns) for _, columns in places],
        ),
        out_shape=[pltpu.VMEM((block, end - start), jnp.bfloat16) for _, (start, end) in places],
        compiler_params=pltpu.CompilerParams(vmem_limit_bytes=32 * 1024 * 1024),
        cost_estimate=pl.CostEstimate(
            flops=2 * rows * inner * width, bytes_accessed=2 * (inner + rows) * width, transcendentals=0
        ),
        name="project",
    )(here, values, weight)


def hidden_kernel(here, *refs, blocks, counts, experts):
    rows, rest = refs[:blocks], refs[blocks:]
    copies = []
    if counts:
        pieces, (hidden, energy_bins, scale, held, row_data, sems) = rest[: sum(counts)], rest[sum(counts) :]
        at = 0
        for part, count in enumerate(counts):
            copies.append([])
            first = 0
            for piece in pieces[at : at + count]:
                into = held.at[part, pl.ds(first, piece.shape[0])]
                copies[-1].append(pltpu.make_async_copy(piece, into, sems.at[at]))
                copies[-1][-1].start()
                first += piece.shape[0]
                at += 1
    else:
        held, hidden, energy_bins, scale, row_data = rest
    parts, inner, units, each = held.shape[0], held.shape[1], held.shape[2] // 2, rows[0].shape[0]
    for at, row in enumerate(rows):
        row_data[at * each : (at + 1) * each, :] = row[:, :inner]
    table = jnp.concatenate([row[:, inner:] for row in rows], axis=0).astype(jnp.float32)
    lane = lax.broadcasted_iota(jnp.int32, table.shape, 1)

    def column(first):
        return jnp.sum(jnp.where(lane == first + here[2], table, 0.0), axis=1, keepdims=True)

    levels = jnp.sum(jnp.where(lane < experts, table, 0.0), axis=1, keepdims=True)
    scale[...] = column(0) / levels
    squares = 0.0
    for part in range(parts):
        for copy in copies[part] if counts else ():
            copy.wait()
        both = jnp.dot(row_data[...], held[part], preferred_element_type=jnp.float32)
        gate_part, up_part = both[:, :units], both[:, units:]
        activation = gate_part / (1.0 + jnp.exp(-gate_part)) * up_part
        hidden[:, part * units : (part + 1) * units] = activation.astype(hidden.dtype)
        squares = squares + jnp.sum(activation * activation, axis=1, keepdims=True)
    place = lane.astype(jnp.float32)
    high = jnp.where(place == column(experts), squares * (1.0 / HID), 0.0)
    low = jnp.where(place == column(2 * experts), 1.0, 0.0)
    counted = jnp.dot(high.T, low, precision=lax.Precision.HIGHEST, preferred_element_type=jnp.float32)
    energy_bins[...] = counted[: energy_bins.shape[0], :]


def hidden_rows(here, rows, weights, experts):
    first = isinstance(weights, list)
    whole = pl.BlockSpec(memory_space=pltpu.VMEM)
    if first:
        counts = tuple(len(pieces) for pieces in weights)
        parts, both = len(weights), weights[0][0].shape[1]
        inner = sum(piece.shape[0] for piece in weights[0])
        operands = [piece for pieces in weights for piece in pieces]
    else:
        counts, (parts, inner, both), operands = None, weights.shape, [weights]
    count = len(rows) * rows[0].shape[0]
    kept = [pltpu.VMEM((parts, inner, both), jnp.bfloat16)] if first else []
    return pl.pallas_call(
        functools.partial(hidden_kernel, blocks=len(rows), counts=counts, experts=experts),
        in_specs=[pl.BlockSpec(memory_space=pltpu.SMEM)]
        + [whole] * len(rows)
        + [pl.BlockSpec(memory_space=pltpu.HBM) if first else whole] * len(operands),
        out_specs=[whole] * (3 + len(kept)),
        out_shape=[
            jax.ShapeDtypeStruct((count, parts * both // 2), jnp.bfloat16),
            jax.ShapeDtypeStruct((NBINS // 128, 128), jnp.float32),
            jax.ShapeDtypeStruct((count, 1), jnp.float32),
            *kept,
        ],
        scratch_shapes=[pltpu.VMEM((count, inner), jnp.bfloat16)]
        + ([pltpu.SemaphoreType.DMA((len(operands),))] if first else []),
        compiler_params=pltpu.CompilerParams(vmem_limit_bytes=VMEM_BYTES),
        cost_estimate=pl.CostEstimate(
            flops=2 * count * inner * parts * both,
            bytes_accessed=2 * inner * (count + parts * both),
            transcendentals=count * parts * both // 2,
        ),
        name="hidden",
    )(here, *rows, *operands)


def down_kernel(*refs, pieces, parts, tile, places):
    hidden, scales, weights = refs[:pieces], refs[pieces : 2 * pieces], refs[2 * pieces : 2 * pieces + parts]
    outs = refs[2 * pieces + parts :]
    rows, units = outs[0].shape[0], weights[0].shape[0]
    each = hidden[0].shape[0]
    for piece in range(pieces):
        for at in range(weights[0].shape[1] // tile):
            columns = slice(at * tile, (at + 1) * tile)
            total = 0.0
            for part, weight in enumerate(weights):
                total = total + jnp.dot(
                    hidden[piece][:, part * units : (part + 1) * units],
                    weight[:, columns],
                    preferred_element_type=jnp.float32,
                )
            total = (total * scales[piece][...]).astype(outs[0].dtype)
            for (first, (start, end)), out in zip(places, outs):
                if piece * each <= first < (piece + 1) * each and start <= at * tile < end:
                    out[:, at * tile - start : (at + 1) * tile - start] = total[first - piece * each :][:rows]


def down_blocks(hidden, scales, weights, count):
    pieces, parts, tile = len(hidden), len(weights), 896
    each, inner = hidden[0].shape
    units, width = weights[0].shape
    whole = pl.BlockSpec(memory_space=pltpu.VMEM)
    places = split_outs(count, pieces * each // count, width)
    return pl.pallas_call(
        functools.partial(down_kernel, pieces=pieces, parts=parts, tile=tile, places=places),
        in_specs=[whole] * (2 * pieces + parts),
        out_specs=[whole] * len(places),
        out_shape=[pltpu.VMEM((pieces * each // count, end - start), jnp.bfloat16) for _, (start, end) in places],
        compiler_params=pltpu.CompilerParams(vmem_limit_bytes=VMEM_BYTES),
        cost_estimate=pl.CostEstimate(
            flops=2 * pieces * each * inner * width,
            bytes_accessed=2 * width * (inner + pieces * each),
            transcendentals=0,
        ),
        name="down",
    )(*hidden, *scales, *weights)


def spread_bins(counts):
    counts = counts.reshape(2, 2, NBINS // 4)
    ctx_here = lax.axis_index("ctx")
    for at, bit in ((ctx_here // 2, 2), (ctx_here % 2, 1)):
        counts = lax.dynamic_index_in_dim(counts, at, 0, keepdims=False) + swap_ctx(
            lax.dynamic_index_in_dim(counts, 1 - at, 0, keepdims=False), bit
        )
    return counts[None, :]


def dense_device(
    residual_in,
    norm_gain,
    q_nope,
    q_rope,
    latent,
    k_rope,
    doc_ids,
    uv_weight,
    out_weight,
    expert_ids,
    gate_levels,
    bin_ids,
    gate_weight,
    up_weight,
    down_weight,
):
    exp_devices, ctx_devices = lax.axis_size("exp"), lax.axis_size("ctx")
    block_len, head_count, lat_width = q_nope.shape
    rope_width = k_rope.shape[1]
    here = positions(exp_devices)

    own, sent = pack_keys(here, latent, k_rope, doc_ids)
    far = lax.ppermute(sent, "ctx", [(c, c + 2) for c in range(ctx_devices - 2)])
    flat_q = q_nope.reshape(block_len, head_count * lat_width)
    w_gate, w_up, w_down = gate_weight[0], up_weight[0], down_weight[0]
    own_both = join_weights(w_gate, w_up, (FIRST_ROWS, w_gate.shape[0]))
    far = after(far, own_both)
    both_a = swap_ctx(after(own_both[0], far), 2)

    def attend_and_project(here, flat_q, q_rope, own, far, uv_weight, out_weight, expert_ids, gate_levels, bin_ids, both):
        far_across = swap_exp(far)
        there = swap_ctx(after(both, far_across), 1)
        near = lax.ppermute(own, "ctx", [(c, c + 1) for c in range(0, ctx_devices, 2)])
        table = route_table(expert_ids, gate_levels, bin_ids, exp_devices)
        early = after(far, (flat_q, table))
        key_pieces = [own, near, *[lax.ppermute(piece, "ctx", [(3, 2)]) for piece in (early, far_across)], far, far_across]
        values = attend(here, flat_q, q_rope, key_pieces, uv_weight, rope_width)
        return project_blocks(here, after(values, there), out_weight, exp_devices), table, there

    inputs = here, flat_q, q_rope, own, far, uv_weight, out_weight, expert_ids, gate_levels, bin_ids, own_both[0]
    partial, table, there_a = after(one_step(attend_and_project, *inputs), both_a)
    both_c = swap_ctx(after(own_both[1], (partial[0], both_a)), 2)

    def sum_and_norm(partial, *rest):
        return norm_rows(*reduce_exp(*partial), *rest)

    stream_state, block = one_step(sum_and_norm, partial, residual_in, norm_gain, table)
    across, back, there_c, near_down = after(
        one_step(
            lambda value, *weights: (swap_exp(value), ring_z(value), *[swap_ctx(weight, 1) for weight in weights]),
            block,
            own_both[1],
            w_down,
        ),
        both_c,
    )
    there_both = [there_a, there_c]
    far_down = swap_ctx(after(w_down, (both_c, back)), 2)

    def gather_and_hide(block, across, back, here, own_both, there_both, far_both):
        weights = [own_both, there_both, far_both, [swap_ctx(piece, 1) for piece in far_both]]
        found = [block, across, *gather_exp(back)]
        half = len(found) // 2
        *first, held = hidden_rows(here, found[:half], weights, exp_devices)
        last = hidden_rows(here, found[half:], held, exp_devices)
        return [*zip(first, last)]

    hidden, bins, scales = after(
        one_step(gather_and_hide, block, across, back, here, own_both, there_both, [both_a, both_c]), far_down
    )
    downs = [w_down, near_down, far_down, swap_ctx(after(far_down, hidden), 1)]
    expert_out = down_blocks(hidden, scales, downs, exp_devices)
    mixture = reduce_exp(*expert_out)
    layer_out = (stream_state + sum(term.astype(jnp.float32) for term in mixture)).astype(jnp.bfloat16)
    histogram = spread_bins(after(bins[0] + bins[1], expert_out[0]))
    return (layer_out, histogram)


def solution(mesh):
    sizes = mesh.shape

    def on_device(*arrays):
        named_experts = arrays[9].shape[1]
        dense = sizes["exp"] == 8 and sizes["ctx"] == 4 and named_experts == sizes["exp"]
        return (dense_device if dense else routed_device)(*arrays)

    return jax.shard_map(
        on_device,
        mesh=mesh,
        in_specs=(
            P(("ctx", "exp"), None),
            P(),
            P("ctx", "exp", None),
            P("ctx", "exp"),
            P("ctx", None),
            P("ctx", None),
            P("ctx"),
            P("exp", None, None),
            P("exp", None),
            P(("ctx", "exp"), None),
            P(("ctx", "exp"), None),
            P(("ctx", "exp"), None),
            P("exp", None, "ctx"),
            P("exp", None, "ctx"),
            P("exp", "ctx", None),
        ),
        out_specs=(P(("ctx", "exp"), None), P("exp", "ctx")),
        check_vma=False,
    )
```

```python
import functools
import math

import jax
import jax.numpy as jnp
from jax import lax
from jax.experimental import pallas as pl
from jax.experimental.pallas import tpu as pltpu
from jax.sharding import PartitionSpec as P

HID = 1024
NBINS = 2048


softmax_scale = 192.0 ** (-0.5)
norm_eps = 1e-06
masked_score = -1e30
LOG2_E = math.log2(math.e)
FIRST_ROWS = 1024
VMEM_BYTES = 14 * 1024 * 1024


def route_slots(expert_ids, experts, capacity):
    flat_ids = expert_ids.reshape(-1)
    onehot = (flat_ids[:, None] == jnp.arange(experts, dtype=jnp.int32)[None, :]).astype(jnp.int32)
    before = jnp.cumsum(onehot, axis=0) - onehot
    slot_rank = jnp.sum(before * onehot, axis=1)
    return (flat_ids * capacity + slot_rank).reshape(expert_ids.shape)


def key_scores(query_nope, query_rope, lat_rows, rope_rows):
    scores = jnp.einsum("qhl,kl->hqk", query_nope, lat_rows, preferred_element_type=jnp.float32)
    scores = scores + jnp.einsum(
        "qhr,kr->hqk", query_rope, rope_rows, preferred_element_type=jnp.float32
    )
    return scores * softmax_scale


def attend_piece(running, key_piece, query_nope, query_rope, query_pos, query_docs):
    lat_rows, rope_rows, doc_rows = key_piece
    key_pos = jnp.arange(lat_rows.shape[0], dtype=jnp.int32)
    allowed = (key_pos[None, :] <= query_pos[:, None]) & (doc_rows[None, :] == query_docs[:, None])
    scores = jnp.where(
        allowed[None], key_scores(query_nope, query_rope, lat_rows, rope_rows), masked_score
    )
    run_max, run_sum, accum = running
    new_max = jnp.maximum(run_max, jnp.max(scores, axis=2))
    probs = jnp.where(allowed[None], jnp.exp(scores - new_max[:, :, None]), 0.0)
    run_sum = jnp.sum(probs, axis=2)
    accum = jnp.einsum(
        "hqk,kl->hql", probs.astype(jnp.bfloat16), lat_rows, preferred_element_type=jnp.float32
    )
    return (new_max, run_sum, accum)


def project_values(context, uv_weight):
    values = jnp.einsum(
        "hql,hlv->qhv", context, uv_weight, preferred_element_type=jnp.float32
    ).astype(jnp.bfloat16)
    return values.reshape(values.shape[0], values.shape[1] * values.shape[2])


def fold_projection(running, uv_weight, out_weight):
    context = (running[2] / running[1][:, :, None]).astype(jnp.bfloat16)
    values = project_values(context, uv_weight)

    def head_rows(row_start, row_count):
        return jnp.dot(values, out_weight, preferred_element_type=jnp.float32)

    return head_rows


def expert_hidden(row_data, w_gate, w_up):
    gate_part = jnp.dot(row_data, w_gate, preferred_element_type=jnp.float32)
    up_part = jnp.dot(row_data, w_up, preferred_element_type=jnp.float32)
    activation = jax.nn.silu(gate_part) * up_part
    return (activation.astype(jnp.bfloat16), jnp.sum(activation * activation, axis=1) / HID)


def bin_energy(energy, slot_bins):
    onehot = (slot_bins[:, None] == jnp.arange(NBINS, dtype=jnp.int32)[None, :]).astype(jnp.float32)
    return jnp.dot(energy[None, :], onehot, precision=lax.Precision.HIGHEST)[0]


def routed_device(
    residual_in,
    norm_gain,
    q_nope,
    q_rope,
    latent,
    k_rope,
    doc_ids,
    uv_weight,
    out_weight,
    expert_ids,
    gate_levels,
    bin_ids,
    gate_weight,
    up_weight,
    down_weight,
):
    exp_devices = lax.axis_size("exp")
    block_len, head_count, lat_width = q_nope.shape
    rope_width = k_rope.shape[1]
    query_first = lax.axis_index("ctx") * block_len
    query_pos = query_first + jnp.arange(block_len, dtype=jnp.int32)
    query_rope = q_rope.reshape(block_len, head_count, rope_width)
    token_count = residual_in.shape[0]
    keys_local = (latent, k_rope, doc_ids)
    initial = (
        jnp.full((head_count, block_len), masked_score, jnp.float32),
        jnp.zeros((head_count, block_len), jnp.float32),
        jnp.zeros((head_count, block_len, lat_width), jnp.float32),
    )
    running = attend_piece(
        initial,
        (
            lax.all_gather(keys_local[0], "ctx", axis=0, tiled=True),
            lax.all_gather(keys_local[1], "ctx", axis=0, tiled=True),
            lax.all_gather(keys_local[2], "ctx", axis=0, tiled=True),
        ),
        q_nope,
        query_rope,
        query_pos,
        doc_ids,
    )
    head_rows = fold_projection(running, uv_weight, out_weight)
    attended = lax.psum_scatter(
        head_rows(jnp.int32(0), token_count * lax.axis_size("exp")),
        "exp",
        scatter_dimension=0,
        tiled=True,
    )
    stream_state = residual_in.astype(jnp.float32) + attended
    normed = (
        stream_state
        * lax.rsqrt(jnp.mean(stream_state * stream_state, axis=1, keepdims=True) + norm_eps)
        * norm_gain
    ).astype(jnp.bfloat16)
    top_count = expert_ids.shape[1]
    capacity = min(token_count, max(2, 2 * token_count * top_count // exp_devices))
    slot_total = exp_devices * capacity
    destination = route_slots(expert_ids, exp_devices, capacity)
    slot_match = destination[:, :, None] == jnp.arange(slot_total, dtype=jnp.int32)[None, None, :]
    selector = jnp.sum(slot_match.astype(jnp.int32), axis=1).astype(jnp.bfloat16)
    outgoing = jnp.einsum("ts,td->sd", selector, normed, preferred_element_type=jnp.float32).astype(
        jnp.bfloat16
    )
    outgoing = outgoing.reshape(exp_devices, capacity, outgoing.shape[1])
    slot_bins = jnp.sum(jnp.where(slot_match, bin_ids[:, :, None], 0), axis=(0, 1)).reshape(
        exp_devices, capacity
    )
    incoming, incoming_bins = (
        lax.all_to_all(outgoing, "exp", split_axis=0, concat_axis=1, tiled=True),
        lax.all_to_all(slot_bins, "exp", split_axis=0, concat_axis=1, tiled=True),
    )
    all_rows, all_bins = (
        lax.all_gather(incoming, "ctx", axis=1, tiled=True),
        lax.all_gather(incoming_bins, "ctx", axis=1, tiled=True),
    )
    hidden, energy = expert_hidden(all_rows[0], gate_weight[0], up_weight[0])
    bin_part = bin_energy(energy, all_bins[0])
    down_local = down_weight[0]
    expert_out = lax.psum_scatter(
        jnp.dot(hidden, down_local, preferred_element_type=jnp.float32).astype(jnp.bfloat16),
        "ctx",
        scatter_dimension=0,
        tiled=True,
    )
    histogram = lax.psum_scatter(bin_part[None, :], "ctx", scatter_dimension=1, tiled=True)
    returned = lax.all_to_all(expert_out[None], "exp", split_axis=1, concat_axis=0, tiled=True)
    levels = gate_levels.astype(jnp.float32)
    route_weights = levels / jnp.sum(levels, axis=1, keepdims=True)
    combiner = jnp.sum(jnp.where(slot_match, route_weights[:, :, None], 0.0), axis=1)
    mixture = jnp.dot(
        combiner,
        returned.reshape(slot_total, returned.shape[2]).astype(jnp.float32),
        precision=lax.Precision.HIGHEST,
    )
    layer_out = (stream_state + mixture).astype(jnp.bfloat16)
    return (layer_out, histogram)


def turn(place):
    return place ^ (place // 2)


def positions(exp_devices):
    ctx_here, here = lax.axis_index("ctx"), lax.axis_index("exp")
    rows = exp_devices // 2
    z_at, x_at = here // 2, here % 2
    order = [
        turn((turn(z_at) - step + rows) % rows) * 2 + (x_at if side == 0 else 1 - x_at)
        for step in range(rows)
        for side in range(2)
    ]
    return jnp.stack([x_at, ctx_here, here, *order]).astype(jnp.int32)


def swap_exp(value, bit=1):
    return lax.ppermute(value, "exp", [(e, e ^ bit) for e in range(lax.axis_size("exp"))])


def ring_z(value):
    rows = lax.axis_size("exp") // 2
    steps = [(turn(at), turn((at + 1) % rows)) for at in range(rows)]
    return lax.ppermute(value, "exp", [(2 * a + x, 2 * b + x) for a, b in steps for x in range(2)])


def swap_ctx(value, bit):
    return lax.ppermute(value, "ctx", [(c, c ^ bit) for c in range(lax.axis_size("ctx"))])


def after(value, earlier):
    return lax.optimization_barrier((value, earlier))[0]


def one_step(work, *inputs):
    taken = lax.axis_index("ctx") // lax.axis_size("ctx") == 0

    def blank(*arrays):
        return jax.tree.map(lambda leaf: jnp.zeros(leaf.shape, leaf.dtype), jax.eval_shape(work, *arrays))

    return lax.cond(taken, work, blank, *inputs)


def reduce_exp(own, own_across, first, first_a, first_b, second, second_across, third, third_across):
    def summed(*terms):
        return sum(term.astype(jnp.float32) for term in terms).astype(jnp.bfloat16)

    got_a, moved_b = swap_exp(first_a), ring_z(first_b)
    total = summed(first, jnp.concatenate([got_a, jnp.zeros_like(first_b)], axis=1))
    second_across = summed(second_across, jnp.concatenate([jnp.zeros_like(first_a), moved_b], axis=1))
    got_second = swap_exp(second_across)
    got_third = swap_exp(after(third_across, second_across))
    total = summed(ring_z(total), second, got_second)
    got_own = swap_exp(after(own_across, got_second))
    total = summed(ring_z(total), third, got_third)
    return ring_z(total), own, got_own


def split_outs(count, rows, width):
    half = width // 2
    places = []
    for at in range(count):
        for columns in ((0, half), (half, width)) if at == 3 else ((0, width),):
            places.append((at * rows, columns))
    return places


def norm_kernel(moved, mine, across, residual, gain, table, stream, out):
    width = stream.shape[1]
    state = residual[...].astype(jnp.float32) + (
        moved[...].astype(jnp.float32) + (mine[...].astype(jnp.float32) + across[...].astype(jnp.float32))
    )
    stream[...] = state
    mean = jnp.sum(state * state, axis=1, keepdims=True) * (1.0 / width)
    out[:, :width] = (state * lax.rsqrt(mean + norm_eps) * gain[...]).astype(out.dtype)
    out[:, width:] = table[...]


def norm_rows(moved, mine, across, residual, gain, table):
    rows, width = residual.shape
    whole = pl.BlockSpec(memory_space=pltpu.VMEM)
    return pl.pallas_call(
        norm_kernel,
        in_specs=[whole] * 6,
        out_specs=[whole] * 2,
        out_shape=[
            pltpu.VMEM((rows, width), jnp.float32),
            pltpu.VMEM((rows, width + table.shape[1]), jnp.bfloat16),
        ],
        compiler_params=pltpu.CompilerParams(vmem_limit_bytes=VMEM_BYTES),
        cost_estimate=pl.CostEstimate(flops=8 * rows * width, bytes_accessed=14 * rows * width, transcendentals=rows),
        name="norm",
    )(moved, mine, across, residual, gain[None, :], table)


def gather_exp(block):
    found = [block, swap_exp(block)]
    for step in range(2, lax.axis_size("exp") // 2):
        block = ring_z(after(block, found[-3]) if len(found) > 2 else block)
        found += [block, swap_exp(block)]
    return found


def pack_kernel(here, latent, k_rope, docs, own, sent, sem):
    keys, lat_width, rope_width = latent.shape[0], latent.shape[1], k_rope.shape[1]
    copy = pltpu.make_async_copy(latent, own.at[:, pl.ds(0, lat_width)], sem)
    copy.start()
    row = lax.broadcasted_iota(jnp.int32, (128, 128), 0)
    lane = lax.broadcasted_iota(jnp.int32, (128, 128), 1)
    for at in range(keys // 128):
        wide = jnp.broadcast_to(docs[at : at + 1, :], (128, 128))
        column = jnp.sum(jnp.where(row == lane, wide, 0), axis=1, keepdims=True)
        ropes = jnp.concatenate(
            [k_rope[at * 128 : (at + 1) * 128, :].astype(jnp.float32), jnp.zeros((128, 128 - rope_width), jnp.float32)],
            axis=1,
        )
        own[at * 128 : (at + 1) * 128, lat_width:] = jnp.where(
            lane == rope_width, column.astype(jnp.float32), ropes
        ).astype(jnp.bfloat16)
    copy.wait()
    half = sent.shape[0]
    sent[...] = own[pl.ds(pl.multiple_of(here[0] * half, half), half), :]


def pack_keys(here, latent, k_rope, doc_ids):
    keys, width = latent.shape[0], latent.shape[1] + 128
    whole = pl.BlockSpec(memory_space=pltpu.VMEM)
    return pl.pallas_call(
        pack_kernel,
        in_specs=[pl.BlockSpec(memory_space=pltpu.SMEM), pl.BlockSpec(memory_space=pltpu.HBM), whole, whole],
        out_specs=[whole] * 2,
        scratch_shapes=[pltpu.SemaphoreType.DMA],
        out_shape=[
            jax.ShapeDtypeStruct((keys, width), jnp.bfloat16),
            jax.ShapeDtypeStruct((keys // 2, width), jnp.bfloat16),
        ],
        cost_estimate=pl.CostEstimate(flops=0, bytes_accessed=6 * keys * width, transcendentals=0),
        compiler_params=pltpu.CompilerParams(vmem_limit_bytes=8 * 1024 * 1024),
        name="pack",
    )(here, pltpu.with_memory_space_constraint(latent, pltpu.HBM), k_rope, doc_ids.reshape(keys // 128, 128))


def join_kernel(left, right, *refs):
    outs, sems = refs[:-1], refs[-1]
    width, first, copies = left.shape[1], 0, []
    for out in outs:
        for side, weight in enumerate((left, right)):
            copies.append(
                pltpu.make_async_copy(
                    weight.at[pl.ds(first, out.shape[0])],
                    out.at[:, pl.ds(side * width, width)],
                    sems.at[len(copies)],
                )
            )
            copies[-1].start()
        first += out.shape[0]
    for copy in copies:
        copy.wait()


def join_weights(left, right, ends):
    width = left.shape[1]
    counts = [end - first for first, end in zip((0, *ends[:-1]), ends)]
    anywhere = pl.BlockSpec(memory_space=pl.ANY)
    return pl.pallas_call(
        join_kernel,
        in_specs=[anywhere] * 2,
        out_specs=[anywhere] * len(ends),
        out_shape=[jax.ShapeDtypeStruct((count, 2 * width), left.dtype) for count in counts],
        scratch_shapes=[pltpu.SemaphoreType.DMA((2 * len(ends),))],
        compiler_params=pltpu.CompilerParams(vmem_limit_bytes=1024 * 1024),
        cost_estimate=pl.CostEstimate(flops=0, bytes_accessed=8 * left.size, transcendentals=0),
        name="join",
    )(left, right)


def route_kernel(ids, levels, bins, out, *, experts):
    lane = lax.broadcasted_iota(jnp.int32, out.shape, 1)
    table = jnp.zeros(out.shape, jnp.int32)
    for at, what in enumerate((levels[...], bins[...] // 128, bins[...] % 128)):
        for expert in range(experts):
            column = jnp.sum(jnp.where(ids[...] == expert, what, 0), axis=1, keepdims=True)
            table = jnp.where(lane == at * experts + expert, column, table)
    out[...] = table.astype(jnp.float32).astype(out.dtype)


def route_table(expert_ids, gate_levels, bin_ids, experts):
    whole = pl.BlockSpec(memory_space=pltpu.VMEM)
    return pl.pallas_call(
        functools.partial(route_kernel, experts=experts),
        in_specs=[whole] * 3,
        out_specs=whole,
        out_shape=jax.ShapeDtypeStruct((expert_ids.shape[0], 128), jnp.bfloat16),
        compiler_params=pltpu.CompilerParams(vmem_limit_bytes=4 * 1024 * 1024),
        name="route",
    )(expert_ids, gate_levels, bin_ids)


def attend_kernel(scalars, q_nope, q_rope, *refs, heads, rope_width):
    own, near_even, near_a, near_b, far_a, far_b, uv, out, keys, more, sems = refs
    tile, block_len, half = out.shape[0], own.shape[0], far_a.shape[0]
    lat_width = uv.shape[1]
    first = pl.program_id(0) * tile
    places = [
        (own, keys, 0),
        (near_even, keys, block_len),
        (near_a, more, 0),
        (near_b, more, half),
        (far_a, keys, 2 * block_len),
        (far_b, keys, 2 * block_len + half),
    ]
    copies = [
        pltpu.make_async_copy(piece, into.at[pl.ds(at, piece.shape[0])], sems.at[number])
        for number, (piece, into, at) in enumerate(places)
    ]

    @pl.when(pl.program_id(0) == 0)
    def _():
        for copy in copies:
            copy.start()
        for copy in copies:
            copy.wait()
        keys[block_len : 2 * block_len, :] = keys[block_len : 2 * block_len, :] + more[...]

    doc_at = lat_width + rope_width
    pick = (lax.broadcasted_iota(jnp.int32, (8, 128), 1) == rope_width).astype(jnp.bfloat16)
    query_docs = keys[pl.ds(pl.multiple_of(first, tile), tile), lat_width:][:, rope_width : rope_width + 1].astype(jnp.float32)
    over = (((1,), (1,)), ((), ()))
    docs = lax.dot_general(pick, keys[:, lat_width:], over, preferred_element_type=jnp.float32)[0:1, :]
    key_at = lax.broadcasted_iota(jnp.int32, (1, keys.shape[0]), 1)
    docs = jnp.where(key_at < (scalars[1] + 1) * block_len, docs, -1.0)
    spare = jnp.zeros((tile, keys.shape[1] - doc_at), jnp.bfloat16)
    query = jnp.concatenate(
        [
            jnp.concatenate(
                [
                    q_nope[:, head * lat_width : (head + 1) * lat_width],
                    q_rope[:, head * rope_width : (head + 1) * rope_width],
                    spare,
                ],
                axis=1,
            )
            for head in range(heads)
        ],
        axis=0,
    )
    scores, top = [], None
    for block in range(keys.shape[0] // block_len):
        at = slice(block * block_len, (block + 1) * block_len)
        same = docs[:, at] == query_docs
        if block == 0:
            within = lax.broadcasted_iota(jnp.int32, (tile, block_len), 1)
            same = same & (within <= lax.broadcasted_iota(jnp.int32, (tile, block_len), 0) + first)
        raw = lax.dot_general(query, keys[at, :], over, preferred_element_type=jnp.float32)
        same = jnp.concatenate([same] * heads, axis=0)
        scores.append(jnp.where(same, raw * (softmax_scale * LOG2_E), masked_score))
        most = jnp.max(scores[-1], axis=1, keepdims=True)
        top = most if top is None else jnp.maximum(top, most)
    total, accum = 0.0, 0.0
    for block, score in enumerate(scores):
        probs = jnp.exp2(score - top)
        total = total + jnp.sum(probs, axis=1, keepdims=True)
        accum = accum + jnp.dot(
            probs.astype(jnp.bfloat16),
            keys[block * block_len : (block + 1) * block_len, :lat_width],
            preferred_element_type=jnp.float32,
        )
    context = (accum / total).astype(jnp.bfloat16)
    width = uv.shape[2]
    for head in range(heads):
        value = jnp.dot(context[head * tile : (head + 1) * tile], uv[head], preferred_element_type=jnp.float32)
        out[:, head * width : (head + 1) * width] = value.astype(out.dtype)


def attend(here, q_nope, q_rope, pieces, uv_weight, rope_width):
    queries, (block_len, width) = q_nope.shape[0], pieces[0].shape
    heads, lat_width, value_width = uv_weight.shape
    tile = 256
    return pl.pallas_call(
        functools.partial(attend_kernel, heads=heads, rope_width=rope_width),
        grid_spec=pltpu.PrefetchScalarGridSpec(
            num_scalar_prefetch=1,
            grid=(queries // tile,),
            in_specs=[
                pl.BlockSpec((tile, heads * lat_width), lambda i, s: (i, 0)),
                pl.BlockSpec((tile, heads * rope_width), lambda i, s: (i, 0)),
                *[pl.BlockSpec(memory_space=pltpu.HBM) for _ in pieces],
                pl.BlockSpec(uv_weight.shape, lambda i, s: (0, 0, 0)),
            ],
            out_specs=pl.BlockSpec((tile, heads * value_width), lambda i, s: (i, 0)),
            scratch_shapes=[
                pltpu.VMEM((3 * block_len, width), jnp.bfloat16),
                pltpu.VMEM((block_len, width), jnp.bfloat16),
                pltpu.SemaphoreType.DMA((len(pieces),)),
            ],
        ),
        out_shape=jax.ShapeDtypeStruct((queries, heads * value_width), jnp.bfloat16),
        compiler_params=pltpu.CompilerParams(vmem_limit_bytes=24 * 1024 * 1024),
        cost_estimate=pl.CostEstimate(
            flops=6 * heads * queries * block_len * (width + lat_width),
            bytes_accessed=2 * (q_nope.size + 4 * block_len * width + uv_weight.size),
            transcendentals=3 * heads * queries * block_len,
        ),
        name="attend",
    )(here, q_nope, q_rope, *pieces, uv_weight)


def project_kernel(order, values, weight, *outs, places):
    rows = outs[0].shape[0]
    picked = jnp.concatenate(
        [values[pl.ds(pl.multiple_of(order[3 + at] * rows, rows), rows), :] for at in range(values.shape[0] // rows)], axis=0
    )
    result = jnp.dot(picked, weight[...], preferred_element_type=jnp.float32).astype(outs[0].dtype)
    tile, step = weight.shape[1], pl.program_id(0)
    for (first, (start, end)), out in zip(places, outs):

        @pl.when((step >= start // tile) & (step < end // tile))
        def _(first=first, out=out):
            out[...] = result[first : first + rows]


def project_blocks(here, values, weight, count):
    rows, inner = values.shape
    width = weight.shape[1]
    block, tile = rows // count, 896
    places = split_outs(count, block, width)

    def out_spec(columns):
        first, last = columns[0] // tile, columns[1] // tile - 1
        return pl.BlockSpec((block, tile), lambda n, s: (0, jnp.clip(n, first, last) - first))

    return pl.pallas_call(
        functools.partial(project_kernel, places=places),
        grid_spec=pltpu.PrefetchScalarGridSpec(
            num_scalar_prefetch=1,
            grid=(width // tile,),
            in_specs=[
                pl.BlockSpec((rows, inner), lambda n, s: (0, 0)),
                pl.BlockSpec((inner, tile), lambda n, s: (0, n)),
            ],
            out_specs=[out_spec(columns) for _, columns in places],
        ),
        out_shape=[pltpu.VMEM((block, end - start), jnp.bfloat16) for _, (start, end) in places],
        compiler_params=pltpu.CompilerParams(vmem_limit_bytes=32 * 1024 * 1024),
        cost_estimate=pl.CostEstimate(
            flops=2 * rows * inner * width, bytes_accessed=2 * (inner + rows) * width, transcendentals=0
        ),
        name="project",
    )(here, values, weight)


def hidden_kernel(here, *refs, blocks, counts, experts):
    rows, rest = refs[:blocks], refs[blocks:]
    copies = []
    if counts:
        pieces, (hidden, energy_bins, scale, held, row_data, sems) = rest[: sum(counts)], rest[sum(counts) :]
        at = 0
        for part, count in enumerate(counts):
            copies.append([])
            first = 0
            for piece in pieces[at : at + count]:
                into = held.at[part, pl.ds(first, piece.shape[0])]
                copies[-1].append(pltpu.make_async_copy(piece, into, sems.at[at]))
                copies[-1][-1].start()
                first += piece.shape[0]
                at += 1
    else:
        held, hidden, energy_bins, scale, row_data = rest
    parts, inner, units, each = held.shape[0], held.shape[1], held.shape[2] // 2, rows[0].shape[0]
    for at, row in enumerate(rows):
        row_data[at * each : (at + 1) * each, :] = row[:, :inner]
    table = jnp.concatenate([row[:, inner:] for row in rows], axis=0).astype(jnp.float32)
    lane = lax.broadcasted_iota(jnp.int32, table.shape, 1)

    def column(first):
        return jnp.sum(jnp.where(lane == first + here[2], table, 0.0), axis=1, keepdims=True)

    levels = jnp.sum(jnp.where(lane < experts, table, 0.0), axis=1, keepdims=True)
    scale[...] = column(0) / levels
    squares = 0.0
    for part in range(parts):
        for copy in copies[part] if counts else ():
            copy.wait()
        both = jnp.dot(row_data[...], held[part], preferred_element_type=jnp.float32)
        gate_part, up_part = both[:, :units], both[:, units:]
        activation = gate_part / (1.0 + jnp.exp(-gate_part)) * up_part
        hidden[:, part * units : (part + 1) * units] = activation.astype(hidden.dtype)
        squares = squares + jnp.sum(activation * activation, axis=1, keepdims=True)
    place = lane.astype(jnp.float32)
    high = jnp.where(place == column(experts), squares * (1.0 / HID), 0.0)
    low = jnp.where(place == column(2 * experts), 1.0, 0.0)
    counted = jnp.dot(high.T, low, precision=lax.Precision.HIGHEST, preferred_element_type=jnp.float32)
    energy_bins[...] = counted[: energy_bins.shape[0], :]


def hidden_rows(here, rows, weights, experts):
    first = isinstance(weights, list)
    whole = pl.BlockSpec(memory_space=pltpu.VMEM)
    if first:
        counts = tuple(len(pieces) for pieces in weights)
        parts, both = len(weights), weights[0][0].shape[1]
        inner = sum(piece.shape[0] for piece in weights[0])
        operands = [piece for pieces in weights for piece in pieces]
    else:
        counts, (parts, inner, both), operands = None, weights.shape, [weights]
    count = len(rows) * rows[0].shape[0]
    kept = [pltpu.VMEM((parts, inner, both), jnp.bfloat16)] if first else []
    return pl.pallas_call(
        functools.partial(hidden_kernel, blocks=len(rows), counts=counts, experts=experts),
        in_specs=[pl.BlockSpec(memory_space=pltpu.SMEM)]
        + [whole] * len(rows)
        + [pl.BlockSpec(memory_space=pltpu.HBM) if first else whole] * len(operands),
        out_specs=[whole] * (3 + len(kept)),
        out_shape=[
            jax.ShapeDtypeStruct((count, parts * both // 2), jnp.bfloat16),
            jax.ShapeDtypeStruct((NBINS // 128, 128), jnp.float32),
            jax.ShapeDtypeStruct((count, 1), jnp.float32),
            *kept,
        ],
        scratch_shapes=[pltpu.VMEM((count, inner), jnp.bfloat16)]
        + ([pltpu.SemaphoreType.DMA((len(operands),))] if first else []),
        compiler_params=pltpu.CompilerParams(vmem_limit_bytes=VMEM_BYTES),
        cost_estimate=pl.CostEstimate(
            flops=2 * count * inner * parts * both,
            bytes_accessed=2 * inner * (count + parts * both),
            transcendentals=count * parts * both // 2,
        ),
        name="hidden",
    )(here, *rows, *operands)


def down_kernel(*refs, pieces, parts, tile, places):
    hidden, scales, weights = refs[:pieces], refs[pieces : 2 * pieces], refs[2 * pieces : 2 * pieces + parts]
    outs = refs[2 * pieces + parts :]
    rows, units = outs[0].shape[0], weights[0].shape[0]
    each = hidden[0].shape[0]
    for piece in range(pieces):
        for at in range(weights[0].shape[1] // tile):
            columns = slice(at * tile, (at + 1) * tile)
            total = 0.0
            for part, weight in enumerate(weights):
                total = total + jnp.dot(
                    hidden[piece][:, part * units : (part + 1) * units],
                    weight[:, columns],
                    preferred_element_type=jnp.float32,
                )
            total = (total * scales[piece][...]).astype(outs[0].dtype)
            for (first, (start, end)), out in zip(places, outs):
                if piece * each <= first < (piece + 1) * each and start <= at * tile < end:
                    out[:, at * tile - start : (at + 1) * tile - start] = total[first - piece * each :][:rows]


def down_blocks(hidden, scales, weights, count):
    pieces, parts, tile = len(hidden), len(weights), 896
    each, inner = hidden[0].shape
    units, width = weights[0].shape
    whole = pl.BlockSpec(memory_space=pltpu.VMEM)
    places = split_outs(count, pieces * each // count, width)
    return pl.pallas_call(
        functools.partial(down_kernel, pieces=pieces, parts=parts, tile=tile, places=places),
        in_specs=[whole] * (2 * pieces + parts),
        out_specs=[whole] * len(places),
        out_shape=[pltpu.VMEM((pieces * each // count, end - start), jnp.bfloat16) for _, (start, end) in places],
        compiler_params=pltpu.CompilerParams(vmem_limit_bytes=VMEM_BYTES),
        cost_estimate=pl.CostEstimate(
            flops=2 * pieces * each * inner * width,
            bytes_accessed=2 * width * (inner + pieces * each),
            transcendentals=0,
        ),
        name="down",
    )(*hidden, *scales, *weights)


def spread_bins(counts):
    counts = counts.reshape(2, 2, NBINS // 4)
    ctx_here = lax.axis_index("ctx")
    for at, bit in ((ctx_here // 2, 2), (ctx_here % 2, 1)):
        counts = lax.dynamic_index_in_dim(counts, at, 0, keepdims=False) + swap_ctx(
            lax.dynamic_index_in_dim(counts, 1 - at, 0, keepdims=False), bit
        )
    return counts[None, :]


def dense_device(
    residual_in,
    norm_gain,
    q_nope,
    q_rope,
    latent,
    k_rope,
    doc_ids,
    uv_weight,
    out_weight,
    expert_ids,
    gate_levels,
    bin_ids,
    gate_weight,
    up_weight,
    down_weight,
):
    exp_devices, ctx_devices = lax.axis_size("exp"), lax.axis_size("ctx")
    block_len, head_count, lat_width = q_nope.shape
    rope_width = k_rope.shape[1]
    here = positions(exp_devices)

    own, sent = pack_keys(here, latent, k_rope, doc_ids)
    far = lax.ppermute(sent, "ctx", [(c, c + 2) for c in range(ctx_devices - 2)])
    flat_q = q_nope.reshape(block_len, head_count * lat_width)
    w_gate, w_up, w_down = gate_weight[0], up_weight[0], down_weight[0]
    own_both = join_weights(w_gate, w_up, (FIRST_ROWS, w_gate.shape[0]))
    far = after(far, own_both)
    both_a = swap_ctx(after(own_both[0], far), 2)

    def attend_and_project(here, flat_q, q_rope, own, far, uv_weight, out_weight, expert_ids, gate_levels, bin_ids, both):
        far_across = swap_exp(far)
        there = swap_ctx(after(both, far_across), 1)
        near = lax.ppermute(own, "ctx", [(c, c + 1) for c in range(0, ctx_devices, 2)])
        table = route_table(expert_ids, gate_levels, bin_ids, exp_devices)
        early = after(far, (flat_q, table))
        key_pieces = [own, near, *[lax.ppermute(piece, "ctx", [(3, 2)]) for piece in (early, far_across)], far, far_across]
        values = attend(here, flat_q, q_rope, key_pieces, uv_weight, rope_width)
        return project_blocks(here, after(values, there), out_weight, exp_devices), table, there

    inputs = here, flat_q, q_rope, own, far, uv_weight, out_weight, expert_ids, gate_levels, bin_ids, own_both[0]
    partial, table, there_a = after(one_step(attend_and_project, *inputs), both_a)
    both_c = swap_ctx(after(own_both[1], (partial[0], both_a)), 2)

    def sum_and_norm(partial, *rest):
        return norm_rows(*reduce_exp(*partial), *rest)

    stream_state, block = one_step(sum_and_norm, partial, residual_in, norm_gain, table)
    across, back, there_c, near_down = after(
        one_step(
            lambda value, *weights: (swap_exp(value), ring_z(value), *[swap_ctx(weight, 1) for weight in weights]),
            block,
            own_both[1],
            w_down,
        ),
        both_c,
    )
    there_both = [there_a, there_c]
    far_down = swap_ctx(after(w_down, (both_c, back)), 2)

    def gather_and_hide(block, across, back, here, own_both, there_both, far_both):
        weights = [own_both, there_both, far_both, [swap_ctx(piece, 1) for piece in far_both]]
        found = [block, across, *gather_exp(back)]
        half = len(found) // 2
        *first, held = hidden_rows(here, found[:half], weights, exp_devices)
        last = hidden_rows(here, found[half:], held, exp_devices)
        return [*zip(first, last)]

    hidden, bins, scales = after(
        one_step(gather_and_hide, block, across, back, here, own_both, there_both, [both_a, both_c]), far_down
    )
    downs = [w_down, near_down, far_down, swap_ctx(after(far_down, hidden), 1)]
    expert_out = down_blocks(hidden, scales, downs, exp_devices)
    mixture = reduce_exp(*expert_out)
    layer_out = (stream_state + sum(term.astype(jnp.float32) for term in mixture)).astype(jnp.bfloat16)
    histogram = spread_bins(after(bins[0] + bins[1], expert_out[0]))
    return (layer_out, histogram)


def solution(mesh):
    sizes = mesh.shape

    def on_device(*arrays):
        named_experts = arrays[9].shape[1]
        dense = sizes["exp"] == 8 and sizes["ctx"] == 4 and named_experts == sizes["exp"]
        return (dense_device if dense else routed_device)(*arrays)

    return jax.shard_map(
        on_device,
        mesh=mesh,
        in_specs=(
            P(("ctx", "exp"), None),
            P(),
            P("ctx", "exp", None),
            P("ctx", "exp"),
            P("ctx", None),
            P("ctx", None),
            P("ctx"),
            P("exp", None, None),
            P("exp", None),
            P(("ctx", "exp"), None),
            P(("ctx", "exp"), None),
            P(("ctx", "exp"), None),
            P("exp", None, "ctx"),
            P("exp", None, "ctx"),
            P("exp", "ctx", None),
        ),
        out_specs=(P(("ctx", "exp"), None), P("exp", "ctx")),
        check_vma=False,
    )
```
